128 devices in a mesh: section: 4 (over x), fsdp: 32 (over y, z, core).
Axes of the slice: x: 4, y: 4, z: 4, core: 2. Of those that a mesh axis runs over, the one named last changes fastest.
Arguments:
- inputs: bfloat16 [4096, 8192], P('fsdp'), may hold values from -6 to 6
- targets: bfloat16 [4096, 8192], P('fsdp'), may hold values from -6 to 6
- down_proj: bfloat16 [4, 8192, 128], P('section', 'fsdp'), may hold values from -0.0625 to 0.0625
- up_proj: bfloat16 [4, 8192, 128], P('section', 'fsdp'), may hold values from -0.5 to 0.5
- direction: float32 [4, 2, 8192, 128], P('section', None, 'fsdp'), may hold values from -6 to 6
- residual: float32 [4, 2, 8192, 128], P('section', None, 'fsdp'), may hold values from -6 to 6
Outputs:
- new_residual: float32 [4, 2, 8192, 128], P('section', None, 'fsdp')
- new_direction: float32 [4, 2, 8192, 128], P('section', None, 'fsdp')
The draws below stay inside these ranges and needn't reach their ends.
All inputs are finite; a program needn't handle non-finite values.
Results may differ from the reference program's by a relative error of at most 0.027.
Values may be sent and summed in bfloat16 or wider, within the bound.
A program may use at most 128 MiB of HBM per device.

```python
import jax
import jax.numpy as jnp
from jax import lax

D = 8192
R = 128
LENGTH = 128
SEQS = 32
TOKENS = 4096
N_SECTION = 4


def shard_levels(key, shape, pieces, smallest, high):
    level = 1.0
    for axis_at, parts in pieces:
        draws = jax.random.uniform(jax.random.fold_in(jax.random.fold_in(key, 6), axis_at), (parts,), jnp.float32, smallest / len(pieces), high / len(pieces))
        level = level * jnp.repeat(jnp.exp(draws), shape[axis_at] // parts).reshape((-1,) + (1,) * (len(shape) - 1 - axis_at))
    return level


def scatter_about(key, extent, scale, most, pieces=(), dtype=jnp.bfloat16):
    array = scale * jax.random.normal(key, extent, jnp.float32)
    if pieces:
        array = array * shard_levels(key, extent, pieces, -0.22, 0.18)
    return jnp.clip(array, -most, most).astype(dtype)


def setup_inputs(seed: int = 0) -> dict:
    key_of = jax.random.split(jax.random.key(seed), 7)
    return {
        "inputs": scatter_about(key_of[0], (TOKENS, D), 1.0, 6.0, ((0, 32),)),
        "targets": scatter_about(key_of[1], (TOKENS, D), 1.0, 6.0, ((0, 32),)),
        "down_proj": scatter_about(key_of[2], (N_SECTION, D, R), D ** -0.5, 0.0625, ((0, 4), (1, 32))),
        "up_proj": scatter_about(key_of[3], (N_SECTION, D, R), R ** -0.5, 0.5, ((0, 4), (1, 32))),
        "direction": scatter_about(key_of[4], (N_SECTION, 2, D, R), 1.0, 6.0, ((0, 4), (2, 32)), jnp.float32),
        "residual": scatter_about(key_of[5], (N_SECTION, 2, D, R), 1.0, 6.0, ((0, 4), (2, 32)), jnp.float32),
    }


norm_eps = 1e-05
damping = 1e-06

def silu_slope(values):
    sig = jax.nn.sigmoid(values)
    return sig * (1.0 + values * (1.0 - sig))

def contract_last(left, right):
    return lax.dot_general(left, right, (((1,), (1,)), ((), ())), preferred_element_type=jnp.float32)

def contract_first(left, right):
    return lax.dot_general(left, right, (((0,), (0,)), ((), ())), preferred_element_type=jnp.float32)

def reference(inputs, targets, down_proj, up_proj, direction, residual):
    hidden = inputs
    tangent = jnp.zeros_like(inputs)
    saved = []
    for layer in range(N_SECTION):
        w_down = down_proj[layer]
        w_up = up_proj[layer]
        tan_down = direction[layer, 0].astype(jnp.bfloat16)
        tan_up = direction[layer, 1].astype(jnp.bfloat16)
        hid = hidden.astype(jnp.float32)
        tan = tangent.astype(jnp.float32)
        scale_rms = jnp.sqrt(lax.optimization_barrier(jnp.mean(hid * hid, axis=1, keepdims=True)) + norm_eps)
        unit = hid / scale_rms
        normed = unit.astype(jnp.bfloat16)
        pre = jnp.dot(normed, w_down, preferred_element_type=jnp.float32)
        hidden_act = jax.nn.silu(pre).astype(jnp.bfloat16)
        normed_tan = ((tan - unit * lax.optimization_barrier(jnp.mean(unit * tan, axis=1, keepdims=True))) / scale_rms).astype(jnp.bfloat16)
        pre_tan = jnp.dot(normed_tan, w_down, preferred_element_type=jnp.float32) + jnp.dot(normed, tan_down, preferred_element_type=jnp.float32)
        act_tan = (silu_slope(pre) * pre_tan).astype(jnp.bfloat16)
        hidden = (hid + contract_last(hidden_act, w_up)).astype(jnp.bfloat16)
        tangent = (tan + contract_last(act_tan, w_up) + contract_last(hidden_act, tan_up)).astype(jnp.bfloat16)
        saved.append((scale_rms, unit, normed, pre, hidden_act))
    error = hidden.astype(jnp.float32) - targets.astype(jnp.float32)
    per_token = lax.optimization_barrier(jnp.sum(error * tangent.astype(jnp.float32), axis=1))
    seq_weight = lax.optimization_barrier(jnp.sum(per_token.reshape(SEQS, LENGTH), axis=1)) / (LENGTH * D)
    cotangent = (error * jnp.repeat(seq_weight, LENGTH)[:, None]).astype(jnp.bfloat16)
    grads = [None] * N_SECTION
    for layer in range(N_SECTION - 1, -1, -1):
        scale_rms, unit, normed, pre, hidden_act = saved[layer]
        w_down = down_proj[layer]
        w_up = up_proj[layer]
        act_cot = jnp.dot(cotangent, w_up, preferred_element_type=jnp.float32)
        pre_cot = (act_cot * silu_slope(pre)).astype(jnp.bfloat16)
        grad_down = contract_first(normed, pre_cot)
        grad_up = contract_first(cotangent, hidden_act)
        grads[layer] = jnp.stack([grad_down, grad_up])
        if layer > 0:
            normed_cot = contract_last(pre_cot, w_down)
            cotangent = (cotangent.astype(jnp.float32) + (normed_cot - unit * lax.optimization_barrier(jnp.mean(unit * normed_cot, axis=1, keepdims=True))) / scale_rms).astype(jnp.bfloat16)
    fisher = jnp.stack(grads) / (SEQS * LENGTH * D)
    product = fisher + damping * direction
    norm_old = jnp.sum(residual * residual)
    alpha = norm_old / jnp.sum(direction * product)
    new_residual = residual - alpha * product
    norm_new = jnp.sum(new_residual * new_residual)
    new_direction = new_residual + norm_new / norm_old * direction
    return (new_residual, new_direction)
```

```python
import functools

import jax
import jax.numpy as jnp
from jax import lax
from jax.experimental import pallas as pl
from jax.experimental.pallas import tpu as pltpu
from jax.sharding import PartitionSpec as P

MESH = pl.DeviceIdType.MESH
bf16 = jnp.bfloat16
f32 = jnp.float32

norm_eps = 1e-05
damping = 1e-06
N_LAYER = 4
SIDE = 4
CHIPS = 16

CROSS = {}
for _j in range(N_LAYER):
    for _l in range(_j + 1, N_LAYER):
        CROSS[(_j, _l)] = len(CROSS)
SELF = {}
for _j in range(N_LAYER):
    for _l in range(_j, N_LAYER):
        SELF[(_j, _l)] = len(CROSS) + len(SELF)
N_GRAM = len(CROSS) + len(SELF)


def dot_nn(a, b):
    return lax.dot_general(a, b, (((1,), (0,)), ((), ())), preferred_element_type=f32)


def dot_nt(a, b):
    return lax.dot_general(a, b, (((1,), (1,)), ((), ())), preferred_element_type=f32)


def dot_tn(a, b):
    return lax.dot_general(a, b, (((0,), (0,)), ((), ())), preferred_element_type=f32)


class Counter:
    def __init__(self):
        self.n = 0

    def take(self):
        self.n += 1
        return self.n - 1


N_SEM = 185


def kernel(
    x_hbm, y_hbm, a_ref, b_ref, dir_ref, res_ref,
    newres_ref, newdir_ref,
    xin, yin, xg, yg, xs, ys, xt, yt, w, pbf,
    prod, prod_out, prod_in, prodx_out, prodx_in,
    gram, gram_out, gram_in, gramx_out, gramx_in, gfull,
    act, ht, g, half_in, full_in, acc2, half2_in, full2_in, fin,
    gx, stat_out, stat_in, stat2_out, stat2_in, dv_out, dv_in,
    send_sem, recv_sem, local_sem,
):
    tseq, width = xin.shape
    rank = a_ref.shape[1]
    own = a_ref.shape[0]
    pr = own // N_LAYER
    feats = CHIPS * pr
    tq = tseq // N_LAYER
    quad = SIDE * pr
    sx = lax.axis_index("section")
    f = lax.axis_index("fsdp")
    c = lax.rem(f, 2)
    z = lax.rem(lax.div(f, 2), SIDE)
    y = lax.div(f, 2 * SIDE)
    me_yz = y * SIDE + z

    def up(v, k):
        return lax.rem(v + k + SIDE, SIDE)

    def fs(yy, zz, cc):
        return (yy * SIDE + zz) * 2 + cc

    barrier = pltpu.get_barrier_semaphore()
    for k in range(1, 8):
        px = up(sx, k // 2)
        pc = lax.rem(c + k, 2)
        pl.semaphore_signal(barrier, inc=1, device_id=(px, fs(y, z, pc)), device_id_type=MESH)
    for k in range(1, CHIPS):
        pl.semaphore_signal(
            barrier, inc=1, device_id=(sx, fs(up(y, k // SIDE), up(z, k % SIDE), c)), device_id_type=MESH
        )

    load_x = pltpu.make_async_copy(x_hbm, xin, local_sem.at[0])
    load_y = pltpu.make_async_copy(y_hbm, yin, local_sem.at[1])
    load_x.start()
    load_y.start()
    pbf[...] = dir_ref[...].astype(bf16)

    pl.semaphore_wait(barrier, 7 + CHIPS - 1)

    counter = Counter()
    pending = []

    def send(src, dst, dev):
        k = counter.take()
        copy = pltpu.make_async_remote_copy(
            src_ref=src, dst_ref=dst, send_sem=send_sem.at[k], recv_sem=recv_sem.at[k],
            device_id=dev, device_id_type=MESH,
        )
        copy.start()
        pending.append(copy)
        return k

    def arrive(k, dst):
        pltpu.make_async_remote_copy(
            src_ref=dst, dst_ref=dst, send_sem=send_sem.at[k], recv_sem=recv_sem.at[k],
            device_id=(sx, f), device_id_type=MESH,
        ).wait_recv()

    sib = (sx, fs(y, z, 1 - c))

    def line(k):
        return (up(sx, k), f)

    def rows(ref, at, size):
        return ref.at[pl.ds(pl.multiple_of(at * size, size), size)]

    def cols(at):
        return pl.ds(pl.multiple_of(at * rank, rank), rank)

    def spread(srcs, arrs):
        keys = []
        for src, arr in zip(srcs, arrs):
            for k in range(1, N_LAYER):
                to = up(sx, k)
                keys.append((arr, k, send(rows(src, to, pr), w.at[arr, me_yz, :, cols(sx)], line(k))))
        copies = []
        for n, (src, arr) in enumerate(zip(srcs, arrs)):
            copy = pltpu.make_async_copy(
                rows(src, sx, pr), w.at[arr, me_yz, :, cols(sx)], local_sem.at[2 + arr]
            )
            copy.start()
            copies.append(copy)
        return keys, copies

    def spread_done(keys, copies):
        for copy in copies:
            copy.wait()
        for arr, k, key in keys:
            arrive(key, w.at[arr, me_yz, :, cols(up(sx, -k))])

    ab_keys = spread((a_ref, b_ref), (0, 1))
    p_keys = spread((pbf.at[0], pbf.at[1]), (2, 3))

    half = pr // 2
    lo, hi = pl.ds(0, half), pl.ds(half, half)

    class Gather:
        def __init__(self, arr, first):
            self.arr, self.first, self.key = arr, first, {}

        def blk(self, i, j):
            dy, dz = (i, j) if self.first == "y" else (j, i)
            return up(y, dy) * SIDE + up(z, dz)

        def dev(self, i, j):
            dy, dz = (i, j) if self.first == "y" else (j, i)
            return (sx, fs(up(y, dy), up(z, dz), c))

        def ref(self, i, j, part=None):
            r = w.at[self.arr, self.blk(i, j)]
            return r if part is None else w.at[self.arr, self.blk(i, j), part]

        def push(self, name, ref, di, dj):
            self.key[name] = send(ref, ref, self.dev(di, dj))

        def start(self):
            self.push("r", self.ref(0, 0), 1, 0)
            self.push("l", self.ref(0, 0), -1, 0)
            self.second(0)

        def second(self, i):
            self.push(("r", i), self.ref(i, 0), 0, 1)
            self.push(("l", i), self.ref(i, 0), 0, -1)

        def relay(self):
            arrive(self.key["r"], self.ref(-1, 0))
            self.push("rh", self.ref(-1, 0, lo), 1, 0)
            arrive(self.key["l"], self.ref(1, 0))
            self.push("lh", self.ref(1, 0, hi), -1, 0)
            self.second(-1)
            self.second(1)

        def relay_far(self):
            arrive(self.key["rh"], self.ref(2, 0, lo))
            arrive(self.key["lh"], self.ref(2, 0, hi))
            self.second(2)

        def relay_second(self, i):
            arrive(self.key[("r", i)], self.ref(i, -1))
            self.push(("rh", i), self.ref(i, -1, lo), 0, 1)
            arrive(self.key[("l", i)], self.ref(i, 1))
            self.push(("lh", i), self.ref(i, 1, hi), 0, -1)

        def finish(self, i):
            arrive(self.key[("rh", i)], self.ref(i, 2, lo))
            arrive(self.key[("lh", i)], self.ref(i, 2, hi))

    ga, gb = Gather(0, "y"), Gather(1, "z")
    gpa, gpb = Gather(2, "y"), Gather(3, "z")
    spread_done(*ab_keys)
    ga.start()
    gb.start()

    load_x.wait()
    load_y.wait()

    def pick(src, dst, cc, put):
        for p in range(0, CHIPS, 2):
            got = []
            for q in (p, p + 1):
                shard = src[:, pl.ds(pl.multiple_of((2 * q + cc) * own, own), own)]
                piece = shard[:, 0:pr]
                for k in range(1, N_LAYER):
                    piece = jnp.where(sx == k, shard[:, k * pr : (k + 1) * pr], piece)
                got.append(piece)
            put(dst, p, jnp.concatenate(got, axis=1))

    def put_other(dst, p, value):
        dst[:, p * pr : (p + 2) * pr] = value

    def put_own(dst, p, value):
        dst[pl.ds(pl.multiple_of(c * tseq, tseq), tseq), p * pr : (p + 2) * pr] = value

    pick(xin, xs, 1 - c, put_other)
    my_rows = pl.ds(pl.multiple_of(c * tseq, tseq), tseq)
    its_rows = pl.ds(pl.multiple_of((1 - c) * tseq, tseq), tseq)
    key_xs = send(xs, xg.at[my_rows], sib)
    pick(yin, ys, 1 - c, put_other)
    key_ys = send(ys, yg.at[my_rows], sib)
    pick(xin, xg, c, put_own)
    pick(yin, yg, c, put_own)

    ga.relay()
    gb.relay()
    ga.relay_second(0)
    gb.relay_second(0)

    xq = xin[pl.ds(pl.multiple_of(sx * tq, tq), tq), :].astype(f32)
    norm = jnp.sum(xq * xq, axis=1, keepdims=True)
    res = res_ref[...]
    direc = dir_ref[...]

    ga.relay_far()
    gb.relay_far()
    arrive(key_xs, xg.at[its_rows])
    arrive(key_ys, yg.at[its_rows])
    xt[...] = xg[...].astype(f32).T.astype(bf16)
    yt[...] = yg[...].astype(f32).T.astype(bf16)
    for i in (-1, 1, 2):
        ga.relay_second(i)
        gb.relay_second(i)
    spread_done(*p_keys)
    gpa.start()
    gpb.start()
    for i in (0, -1, 1, 2):
        ga.finish(i)
        gb.finish(i)

    wide = N_LAYER * rank
    wa = w[0].reshape(feats, wide)
    wb = w[1].reshape(feats, wide)
    xv = xg[...]
    yv = yg[...]
    prod[:, 0:wide] = dot_nn(xv, wa)
    prod[:, wide : 2 * wide] = dot_nn(xv, wb)
    prod[:, 2 * wide : 3 * wide] = dot_nn(yv, wb)
    prod_out[...] = prod[its_rows, :].astype(bf16)
    key_prod = send(prod_out, prod_in, sib)
    gpa.relay()
    gpb.relay()
    for j in range(N_LAYER):
        left = w[1, :, :, j * rank : (j + 1) * rank].reshape(feats, rank)
        if j < N_LAYER - 1:
            right = w[0, :, :, (j + 1) * rank : wide].reshape(feats, wide - (j + 1) * rank)
            block = dot_tn(left, right)
            for l in range(j + 1, N_LAYER):
                gram[CROSS[(j, l)]] = block[:, (l - j - 1) * rank : (l - j) * rank]
        right = w[1, :, :, j * rank : wide].reshape(feats, wide - j * rank)
        block = dot_tn(left, right)
        for l in range(j, N_LAYER):
            gram[SELF[(j, l)]] = block[:, (l - j) * rank : (l - j + 1) * rank]
    n_half = N_GRAM // 2
    my_gram = pl.ds(c * n_half, n_half)
    gram_out[...] = gram[pl.ds((1 - c) * n_half, n_half)].astype(bf16)
    key_gram = send(gram_out, gram_in, sib)
    gpa.relay_second(0)
    gpb.relay_second(0)

    arrive(key_prod, prod_in)
    pair = prod[my_rows, :] + prod_in[...].astype(f32)
    prod[my_rows, :] = pair
    prodx_out[...] = pair.astype(bf16)
    keys = []
    for k in range(1, N_LAYER):
        keys.append(send(rows(prodx_out, up(sx, k), tq), prodx_in.at[k - 1], line(k)))
    arrive(key_gram, gram_in)
    gpair = gram[my_gram] + gram_in[...].astype(f32)
    gram[my_gram] = gpair
    gramx_out[...] = gpair.astype(bf16)
    n_own = n_half // N_LAYER
    gkeys = []
    for k in range(1, N_LAYER):
        gkeys.append(send(gramx_out.at[pl.ds(up(sx, k) * n_own, n_own)], gramx_in.at[k - 1], line(k)))
    gpa.relay_far()
    gpb.relay_far()
    gsum = gram[pl.ds(c * n_half + sx * n_own, n_own)]
    for k in range(1, N_LAYER):
        arrive(gkeys[k - 1], gramx_in.at[k - 1])
        gsum = gsum + gramx_in[k - 1].astype(f32)
    mine = pl.ds(c * n_half + sx * n_own, n_own)
    gfull[mine] = gsum.astype(bf16)
    gkeys = []
    for k in range(1, N_LAYER):
        gkeys.append(send(gfull.at[mine], gfull.at[mine], line(k)))
    for i in (-1, 1):
        gpa.relay_second(i)
        gpb.relay_second(i)
    psum = prod[pl.ds(pl.multiple_of(c * tseq + sx * tq, tq), tq), :]
    for k in range(1, N_LAYER):
        arrive(keys[k - 1], prodx_in.at[k - 1])
        psum = psum + prodx_in[k - 1].astype(f32)
    for k in range(1, N_LAYER):
        arrive(gkeys[k - 1], gfull.at[pl.ds(c * n_half + up(sx, -k) * n_own, n_own)])
    key_gfull = send(gfull.at[my_gram], gfull.at[my_gram], sib)
    gpa.relay_second(2)
    gpb.relay_second(2)
    arrive(key_gfull, gfull.at[pl.ds((1 - c) * n_half, n_half)])

    def part(value, k):
        return value[:, k * rank : (k + 1) * rank]

    ha = [part(psum, l) for l in range(N_LAYER)]
    hb = [part(psum, N_LAYER + l) for l in range(N_LAYER)]
    yb = [part(psum, 2 * N_LAYER + l) for l in range(N_LAYER)]
    acts, slopes, rhos, pres, hbs = [], [], [], [], []
    for l in range(N_LAYER):
        rho = jnp.sqrt(norm / width + norm_eps)
        pre = ha[l] / rho
        sig = jax.nn.sigmoid(pre)
        a = (pre * sig).astype(bf16)
        hbs.append(hb[:l])
        before = hb[l]
        for m in range(l + 1, N_LAYER):
            ha[m] = ha[m] + dot_nn(a, gfull[CROSS[(l, m)]])
        nxt = []
        for m in range(N_LAYER):
            if l <= m:
                nxt.append(hb[m] + dot_nn(a, gfull[SELF[(l, m)]]))
            else:
                nxt.append(hb[m] + dot_nt(a, gfull[SELF[(m, l)]]))
        hb = nxt
        norm = norm + jnp.sum(a.astype(f32) * (before + hb[l]), axis=1, keepdims=True)
        acts.append(a)
        slopes.append(sig * (1.0 + pre * (1.0 - sig)))
        rhos.append(rho)
        pres.append(pre)
    cb = [hb[l] - yb[l] for l in range(N_LAYER)]
    qs = [None] * N_LAYER
    lane = lax.broadcasted_iota(jnp.int32, (tq, rank), 1)
    gains = jnp.zeros((tq, rank), f32)
    for l in range(N_LAYER - 1, -1, -1):
        cot = cb[l] * slopes[l]
        qs[l] = (cot / rhos[l]).astype(bf16)
        if l > 0:
            gain = jnp.sum(cot * pres[l], axis=1, keepdims=True) / (width * rhos[l] * rhos[l])
            gains = jnp.where(lane == l, gain, gains)
            for j in range(l):
                cb[j] = cb[j] + dot_nt(qs[l], gfull[CROSS[(j, l)]]) - gain * hbs[l][j]
    my_act = pl.ds(pl.multiple_of(c * tseq + sx * tq, tq), tq)
    for l in range(N_LAYER):
        act[my_act, l * rank : (l + 1) * rank] = acts[l]
        act[my_act, (N_LAYER + l) * rank : (N_LAYER + l + 1) * rank] = qs[l]
    act[my_act, 2 * N_LAYER * rank :] = gains.astype(bf16)
    keys = []
    for k in range(1, N_LAYER):
        keys.append(send(act.at[my_act], act.at[my_act], line(k)))
    for i in (0, -1, 1, 2):
        gpa.finish(i)
        gpb.finish(i)
    for k in range(1, N_LAYER):
        arrive(keys[k - 1], act.at[pl.ds(pl.multiple_of(c * tseq + up(sx, -k) * tq, tq), tq)])
    key_act = send(act.at[my_rows], act.at[my_rows], sib)
    arrive(key_act, act.at[its_rows])

    av = [act[:, l * rank : (l + 1) * rank] for l in range(N_LAYER)]
    qv = [act[:, (N_LAYER + l) * rank : (N_LAYER + l + 1) * rank] for l in range(N_LAYER)]
    gain_t = act[:, 2 * N_LAYER * rank :].astype(f32).T
    d0 = jnp.zeros((quad, rank), f32)
    d1 = jnp.zeros((quad, rank), f32)
    for q in range(SIDE):
        fr = slice(q * quad, (q + 1) * quad)

        def wq(arr, l):
            return w[arr, q * SIDE : (q + 1) * SIDE, :, l * rank : (l + 1) * rank].reshape(quad, rank)

        h = xt[fr, :].astype(f32)
        hs = []
        for l in range(N_LAYER):
            hb16 = h.astype(bf16)
            hs.append(hb16)
            ht[l, fr, :] = hb16
            h = hb16.astype(f32) + dot_nt(wq(1, l), av[l])
        cot = (h - yt[fr, :].astype(f32)).astype(bf16)
        for l in range(N_LAYER - 1, -1, -1):
            ht[N_LAYER + l, fr, :] = cot
            for arr, left, right in ((2, hs[l], qv[l]), (3, cot, av[l])):
                pw = wq(arr, l).astype(f32)
                d0 = d0 + dot_nn(left[:, :tseq], right[:tseq]) * pw
                d1 = d1 + dot_nn(left[:, tseq:], right[tseq:]) * pw
            if l > 0:
                cot = (
                    cot.astype(f32) + dot_nt(wq(0, l), qv[l]) - gain_t[l : l + 1, :] * hs[l].astype(f32)
                ).astype(bf16)
    def fold(v):
        return jnp.sum(v.reshape(quad // 8, 8, rank), axis=0)

    dv_out[...] = jnp.concatenate([fold(d0), fold(d1)], axis=0)
    keys = []
    for k in range(1, 8):
        keys.append(send(dv_out, dv_in.at[k - 1], (up(sx, k // 2), fs(y, z, lax.rem(c + k, 2)))))
    dv = dv_out[...]
    for k in range(1, 8):
        arrive(keys[k - 1], dv_in.at[k - 1])
        dv = dv + dv_in[k - 1]
    s0 = jnp.sum(dv[:8], keepdims=True) / (tseq * width)
    s1 = jnp.sum(dv[8:], keepdims=True) / (tseq * width)
    token = lax.broadcasted_iota(jnp.int32, (2 * tseq, 1), 0)
    scale = jnp.where(token < tseq, s0, s1)
    qd = [(qv[l].astype(f32) * scale).astype(bf16) for l in range(N_LAYER)]
    ad = [(av[l].astype(f32) * scale).astype(bf16) for l in range(N_LAYER)]

    for arr, base, right in ((0, 0, qd), (1, N_LAYER, ad)):
        for l in range(N_LAYER):
            for q in range(SIDE):
                value = dot_nn(ht[base + l, q * quad : (q + 1) * quad, :], right[l])
                g[arr, q * SIDE : (q + 1) * SIDE, :, l * rank : (l + 1) * rank] = value.astype(bf16).reshape(
                    SIDE, pr, rank
                )

    class Scatter:
        def __init__(self, arr, first):
            self.arr, self.first, self.key = arr, first, {}

        def blk(self, i, j):
            dy, dz = (j, i) if self.first == "y" else (i, j)
            return up(y, dy) * SIDE + up(z, dz)

        def dev(self, i, j):
            dy, dz = (j, i) if self.first == "y" else (i, j)
            return (sx, fs(up(y, dy), up(z, dz), c))

        def start(self, i):
            far = self.blk(i, 2)
            n = i % SIDE
            self.key[("rh", i)] = send(g.at[self.arr, far, lo], half_in.at[self.arr, n, 0], self.dev(0, 1))
            self.key[("lh", i)] = send(g.at[self.arr, far, hi], half_in.at[self.arr, n, 1], self.dev(0, -1))

        def middle(self, i):
            n = i % SIDE
            arrive(self.key[("rh", i)], half_in.at[self.arr, n, 0])
            b = self.blk(i, 1)
            g[self.arr, b, lo] = (g[self.arr, b, lo].astype(f32) + half_in[self.arr, n, 0].astype(f32)).astype(bf16)
            self.key[("r", i)] = send(g.at[self.arr, b], full_in.at[self.arr, n, 0], self.dev(0, 1))
            arrive(self.key[("lh", i)], half_in.at[self.arr, n, 1])
            b = self.blk(i, -1)
            g[self.arr, b, hi] = (g[self.arr, b, hi].astype(f32) + half_in[self.arr, n, 1].astype(f32)).astype(bf16)
            self.key[("l", i)] = send(g.at[self.arr, b], full_in.at[self.arr, n, 1], self.dev(0, -1))

        def end(self, i):
            n = i % SIDE
            arrive(self.key[("r", i)], full_in.at[self.arr, n, 0])
            arrive(self.key[("l", i)], full_in.at[self.arr, n, 1])
            value = (
                g[self.arr, self.blk(i, 0)].astype(f32)
                + full_in[self.arr, n, 0].astype(f32)
                + full_in[self.arr, n, 1].astype(f32)
            )
            acc2[self.arr, n] = value
            return value

        def start2(self):
            fin[self.arr, 1] = acc2[self.arr, 2].astype(bf16)
            self.key["rh"] = send(fin.at[self.arr, 1, lo], half2_in.at[self.arr, 0], self.dev(1, 0))
            self.key["lh"] = send(fin.at[self.arr, 1, hi], half2_in.at[self.arr, 1], self.dev(-1, 0))

        def middle2(self):
            arrive(self.key["rh"], half2_in.at[self.arr, 0])
            acc2[self.arr, 1, lo] = acc2[self.arr, 1, lo] + half2_in[self.arr, 0].astype(f32)
            fin[self.arr, 2] = acc2[self.arr, 1].astype(bf16)
            self.key["r"] = send(fin.at[self.arr, 2], full2_in.at[self.arr, 0], self.dev(1, 0))
            arrive(self.key["lh"], half2_in.at[self.arr, 1])
            acc2[self.arr, 3, hi] = acc2[self.arr, 3, hi] + half2_in[self.arr, 1].astype(f32)
            fin[self.arr, 3] = acc2[self.arr, 3].astype(bf16)
            self.key["l"] = send(fin.at[self.arr, 3], full2_in.at[self.arr, 1], self.dev(-1, 0))

        def end2(self):
            arrive(self.key["r"], full2_in.at[self.arr, 0])
            arrive(self.key["l"], full2_in.at[self.arr, 1])
            value = (
                acc2[self.arr, 0] + full2_in[self.arr, 0].astype(f32) + full2_in[self.arr, 1].astype(f32)
            )
            fin[self.arr, 0] = value.astype(bf16)
            self.back = []
            for k in range(1, N_LAYER):
                to = up(sx, k)
                self.back.append(send(fin.at[self.arr, 0, :, cols(to)], gx.at[self.arr, sx], line(k)))
            gx[self.arr, sx] = fin[self.arr, 0, :, cols(sx)]

        def done(self):
            for k in range(1, N_LAYER):
                arrive(self.back[k - 1], gx.at[self.arr, up(sx, -k)])

    sa, sb = Scatter(0, "z"), Scatter(1, "y")
    both = (sa, sb)
    order = (2, 1, -1, 0)
    for i in order:
        for s in both:
            s.start(i)
    for i in order:
        for s in both:
            s.middle(i)
    for s in both:
        s.end(2)
        s.start2()
    for i in (1, -1):
        for s in both:
            s.end(i)
    for s in both:
        s.middle2()
    for s in both:
        s.end(0)
    for s in both:
        s.end2()
    for s in both:
        s.done()

    tokens_total = tseq * 2 * CHIPS
    shrink = 1.0 / (damping * tokens_total * width)
    grad = gx[...].astype(f32).reshape(2, own, rank)
    big = grad * shrink + direc

    def fold2(v):
        return jnp.sum(v.reshape(2 * own // 8, 8, rank), axis=0)

    stat_out[...] = jnp.concatenate([fold2(res * res), fold2(direc * big), fold2(res * big), fold2(big * big)], axis=0)
    keys = []
    for k in range(1, 8):
        keys.append(send(stat_out, stat_in.at[k - 1], (up(sx, k // 2), fs(y, z, lax.rem(c + k, 2)))))
    total = stat_out[...]
    for k in range(1, 8):
        arrive(keys[k - 1], stat_in.at[k - 1])
        total = total + stat_in[k - 1]
    stat2_out[...] = total
    keys = []
    for k in range(1, CHIPS):
        keys.append(send(stat2_out, stat2_in.at[k - 1], (sx, fs(up(y, k // SIDE), up(z, k % SIDE), c))))
    for k in range(1, CHIPS):
        arrive(keys[k - 1], stat2_in.at[k - 1])
        total = total + stat2_in[k - 1]
    rr = jnp.sum(total[0:8], keepdims=True)
    pq = jnp.sum(total[8:16], keepdims=True) * damping
    rp = jnp.sum(total[16:24], keepdims=True)
    pp = jnp.sum(total[24:32], keepdims=True)
    step = rr / pq * damping
    norm_new = rr - 2.0 * (step * rp) + step * (step * pp)
    beta = norm_new / rr
    new_res = res - step * big
    newres_ref[...] = new_res
    newdir_ref[...] = new_res + beta * direc
    for copy in pending:
        copy.wait_send()


def step_kernel(inputs, targets, down_proj, up_proj, direction, residual):
    tseq, width = inputs.shape
    _, own, rank = down_proj.shape
    pr = own // N_LAYER
    feats = CHIPS * pr
    tq = tseq // N_LAYER
    wide = N_LAYER * rank
    n_half = N_GRAM // 2
    n_own = n_half // N_LAYER
    vm = pltpu.VMEM
    scratch = [
        vm((tseq, width), bf16), vm((tseq, width), bf16),
        vm((2 * tseq, feats), bf16), vm((2 * tseq, feats), bf16),
        vm((tseq, feats), bf16), vm((tseq, feats), bf16),
        vm((feats, 2 * tseq), bf16), vm((feats, 2 * tseq), bf16),
        vm((4, CHIPS, pr, wide), bf16), vm((2, own, rank), bf16),
        vm((2 * tseq, 3 * wide), f32), vm((tseq, 3 * wide), bf16), vm((tseq, 3 * wide), bf16),
        vm((tseq, 3 * wide), bf16), vm((N_LAYER - 1, tq, 3 * wide), bf16),
        vm((N_GRAM, rank, rank), f32), vm((n_half, rank, rank), bf16), vm((n_half, rank, rank), bf16),
        vm((n_half, rank, rank), bf16), vm((N_LAYER - 1, n_own, rank, rank), bf16), vm((N_GRAM, rank, rank), bf16),
        vm((2 * tseq, 2 * wide + rank), bf16), vm((2 * N_LAYER, feats, 2 * tseq), bf16),
        vm((2, CHIPS, pr, wide), bf16),
        vm((2, SIDE, 2, pr // 2, wide), bf16), vm((2, SIDE, 2, pr, wide), bf16),
        vm((2, SIDE, pr, wide), f32),
        vm((2, 2, pr // 2, wide), bf16), vm((2, 2, pr, wide), bf16), vm((2, SIDE, pr, wide), bf16),
        vm((2, N_LAYER, pr, rank), bf16),
        vm((32, rank), f32), vm((7, 32, rank), f32), vm((32, rank), f32), vm((CHIPS - 1, 32, rank), f32),
        vm((16, rank), f32), vm((7, 16, rank), f32),
        pltpu.SemaphoreType.DMA((N_SEM,)), pltpu.SemaphoreType.DMA((N_SEM,)), pltpu.SemaphoreType.DMA((6,)),
    ]
    spec = pl.BlockSpec(memory_space=pltpu.VMEM)
    hbm = pl.BlockSpec(memory_space=pl.ANY)
    out = jax.ShapeDtypeStruct((2, own, rank), f32)
    new_res, new_dir = pl.pallas_call(
        kernel,
        out_shape=(out, out),
        in_specs=[hbm, hbm, spec, spec, spec, spec],
        out_specs=(spec, spec),
        scratch_shapes=scratch,
        compiler_params=pltpu.CompilerParams(
            collective_id=0, has_side_effects=True, vmem_limit_bytes=52 * 1024 * 1024
        ),
        cost_estimate=pl.CostEstimate(flops=4_000_000_000, bytes_accessed=8_000_000, transcendentals=0),
    )(inputs, targets, down_proj[0], up_proj[0], direction[0], residual[0])
    return new_res[None], new_dir[None]


def solution(mesh):
    in_specs = (
        P("fsdp", None),
        P("fsdp", None),
        P("section", "fsdp", None),
        P("section", "fsdp", None),
        P("section", None, "fsdp", None),
        P("section", None, "fsdp", None),
    )
    out_specs = (P("section", None, "fsdp", None), P("section", None, "fsdp", None))
    return jax.shard_map(step_kernel, mesh=mesh, in_specs=in_specs, out_specs=out_specs, check_vma=False)
```

```python
import functools

import jax
import jax.numpy as jnp
from jax import lax
from jax.experimental import pallas as pl
from jax.experimental.pallas import tpu as pltpu
from jax.sharding import PartitionSpec as P

MESH = pl.DeviceIdType.MESH
bf16 = jnp.bfloat16
f32 = jnp.float32

norm_eps = 1e-05
damping = 1e-06
N_LAYER = 4
SIDE = 4
CHIPS = 16

CROSS = {}
for _j in range(N_LAYER):
    for _l in range(_j + 1, N_LAYER):
        CROSS[(_j, _l)] = len(CROSS)
SELF = {}
for _j in range(N_LAYER):
    for _l in range(_j, N_LAYER):
        SELF[(_j, _l)] = len(CROSS) + len(SELF)
N_GRAM = len(CROSS) + len(SELF)


def dot_nn(a, b):
    return lax.dot_general(a, b, (((1,), (0,)), ((), ())), preferred_element_type=f32)


def dot_nt(a, b):
    return lax.dot_general(a, b, (((1,), (1,)), ((), ())), preferred_element_type=f32)


def dot_tn(a, b):
    return lax.dot_general(a, b, (((0,), (0,)), ((), ())), preferred_element_type=f32)


class Counter:
    def __init__(self):
        self.n = 0

    def take(self):
        self.n += 1
        return self.n - 1


N_SEM = 119


def kernel(
    x_hbm, y_hbm, a_ref, b_ref, dir_hbm, res_hbm,
    newres_ref, newdir_ref,
    xin, yin, dir_ref, res_ref, xg, yg, xs, ys, xt, yt, w, pbf,
    prod, prod_out, prod_in, prodx_out, prodx_in,
    gram, gram_out, gram_in, gramx_out, gramx_in, gfull,
    act, ht, g, pair_in, acc2, block_in, fin,
    gx, stat_out, stat_in, stat2_out, stat2_in, dv_out, dv_in,
    send_sem, recv_sem, local_sem,
):
    tseq, width = xin.shape
    rank = a_ref.shape[1]
    own = a_ref.shape[0]
    pr = own // N_LAYER
    feats = CHIPS * pr
    tq = tseq // N_LAYER
    quad = SIDE * pr
    sx = lax.axis_index("section")
    f = lax.axis_index("fsdp")
    c = lax.rem(f, 2)
    z = lax.rem(lax.div(f, 2), SIDE)
    y = lax.div(f, 2 * SIDE)

    def up(v, k):
        return lax.rem(v + k + SIDE, SIDE)

    def fs(yy, zz, cc):
        return (yy * SIDE + zz) * 2 + cc

    barrier = pltpu.get_barrier_semaphore()
    for k in range(1, 8):
        px = up(sx, k // 2)
        pc = lax.rem(c + k, 2)
        pl.semaphore_signal(barrier, inc=1, device_id=(px, fs(y, z, pc)), device_id_type=MESH)
    for k in range(1, SIDE):
        pl.semaphore_signal(barrier, inc=1, device_id=(sx, fs(up(y, k), z, c)), device_id_type=MESH)
        pl.semaphore_signal(barrier, inc=1, device_id=(sx, fs(y, up(z, k), c)), device_id_type=MESH)

    load_x = pltpu.make_async_copy(x_hbm, xin, local_sem.at[0])
    load_y = pltpu.make_async_copy(y_hbm, yin, local_sem.at[1])
    load_d = pltpu.make_async_copy(dir_hbm, dir_ref, local_sem.at[6])
    load_r = pltpu.make_async_copy(res_hbm, res_ref, local_sem.at[7])
    load_d.start()
    load_x.start()
    load_y.start()
    load_r.start()
    load_d.wait()
    pbf[...] = dir_ref[...].astype(bf16)

    pl.semaphore_wait(barrier, 7 + 2 * (SIDE - 1))

    counter = Counter()
    pending = []

    def send(src, dst, dev):
        k = counter.take()
        copy = pltpu.make_async_remote_copy(
            src_ref=src, dst_ref=dst, send_sem=send_sem.at[k], recv_sem=recv_sem.at[k],
            device_id=dev, device_id_type=MESH,
        )
        copy.start()
        pending.append(copy)
        return k

    def arrive(k, dst):
        pltpu.make_async_remote_copy(
            src_ref=dst, dst_ref=dst, send_sem=send_sem.at[k], recv_sem=recv_sem.at[k],
            device_id=(sx, f), device_id_type=MESH,
        ).wait_recv()

    sib = (sx, fs(y, z, 1 - c))

    def line(k):
        return (up(sx, k), f)

    def rows(ref, at, size):
        return ref.at[pl.ds(pl.multiple_of(at * size, size), size)]

    def cols(at):
        return pl.ds(pl.multiple_of(at * rank, rank), rank)

    def spread(srcs, arrs):
        keys = []
        for src, arr in zip(srcs, arrs):
            for k in range(1, N_LAYER):
                to = up(sx, k)
                keys.append((arr, k, send(rows(src, to, pr), w.at[arr, y, z, :, cols(sx)], line(k))))
        copies = []
        for n, (src, arr) in enumerate(zip(srcs, arrs)):
            copy = pltpu.make_async_copy(
                rows(src, sx, pr), w.at[arr, y, z, :, cols(sx)], local_sem.at[2 + arr]
            )
            copy.start()
            copies.append(copy)
        return keys, copies

    def spread_done(keys, copies):
        for copy in copies:
            copy.wait()
        for arr, k, key in keys:
            arrive(key, w.at[arr, y, z, :, cols(up(sx, -k))])

    ab_keys = spread((a_ref, b_ref), (0, 1))
    p_keys = spread((pbf.at[0], pbf.at[1]), (2, 3))

    class Gather:
        def __init__(self, arr, first):
            self.arr, self.first, self.key = arr, first, {}

        def dev(self, i, j):
            dy, dz = (i, j) if self.first == "y" else (j, i)
            return (sx, fs(up(y, dy), up(z, dz), c))

        def block(self, i):
            if self.first == "y":
                return w.at[self.arr, up(y, i), z]
            return w.at[self.arr, y, up(z, i)]

        def pair(self, p, j):
            if self.first == "y":
                return w.at[self.arr, pl.ds(2 * p, 2), up(z, j)]
            return w.at[self.arr, up(y, j), pl.ds(2 * p, 2)]

        def push(self, name, ref, di, dj):
            self.key[name] = send(ref, ref, self.dev(di, dj))

        def start(self):
            for i in (2, 1, -1):
                self.push(i, self.block(0), i, 0)

        def second(self):
            for i in (1, -1, 2):
                arrive(self.key[i], self.block(-i))
            self.push("r1", self.pair(0, 0), 0, 1)
            self.push("l1", self.pair(1, 0), 0, -1)
            self.push("r2", self.pair(1, 0), 0, 1)
            self.push("l2", self.pair(0, 0), 0, -1)

        def relay(self):
            arrive(self.key["r1"], self.pair(0, -1))
            self.push("rr", self.pair(0, -1), 0, 1)
            arrive(self.key["l1"], self.pair(1, 1))
            self.push("ll", self.pair(1, 1), 0, -1)

        def finish(self):
            arrive(self.key["r2"], self.pair(1, -1))
            arrive(self.key["l2"], self.pair(0, 1))
            arrive(self.key["rr"], self.pair(0, 2))
            arrive(self.key["ll"], self.pair(1, 2))

    ga, gb = Gather(0, "y"), Gather(1, "z")
    gpa, gpb = Gather(2, "y"), Gather(3, "z")
    spread_done(*ab_keys)
    ga.start()
    gb.start()

    load_x.wait()
    load_y.wait()

    def pick(src, dst, cc, put):
        for p in range(0, CHIPS, 2):
            got = []
            for q in (p, p + 1):
                shard = src[:, pl.ds(pl.multiple_of((2 * q + cc) * own, own), own)]
                piece = shard[:, 0:pr]
                for k in range(1, N_LAYER):
                    piece = jnp.where(sx == k, shard[:, k * pr : (k + 1) * pr], piece)
                got.append(piece)
            put(dst, p, jnp.concatenate(got, axis=1))

    def put_other(dst, p, value):
        dst[:, p * pr : (p + 2) * pr] = value

    def put_own(dst, p, value):
        dst[pl.ds(pl.multiple_of(c * tseq, tseq), tseq), p * pr : (p + 2) * pr] = value

    pick(xin, xs, 1 - c, put_other)
    my_rows = pl.ds(pl.multiple_of(c * tseq, tseq), tseq)
    its_rows = pl.ds(pl.multiple_of((1 - c) * tseq, tseq), tseq)
    key_xs = send(xs, xg.at[my_rows], sib)
    pick(yin, ys, 1 - c, put_other)
    key_ys = send(ys, yg.at[my_rows], sib)
    pick(xin, xg, c, put_own)
    pick(yin, yg, c, put_own)

    ga.second()
    gb.second()

    xq = xin[pl.ds(pl.multiple_of(sx * tq, tq), tq), :].astype(f32)
    norm = jnp.sum(xq * xq, axis=1, keepdims=True)
    load_r.wait()
    res = res_ref[...]
    direc = dir_ref[...]

    spread_done(*p_keys)
    gpa.start()
    gpb.start()
    arrive(key_xs, xg.at[its_rows])
    arrive(key_ys, yg.at[its_rows])
    xt[...] = xg[...].astype(f32).T.astype(bf16)
    yt[...] = yg[...].astype(f32).T.astype(bf16)
    ga.relay()
    gb.relay()
    gpa.second()
    gpb.second()
    ga.finish()
    gb.finish()

    wide = N_LAYER * rank
    wa = w[0].reshape(feats, wide)
    wb = w[1].reshape(feats, wide)
    xv = xg[...]
    yv = yg[...]
    prod[:, 0:wide] = dot_nn(xv, wa)
    prod[:, wide : 2 * wide] = dot_nn(xv, wb)
    prod[:, 2 * wide : 3 * wide] = dot_nn(yv, wb)
    prod_out[...] = prod[its_rows, :].astype(bf16)
    key_prod = send(prod_out, prod_in, sib)
    for j in range(N_LAYER):
        left = w[1, :, :, :, j * rank : (j + 1) * rank].reshape(feats, rank)
        if j < N_LAYER - 1:
            right = w[0, :, :, :, (j + 1) * rank : wide].reshape(feats, wide - (j + 1) * rank)
            block = dot_tn(left, right)
            for l in range(j + 1, N_LAYER):
                gram[CROSS[(j, l)]] = block[:, (l - j - 1) * rank : (l - j) * rank]
        right = w[1, :, :, :, j * rank : wide].reshape(feats, wide - j * rank)
        block = dot_tn(left, right)
        for l in range(j, N_LAYER):
            gram[SELF[(j, l)]] = block[:, (l - j) * rank : (l - j + 1) * rank]
    n_half = N_GRAM // 2
    my_gram = pl.ds(c * n_half, n_half)
    gram_out[...] = gram[pl.ds((1 - c) * n_half, n_half)].astype(bf16)
    key_gram = send(gram_out, gram_in, sib)

    arrive(key_prod, prod_in)
    pair = prod[my_rows, :] + prod_in[...].astype(f32)
    prod[my_rows, :] = pair
    prodx_out[...] = pair.astype(bf16)
    keys = []
    for k in range(1, N_LAYER):
        keys.append(send(rows(prodx_out, up(sx, k), tq), prodx_in.at[k - 1], line(k)))
    arrive(key_gram, gram_in)
    gpair = gram[my_gram] + gram_in[...].astype(f32)
    gram[my_gram] = gpair
    gramx_out[...] = gpair.astype(bf16)
    n_own = n_half // N_LAYER
    gkeys = []
    for k in range(1, N_LAYER):
        gkeys.append(send(gramx_out.at[pl.ds(up(sx, k) * n_own, n_own)], gramx_in.at[k - 1], line(k)))
    gpa.relay()
    gpb.relay()
    gsum = gram[pl.ds(c * n_half + sx * n_own, n_own)]
    for k in range(1, N_LAYER):
        arrive(gkeys[k - 1], gramx_in.at[k - 1])
        gsum = gsum + gramx_in[k - 1].astype(f32)
    mine = pl.ds(c * n_half + sx * n_own, n_own)
    gfull[mine] = gsum.astype(bf16)
    gkeys = []
    for k in range(1, N_LAYER):
        gkeys.append(send(gfull.at[mine], gfull.at[mine], line(k)))
    psum = prod[pl.ds(pl.multiple_of(c * tseq + sx * tq, tq), tq), :]
    for k in range(1, N_LAYER):
        arrive(keys[k - 1], prodx_in.at[k - 1])
        psum = psum + prodx_in[k - 1].astype(f32)
    for k in range(1, N_LAYER):
        arrive(gkeys[k - 1], gfull.at[pl.ds(c * n_half + up(sx, -k) * n_own, n_own)])
    key_gfull = send(gfull.at[my_gram], gfull.at[my_gram], sib)
    arrive(key_gfull, gfull.at[pl.ds((1 - c) * n_half, n_half)])

    def part(value, k):
        return value[:, k * rank : (k + 1) * rank]

    ha = [part(psum, l) for l in range(N_LAYER)]
    hb = [part(psum, N_LAYER + l) for l in range(N_LAYER)]
    yb = [part(psum, 2 * N_LAYER + l) for l in range(N_LAYER)]
    acts, slopes, rhos, pres, hbs = [], [], [], [], []
    for l in range(N_LAYER):
        rho = jnp.sqrt(norm / width + norm_eps)
        pre = ha[l] / rho
        sig = jax.nn.sigmoid(pre)
        a = (pre * sig).astype(bf16)
        hbs.append(hb[:l])
        before = hb[l]
        for m in range(l + 1, N_LAYER):
            ha[m] = ha[m] + dot_nn(a, gfull[CROSS[(l, m)]])
        nxt = []
        for m in range(N_LAYER):
            if l <= m:
                nxt.append(hb[m] + dot_nn(a, gfull[SELF[(l, m)]]))
            else:
                nxt.append(hb[m] + dot_nt(a, gfull[SELF[(m, l)]]))
        hb = nxt
        norm = norm + jnp.sum(a.astype(f32) * (before + hb[l]), axis=1, keepdims=True)
        acts.append(a)
        slopes.append(sig * (1.0 + pre * (1.0 - sig)))
        rhos.append(rho)
        pres.append(pre)
    cb = [hb[l] - yb[l] for l in range(N_LAYER)]
    qs = [None] * N_LAYER
    lane = lax.broadcasted_iota(jnp.int32, (tq, rank), 1)
    gains = jnp.zeros((tq, rank), f32)
    for l in range(N_LAYER - 1, -1, -1):
        cot = cb[l] * slopes[l]
        qs[l] = (cot / rhos[l]).astype(bf16)
        if l > 0:
            gain = jnp.sum(cot * pres[l], axis=1, keepdims=True) / (width * rhos[l] * rhos[l])
            gains = jnp.where(lane == l, gain, gains)
            for j in range(l):
                cb[j] = cb[j] + dot_nt(qs[l], gfull[CROSS[(j, l)]]) - gain * hbs[l][j]
    my_act = pl.ds(pl.multiple_of(c * tseq + sx * tq, tq), tq)
    for l in range(N_LAYER):
        act[my_act, l * rank : (l + 1) * rank] = acts[l]
        act[my_act, (N_LAYER + l) * rank : (N_LAYER + l + 1) * rank] = qs[l]
    act[my_act, 2 * N_LAYER * rank :] = gains.astype(bf16)
    keys = []
    for k in range(1, N_LAYER):
        keys.append(send(act.at[my_act], act.at[my_act], line(k)))
    gpa.finish()
    gpb.finish()
    for k in range(1, N_LAYER):
        arrive(keys[k - 1], act.at[pl.ds(pl.multiple_of(c * tseq + up(sx, -k) * tq, tq), tq)])
    key_act = send(act.at[my_rows], act.at[my_rows], sib)
    arrive(key_act, act.at[its_rows])

    av = [act[:, l * rank : (l + 1) * rank] for l in range(N_LAYER)]
    qv = [act[:, (N_LAYER + l) * rank : (N_LAYER + l + 1) * rank] for l in range(N_LAYER)]
    gain_t = act[:, 2 * N_LAYER * rank :].astype(f32).T
    d0 = jnp.zeros((quad, rank), f32)
    d1 = jnp.zeros((quad, rank), f32)
    for q in range(SIDE):
        fr = slice(q * quad, (q + 1) * quad)

        def wq(arr, l):
            return w[arr, q, :, :, l * rank : (l + 1) * rank].reshape(quad, rank)

        h = xt[fr, :].astype(f32)
        hs = []
        for l in range(N_LAYER):
            hb16 = h.astype(bf16)
            hs.append(hb16)
            ht[l, fr, :] = hb16
            h = hb16.astype(f32) + dot_nt(wq(1, l), av[l])
        cot = (h - yt[fr, :].astype(f32)).astype(bf16)
        for l in range(N_LAYER - 1, -1, -1):
            ht[N_LAYER + l, fr, :] = cot
            for arr, left, right in ((2, hs[l], qv[l]), (3, cot, av[l])):
                pw = wq(arr, l).astype(f32)
                d0 = d0 + dot_nn(left[:, :tseq], right[:tseq]) * pw
                d1 = d1 + dot_nn(left[:, tseq:], right[tseq:]) * pw
            if l > 0:
                cot = (
                    cot.astype(f32) + dot_nt(wq(0, l), qv[l]) - gain_t[l : l + 1, :] * hs[l].astype(f32)
                ).astype(bf16)
    def fold(v):
        return jnp.sum(v.reshape(quad // 8, 8, rank), axis=0)

    dv_out[...] = jnp.concatenate([fold(d0), fold(d1)], axis=0)
    keys = []
    for k in range(1, 8):
        keys.append(send(dv_out, dv_in.at[k - 1], (up(sx, k // 2), fs(y, z, lax.rem(c + k, 2)))))
    dv = dv_out[...]
    for k in range(1, 8):
        arrive(keys[k - 1], dv_in.at[k - 1])
        dv = dv + dv_in[k - 1]
    s0 = jnp.sum(dv[:8], keepdims=True) / (tseq * width)
    s1 = jnp.sum(dv[8:], keepdims=True) / (tseq * width)
    token = lax.broadcasted_iota(jnp.int32, (2 * tseq, 1), 0)
    scale = jnp.where(token < tseq, s0, s1)
    qd = [(qv[l].astype(f32) * scale).astype(bf16) for l in range(N_LAYER)]
    ad = [(av[l].astype(f32) * scale).astype(bf16) for l in range(N_LAYER)]

    for arr, base, right in ((0, 0, qd), (1, N_LAYER, ad)):
        for l in range(N_LAYER):
            for q in range(SIDE):
                value = dot_nn(ht[base + l, q * quad : (q + 1) * quad, :], right[l])
                g[arr, q, :, :, l * rank : (l + 1) * rank] = value.astype(bf16).reshape(SIDE, pr, rank)

    class Scatter:
        def __init__(self, arr, last):
            self.arr, self.last, self.key = arr, last, {}
            self.at = y if last == "y" else z

        def dev(self, i, j):
            dy, dz = (i, j) if self.last == "y" else (j, i)
            return (sx, fs(up(y, dy), up(z, dz), c))

        def pair(self, p, j):
            if self.last == "y":
                return self.arr, pl.ds(2 * p, 2), up(z, j)
            return self.arr, up(y, j), pl.ds(2 * p, 2)

        def push(self, n, p, j, dj):
            self.key[n] = send(g.at[self.pair(p, j)], pair_in.at[self.arr, n], self.dev(0, dj))

        def arrived(self, n):
            arrive(self.key[n], pair_in.at[self.arr, n])
            return pair_in[self.arr, n].astype(f32)

        def start(self):
            self.push(0, 0, 2, 1)
            self.push(1, 1, 2, -1)
            self.push(2, 1, 1, 1)
            self.push(3, 0, -1, -1)

        def middle(self):
            at = self.pair(0, 1)
            g[at] = (g[at].astype(f32) + self.arrived(0)).astype(bf16)
            self.push(4, 0, 1, 1)
            at = self.pair(1, -1)
            g[at] = (g[at].astype(f32) + self.arrived(1)).astype(bf16)
            self.push(5, 1, -1, -1)

        def end(self):
            acc2[self.arr, 2:4] = g[self.pair(1, 0)].astype(f32) + self.arrived(2) + self.arrived(5)
            acc2[self.arr, 0:2] = g[self.pair(0, 0)].astype(f32) + self.arrived(3) + self.arrived(4)
            fin[self.arr, 0:SIDE] = acc2[self.arr].astype(bf16)
            for i in (2, 1, -1):
                self.key[("s", i)] = send(
                    fin.at[self.arr, up(self.at, i)], block_in.at[self.arr, i % SIDE - 1], self.dev(i, 0)
                )

        def end2(self):
            value = acc2[self.arr, self.at]
            for i in (1, -1, 2):
                arrive(self.key[("s", i)], block_in.at[self.arr, i % SIDE - 1])
                value = value + block_in[self.arr, i % SIDE - 1].astype(f32)
            fin[self.arr, SIDE] = value.astype(bf16)
            self.back = []
            for k in range(1, N_LAYER):
                to = up(sx, k)
                self.back.append(send(fin.at[self.arr, SIDE, :, cols(to)], gx.at[self.arr, sx], line(k)))
            gx[self.arr, sx] = fin[self.arr, SIDE, :, cols(sx)]

        def done(self):
            for k in range(1, N_LAYER):
                arrive(self.back[k - 1], gx.at[self.arr, up(sx, -k)])

    both = (Scatter(0, "y"), Scatter(1, "z"))
    for s in both:
        s.start()
    for s in both:
        s.middle()
    for s in both:
        s.end()
    for s in both:
        s.end2()
    for s in both:
        s.done()

    tokens_total = tseq * 2 * CHIPS
    shrink = 1.0 / (damping * tokens_total * width)
    grad = gx[...].astype(f32).reshape(2, own, rank)
    big = grad * shrink + direc

    def fold2(v):
        return jnp.sum(v.reshape(2 * own // 8, 8, rank), axis=0)

    stat_out[...] = jnp.concatenate([fold2(res * res), fold2(direc * big), fold2(res * big), fold2(big * big)], axis=0)
    keys = []
    for k in range(1, 8):
        keys.append(send(stat_out, stat_in.at[k - 1], (up(sx, k // 2), fs(y, z, lax.rem(c + k, 2)))))
    total = stat_out[...]
    for k in range(1, 8):
        arrive(keys[k - 1], stat_in.at[k - 1])
        total = total + stat_in[k - 1]
    stat2_out[...] = total
    keys = []
    for k in range(1, CHIPS):
        keys.append(send(stat2_out, stat2_in.at[k - 1], (sx, fs(up(y, k // SIDE), up(z, k % SIDE), c))))
    for k in range(1, CHIPS):
        arrive(keys[k - 1], stat2_in.at[k - 1])
        total = total + stat2_in[k - 1]
    rr = jnp.sum(total[0:8], keepdims=True)
    pq = jnp.sum(total[8:16], keepdims=True) * damping
    rp = jnp.sum(total[16:24], keepdims=True)
    pp = jnp.sum(total[24:32], keepdims=True)
    step = rr / pq * damping
    norm_new = rr - 2.0 * (step * rp) + step * (step * pp)
    beta = norm_new / rr
    new_res = res - step * big
    newres_ref[...] = new_res
    newdir_ref[...] = new_res + beta * direc
    for copy in pending:
        copy.wait_send()


def step_kernel(inputs, targets, down_proj, up_proj, direction, residual):
    tseq, width = inputs.shape
    _, own, rank = down_proj.shape
    pr = own // N_LAYER
    feats = CHIPS * pr
    tq = tseq // N_LAYER
    wide = N_LAYER * rank
    n_half = N_GRAM // 2
    n_own = n_half // N_LAYER
    vm = pltpu.VMEM
    scratch = [
        vm((tseq, width), bf16), vm((tseq, width), bf16),
        vm((2, own, rank), f32), vm((2, own, rank), f32),
        vm((2 * tseq, feats), bf16), vm((2 * tseq, feats), bf16),
        vm((tseq, feats), bf16), vm((tseq, feats), bf16),
        vm((feats, 2 * tseq), bf16), vm((feats, 2 * tseq), bf16),
        vm((4, SIDE, SIDE, pr, wide), bf16), vm((2, own, rank), bf16),
        vm((2 * tseq, 3 * wide), f32), vm((tseq, 3 * wide), bf16), vm((tseq, 3 * wide), bf16),
        vm((tseq, 3 * wide), bf16), vm((N_LAYER - 1, tq, 3 * wide), bf16),
        vm((N_GRAM, rank, rank), f32), vm((n_half, rank, rank), bf16), vm((n_half, rank, rank), bf16),
        vm((n_half, rank, rank), bf16), vm((N_LAYER - 1, n_own, rank, rank), bf16), vm((N_GRAM, rank, rank), bf16),
        vm((2 * tseq, 2 * wide + rank), bf16), vm((2 * N_LAYER, feats, 2 * tseq), bf16),
        vm((2, SIDE, SIDE, pr, wide), bf16),
        vm((2, 6, 2, pr, wide), bf16),
        vm((2, SIDE, pr, wide), f32),
        vm((2, 3, pr, wide), bf16), vm((2, SIDE + 1, pr, wide), bf16),
        vm((2, N_LAYER, pr, rank), bf16),
        vm((32, rank), f32), vm((7, 32, rank), f32), vm((32, rank), f32), vm((CHIPS - 1, 32, rank), f32),
        vm((16, rank), f32), vm((7, 16, rank), f32),
        pltpu.SemaphoreType.DMA((N_SEM,)), pltpu.SemaphoreType.DMA((N_SEM,)), pltpu.SemaphoreType.DMA((8,)),
    ]
    spec = pl.BlockSpec(memory_space=pltpu.VMEM)
    hbm = pl.BlockSpec(memory_space=pl.ANY)
    out = jax.ShapeDtypeStruct((2, own, rank), f32)
    new_res, new_dir = pl.pallas_call(
        kernel,
        out_shape=(out, out),
        in_specs=[hbm] * 6,
        out_specs=(spec, spec),
        scratch_shapes=scratch,
        compiler_params=pltpu.CompilerParams(
            collective_id=0, has_side_effects=True, vmem_limit_bytes=60 * 1024 * 1024
        ),
        cost_estimate=pl.CostEstimate(flops=4_000_000_000, bytes_accessed=8_000_000, transcendentals=0),
    )(inputs, targets, down_proj[0], up_proj[0], direction[0], residual[0])
    return new_res[None], new_dir[None]


def solution(mesh):
    in_specs = (
        P("fsdp", None),
        P("fsdp", None),
        P("section", "fsdp", None),
        P("section", "fsdp", None),
        P("section", None, "fsdp", None),
        P("section", None, "fsdp", None),
    )
    out_specs = (P("section", None, "fsdp", None), P("section", None, "fsdp", None))
    return jax.shard_map(step_kernel, mesh=mesh, in_specs=in_specs, out_specs=out_specs, check_vma=False)
```

```python
import functools

import jax
import jax.numpy as jnp
from jax import lax
from jax.experimental import pallas as pl
from jax.experimental.pallas import tpu as pltpu
from jax.sharding import PartitionSpec as P

MESH = pl.DeviceIdType.MESH
bf16 = jnp.bfloat16
f32 = jnp.float32

norm_eps = 1e-05
damping = 1e-06
N_LAYER = 4
SIDE = 4
CHIPS = 16

CROSS = {}
for _j in range(N_LAYER):
    for _l in range(_j + 1, N_LAYER):
        CROSS[(_j, _l)] = len(CROSS)
SELF = {}
for _j in range(N_LAYER):
    for _l in range(_j, N_LAYER):
        SELF[(_j, _l)] = len(CROSS) + len(SELF)
N_GRAM = len(CROSS) + len(SELF)


def dot_nn(a, b):
    return lax.dot_general(a, b, (((1,), (0,)), ((), ())), preferred_element_type=f32)


def dot_nt(a, b):
    return lax.dot_general(a, b, (((1,), (1,)), ((), ())), preferred_element_type=f32)


def dot_tn(a, b):
    return lax.dot_general(a, b, (((0,), (0,)), ((), ())), preferred_element_type=f32)


class Counter:
    def __init__(self):
        self.n = 0

    def take(self):
        self.n += 1
        return self.n - 1


N_SEM = 125


def kernel(
    x_hbm, y_hbm, a_ref, b_ref, dir_hbm, res_hbm,
    newres_ref, newdir_ref,
    xin, yin, dir_ref, res_ref, xg, yg, xs, ys, xt, yt, w, pbf,
    prod, prod_out, prod_in, prodx_out, prodx_in,
    gram, gram_out, gram_in, gramx_out, gramx_in, gfull,
    act, ht, g, pair_in, acc2, block_in, fin,
    gx, stat_out, stat_in, stat2_out, stat2_in, dv_out, dv_in,
    send_sem, recv_sem, local_sem,
):
    tseq, width = xin.shape
    rank = a_ref.shape[1]
    own = a_ref.shape[0]
    pr = own // N_LAYER
    feats = CHIPS * pr
    tq = tseq // N_LAYER
    quad = SIDE * pr
    sx = lax.axis_index("section")
    f = lax.axis_index("fsdp")
    c = lax.rem(f, 2)
    z = lax.rem(lax.div(f, 2), SIDE)
    y = lax.div(f, 2 * SIDE)

    def up(v, k):
        return lax.rem(v + k + SIDE, SIDE)

    def fs(yy, zz, cc):
        return (yy * SIDE + zz) * 2 + cc

    barrier = pltpu.get_barrier_semaphore()
    for k in range(1, 8):
        px = up(sx, k // 2)
        pc = lax.rem(c + k, 2)
        pl.semaphore_signal(barrier, inc=1, device_id=(px, fs(y, z, pc)), device_id_type=MESH)
    for k in range(1, SIDE):
        pl.semaphore_signal(barrier, inc=1, device_id=(sx, fs(up(y, k), z, c)), device_id_type=MESH)
        pl.semaphore_signal(barrier, inc=1, device_id=(sx, fs(y, up(z, k), c)), device_id_type=MESH)

    load_x = pltpu.make_async_copy(x_hbm, xin, local_sem.at[0])
    load_y = pltpu.make_async_copy(y_hbm, yin, local_sem.at[1])
    load_d = pltpu.make_async_copy(dir_hbm, dir_ref, local_sem.at[6])
    load_r = pltpu.make_async_copy(res_hbm, res_ref, local_sem.at[7])
    load_d.start()
    load_x.start()
    load_y.start()
    load_r.start()
    load_d.wait()
    pbf[...] = dir_ref[...].astype(bf16)

    pl.semaphore_wait(barrier, 7 + 2 * (SIDE - 1))

    counter = Counter()
    pending = []

    def send(src, dst, dev):
        k = counter.take()
        copy = pltpu.make_async_remote_copy(
            src_ref=src, dst_ref=dst, send_sem=send_sem.at[k], recv_sem=recv_sem.at[k],
            device_id=dev, device_id_type=MESH,
        )
        copy.start()
        pending.append(copy)
        return k

    def arrive(k, dst):
        pltpu.make_async_remote_copy(
            src_ref=dst, dst_ref=dst, send_sem=send_sem.at[k], recv_sem=recv_sem.at[k],
            device_id=(sx, f), device_id_type=MESH,
        ).wait_recv()

    sib = (sx, fs(y, z, 1 - c))

    def line(k):
        return (up(sx, k), f)

    def rows(ref, at, size):
        return ref.at[pl.ds(pl.multiple_of(at * size, size), size)]

    def cols(at):
        return pl.ds(pl.multiple_of(at * rank, rank), rank)

    def spread(srcs, arrs):
        keys = []
        for src, arr in zip(srcs, arrs):
            for k in range(1, N_LAYER):
                to = up(sx, k)
                keys.append((arr, k, send(rows(src, to, pr), w.at[arr, y, z, :, cols(sx)], line(k))))
        copies = []
        for n, (src, arr) in enumerate(zip(srcs, arrs)):
            copy = pltpu.make_async_copy(
                rows(src, sx, pr), w.at[arr, y, z, :, cols(sx)], local_sem.at[2 + arr]
            )
            copy.start()
            copies.append(copy)
        return keys, copies

    def spread_done(keys, copies):
        for copy in copies:
            copy.wait()
        for arr, k, key in keys:
            arrive(key, w.at[arr, y, z, :, cols(up(sx, -k))])

    ab_keys = spread((a_ref, b_ref), (0, 1))

    class Gather:
        def __init__(self, arr, first):
            self.arr, self.first, self.key = arr, first, {}

        def dev(self, i, j):
            dy, dz = (i, j) if self.first == "y" else (j, i)
            return (sx, fs(up(y, dy), up(z, dz), c))

        def block(self, i):
            if self.first == "y":
                return w.at[self.arr, up(y, i), z]
            return w.at[self.arr, y, up(z, i)]

        def pair(self, p, j):
            if self.first == "y":
                return w.at[self.arr, pl.ds(2 * p, 2), up(z, j)]
            return w.at[self.arr, up(y, j), pl.ds(2 * p, 2)]

        def push(self, name, ref, di, dj):
            self.key[name] = send(ref, ref, self.dev(di, dj))

        def start(self):
            for i in (2, 1, -1):
                self.push(i, self.block(0), i, 0)

        def second_direct(self):
            for i in (1, -1, 2):
                arrive(self.key[i], self.block(-i))
            for j in (2, 1, -1):
                self.key[("d", j)] = send(self.whole(0), self.whole(0), self.dev(0, j))

        def finish_direct(self):
            for j in (1, -1, 2):
                arrive(self.key[("d", j)], self.whole(-j))

        def whole(self, j):
            if self.first == "y":
                return w.at[self.arr, :, up(z, j)]
            return w.at[self.arr, up(y, j)]

        def second(self):
            for i in (1, -1, 2):
                arrive(self.key[i], self.block(-i))
            self.push("r1", self.pair(0, 0), 0, 1)
            self.push("l1", self.pair(1, 0), 0, -1)
            self.push("r2", self.pair(1, 0), 0, 1)
            self.push("l2", self.pair(0, 0), 0, -1)

        def relay(self):
            arrive(self.key["r1"], self.pair(0, -1))
            self.push("rr", self.pair(0, -1), 0, 1)
            arrive(self.key["l1"], self.pair(1, 1))
            self.push("ll", self.pair(1, 1), 0, -1)

        def finish(self):
            arrive(self.key["r2"], self.pair(1, -1))
            arrive(self.key["l2"], self.pair(0, 1))
            arrive(self.key["rr"], self.pair(0, 2))
            arrive(self.key["ll"], self.pair(1, 2))

    ga, gb = Gather(0, "y"), Gather(1, "z")
    gpa, gpb = Gather(2, "y"), Gather(3, "z")
    def pick(src, dst, cc, put):
        odd = lax.rem(sx, 2) == 1
        for p in range(0, CHIPS, 2):
            tiles = []
            for q in (p, p + 1):
                at = (2 * q + cc) * own + lax.div(sx, 2) * (2 * pr)
                tiles.append(src[:, pl.ds(pl.multiple_of(at, 2 * pr), 2 * pr)])
            even = jnp.concatenate([t[:, :pr] for t in tiles], axis=1)
            put(dst, p, jnp.where(odd, jnp.concatenate([t[:, pr:] for t in tiles], axis=1), even))

    def put_other(dst, p, value):
        dst[:, p * pr : (p + 2) * pr] = value

    def put_own(dst, p, value):
        dst[pl.ds(pl.multiple_of(c * tseq, tseq), tseq), p * pr : (p + 2) * pr] = value

    my_rows = pl.ds(pl.multiple_of(c * tseq, tseq), tseq)
    its_rows = pl.ds(pl.multiple_of((1 - c) * tseq, tseq), tseq)
    load_x.wait()
    pick(xin, xs, 1 - c, put_other)
    key_xs = send(xs, xg.at[my_rows], sib)
    load_y.wait()
    pick(yin, ys, 1 - c, put_other)
    key_ys = send(ys, yg.at[my_rows], sib)
    spread_done(*ab_keys)
    ga.start()
    gb.start()
    p_keys = spread((pbf.at[0], pbf.at[1]), (2, 3))
    pick(xin, xg, c, put_own)
    pick(yin, yg, c, put_own)
    ga.second()
    gb.second()
    xq = xin[pl.ds(pl.multiple_of(sx * tq, tq), tq), :].astype(f32)
    norm = jnp.sum(xq * xq, axis=1, keepdims=True)
    load_r.wait()
    res = res_ref[...]
    direc = dir_ref[...]
    arrive(key_xs, xg.at[its_rows])
    arrive(key_ys, yg.at[its_rows])
    xt[...] = xg[...].astype(f32).T.astype(bf16)
    yt[...] = yg[...].astype(f32).T.astype(bf16)
    ga.relay()
    gb.relay()
    spread_done(*p_keys)
    gpa.start()
    gpb.start()
    ga.finish()
    gb.finish()
    wide = N_LAYER * rank
    wa = w[0].reshape(feats, wide)
    wb = w[1].reshape(feats, wide)
    xv = xg[...]
    yv = yg[...]
    both_x = 2 * wide
    prod[:, 0:wide] = dot_nn(xv, wa)
    prod[:, wide:both_x] = dot_nn(xv, wb)
    prod_out[:, 0:both_x] = prod[its_rows, 0:both_x].astype(bf16)
    key_px = send(prod_out.at[:, 0:both_x], prod_in.at[:, 0:both_x], sib)
    n_half = N_GRAM // 2
    n_own = n_half // N_LAYER
    for j in range(N_LAYER):
        left = w[1, :, :, :, j * rank : (j + 1) * rank].reshape(feats, rank)
        if j < N_LAYER - 1:
            right = w[0, :, :, :, (j + 1) * rank : wide].reshape(feats, wide - (j + 1) * rank)
            block = dot_tn(left, right)
            for l in range(j + 1, N_LAYER):
                gram[CROSS[(j, l)]] = block[:, (l - j - 1) * rank : (l - j) * rank]
        right = w[1, :, :, :, j * rank : wide].reshape(feats, wide - j * rank)
        block = dot_tn(left, right)
        for l in range(j, N_LAYER):
            gram[SELF[(j, l)]] = block[:, (l - j) * rank : (l - j + 1) * rank]
    my_gram = pl.ds(c * n_half, n_half)
    gram_out[...] = gram[pl.ds((1 - c) * n_half, n_half)].astype(bf16)
    key_gram = send(gram_out, gram_in, sib)
    prod[:, both_x:] = dot_nn(yv, wb)
    prod_out[:, both_x:] = prod[its_rows, both_x:].astype(bf16)
    key_py = send(prod_out.at[:, both_x:], prod_in.at[:, both_x:], sib)

    def pair_sum(key, at):
        arrive(key, prod_in.at[:, at])
        pair = prod[my_rows, at] + prod_in[:, at].astype(f32)
        prod[my_rows, at] = pair
        prodx_out[:, at] = pair.astype(bf16)
        keys = []
        for k in (2, 1, 3):
            src = prodx_out.at[pl.ds(pl.multiple_of(up(sx, k) * tq, tq), tq), at]
            keys.append(send(src, prodx_in.at[k - 1, :, at], line(k)))
        return keys

    arrive(key_gram, gram_in)
    gpair = gram[my_gram] + gram_in[...].astype(f32)
    gram[my_gram] = gpair
    gramx_out[...] = gpair.astype(bf16)
    gkeys = []
    for k in (2, 1, 3):
        gkeys.append(send(gramx_out.at[pl.ds(up(sx, k) * n_own, n_own)], gramx_in.at[k - 1], line(k)))
    in_x, in_y = slice(0, both_x), slice(both_x, 3 * wide)
    pxkeys = pair_sum(key_px, in_x)
    pykeys = pair_sum(key_py, in_y)
    gpa.second_direct()
    gpb.second_direct()
    mine = pl.ds(c * n_half + sx * n_own, n_own)
    gsum = gram[mine]
    for key, k in zip(gkeys, (2, 1, 3)):
        arrive(key, gramx_in.at[k - 1])
        gsum = gsum + gramx_in[k - 1].astype(f32)
    gfull[mine] = gsum.astype(bf16)
    gkeys = []
    for k in (2, 1, 3):
        gkeys.append(send(gfull.at[mine], gfull.at[mine], line(k)))
    token_rows = pl.ds(pl.multiple_of(c * tseq + sx * tq, tq), tq)

    def line_sum(keys, at):
        total = prod[token_rows, at]
        for key, k in zip(keys, (2, 1, 3)):
            arrive(key, prodx_in.at[k - 1, :, at])
            total = total + prodx_in[k - 1, :, at].astype(f32)
        return total

    psum = line_sum(pxkeys, in_x)
    for key, k in zip(gkeys, (2, 1, 3)):
        arrive(key, gfull.at[pl.ds(c * n_half + up(sx, -k) * n_own, n_own)])
    key_gfull = send(gfull.at[my_gram], gfull.at[my_gram], sib)
    arrive(key_gfull, gfull.at[pl.ds((1 - c) * n_half, n_half)])
    def part(value, k):
        return value[:, k * rank : (k + 1) * rank]

    ha = [part(psum, l) for l in range(N_LAYER)]
    hb = [part(psum, N_LAYER + l) for l in range(N_LAYER)]
    acts, slopes, rhos, pres, hbs = [], [], [], [], []
    for l in range(N_LAYER):
        rho = jnp.sqrt(norm / width + norm_eps)
        pre = ha[l] / rho
        sig = jax.nn.sigmoid(pre)
        a = (pre * sig).astype(bf16)
        hbs.append(hb[:l])
        before = hb[l]
        for m in range(l + 1, N_LAYER):
            ha[m] = ha[m] + dot_nn(a, gfull[CROSS[(l, m)]])
        nxt = []
        for m in range(N_LAYER):
            if l <= m:
                nxt.append(hb[m] + dot_nn(a, gfull[SELF[(l, m)]]))
            else:
                nxt.append(hb[m] + dot_nt(a, gfull[SELF[(m, l)]]))
        hb = nxt
        norm = norm + jnp.sum(a.astype(f32) * (before + hb[l]), axis=1, keepdims=True)
        acts.append(a)
        slopes.append(sig * (1.0 + pre * (1.0 - sig)))
        rhos.append(rho)
        pres.append(pre)
    my_act = token_rows
    a_cols, q_cols = slice(0, wide), slice(wide, 2 * wide + rank)
    for l in range(N_LAYER):
        act[my_act, l * rank : (l + 1) * rank] = acts[l]
    akeys = [send(act.at[my_act, a_cols], act.at[my_act, a_cols], line(k)) for k in (2, 1, 3)]
    ysum = line_sum(pykeys, in_y)
    cb = [hb[l] - part(ysum, l) for l in range(N_LAYER)]
    qs = [None] * N_LAYER
    lane = lax.broadcasted_iota(jnp.int32, (tq, rank), 1)
    gains = jnp.zeros((tq, rank), f32)
    for l in range(N_LAYER - 1, -1, -1):
        cot = cb[l] * slopes[l]
        qs[l] = (cot / rhos[l]).astype(bf16)
        if l > 0:
            gain = jnp.sum(cot * pres[l], axis=1, keepdims=True) / (width * rhos[l] * rhos[l])
            gains = jnp.where(lane == l, gain, gains)
            for j in range(l):
                cb[j] = cb[j] + dot_nt(qs[l], gfull[CROSS[(j, l)]]) - gain * hbs[l][j]
    for l in range(N_LAYER):
        act[my_act, (N_LAYER + l) * rank : (N_LAYER + l + 1) * rank] = qs[l]
    act[my_act, 2 * wide :] = gains.astype(bf16)
    qkeys = [send(act.at[my_act, q_cols], act.at[my_act, q_cols], line(k)) for k in (2, 1, 3)]
    sib_keys = []
    for at, keys in ((a_cols, akeys), (q_cols, qkeys)):
        for key, k in zip(keys, (2, 1, 3)):
            arrive(key, act.at[pl.ds(pl.multiple_of(c * tseq + up(sx, -k) * tq, tq), tq), at])
        sib_keys.append(send(act.at[my_rows, at], act.at[my_rows, at], sib))
    gpa.finish_direct()
    gpb.finish_direct()
    for key, at in zip(sib_keys, (a_cols, q_cols)):
        arrive(key, act.at[its_rows, at])

    av = [act[:, l * rank : (l + 1) * rank] for l in range(N_LAYER)]
    qv = [act[:, (N_LAYER + l) * rank : (N_LAYER + l + 1) * rank] for l in range(N_LAYER)]
    gain_t = act[:, 2 * N_LAYER * rank :].astype(f32).T
    d0 = jnp.zeros((quad, rank), f32)
    d1 = jnp.zeros((quad, rank), f32)
    for q in range(SIDE):
        fr = slice(q * quad, (q + 1) * quad)

        def wq(arr, l):
            return w[arr, q, :, :, l * rank : (l + 1) * rank].reshape(quad, rank)

        h = xt[fr, :].astype(f32)
        hs = []
        for l in range(N_LAYER):
            hb16 = h.astype(bf16)
            hs.append(hb16)
            ht[l, fr, :] = hb16
            h = hb16.astype(f32) + dot_nt(wq(1, l), av[l])
        cot = (h - yt[fr, :].astype(f32)).astype(bf16)
        for l in range(N_LAYER - 1, -1, -1):
            ht[N_LAYER + l, fr, :] = cot
            for arr, left, right in ((2, hs[l], qv[l]), (3, cot, av[l])):
                pw = wq(arr, l).astype(f32)
                d0 = d0 + dot_nn(left[:, :tseq], right[:tseq]) * pw
                d1 = d1 + dot_nn(left[:, tseq:], right[tseq:]) * pw
            if l > 0:
                cot = (
                    cot.astype(f32) + dot_nt(wq(0, l), qv[l]) - gain_t[l : l + 1, :] * hs[l].astype(f32)
                ).astype(bf16)
    def fold(v):
        return jnp.sum(v.reshape(quad // 8, 8, rank), axis=0)

    dv_out[...] = jnp.concatenate([fold(d0), fold(d1)], axis=0)
    keys = []
    for k in range(1, 8):
        keys.append(send(dv_out, dv_in.at[k - 1], (up(sx, k // 2), fs(y, z, lax.rem(c + k, 2)))))
    dv = dv_out[...]
    for k in range(1, 8):
        arrive(keys[k - 1], dv_in.at[k - 1])
        dv = dv + dv_in[k - 1]
    s0 = jnp.sum(dv[:8], keepdims=True) / (tseq * width)
    s1 = jnp.sum(dv[8:], keepdims=True) / (tseq * width)
    token = lax.broadcasted_iota(jnp.int32, (2 * tseq, 1), 0)
    scale = jnp.where(token < tseq, s0, s1)
    qd = [(qv[l].astype(f32) * scale).astype(bf16) for l in range(N_LAYER)]
    ad = [(av[l].astype(f32) * scale).astype(bf16) for l in range(N_LAYER)]

    for arr, base, right in ((0, 0, qd), (1, N_LAYER, ad)):
        for l in range(N_LAYER):
            for q in range(SIDE):
                value = dot_nn(ht[base + l, q * quad : (q + 1) * quad, :], right[l])
                g[arr, q, :, :, l * rank : (l + 1) * rank] = value.astype(bf16).reshape(SIDE, pr, rank)

    class Scatter:
        def __init__(self, arr, last):
            self.arr, self.last, self.key = arr, last, {}
            self.at = y if last == "y" else z

        def dev(self, i, j):
            dy, dz = (i, j) if self.last == "y" else (j, i)
            return (sx, fs(up(y, dy), up(z, dz), c))

        def pair(self, p, j):
            if self.last == "y":
                return self.arr, pl.ds(2 * p, 2), up(z, j)
            return self.arr, up(y, j), pl.ds(2 * p, 2)

        def push(self, n, p, j, dj):
            self.key[n] = send(g.at[self.pair(p, j)], pair_in.at[self.arr, n], self.dev(0, dj))

        def arrived(self, n):
            arrive(self.key[n], pair_in.at[self.arr, n])
            return pair_in[self.arr, n].astype(f32)

        def start(self):
            self.push(0, 0, 2, 1)
            self.push(1, 1, 2, -1)
            self.push(2, 1, 1, 1)
            self.push(3, 0, -1, -1)

        def middle(self):
            at = self.pair(0, 1)
            g[at] = (g[at].astype(f32) + self.arrived(0)).astype(bf16)
            self.push(4, 0, 1, 1)
            at = self.pair(1, -1)
            g[at] = (g[at].astype(f32) + self.arrived(1)).astype(bf16)
            self.push(5, 1, -1, -1)

        def end(self):
            acc2[self.arr, 2:4] = g[self.pair(1, 0)].astype(f32) + self.arrived(2) + self.arrived(5)
            acc2[self.arr, 0:2] = g[self.pair(0, 0)].astype(f32) + self.arrived(3) + self.arrived(4)
            fin[self.arr, 0:SIDE] = acc2[self.arr].astype(bf16)
            for i in (2, 1, -1):
                self.key[("s", i)] = send(
                    fin.at[self.arr, up(self.at, i)], block_in.at[self.arr, i % SIDE - 1], self.dev(i, 0)
                )

        def end2(self):
            value = acc2[self.arr, self.at]
            for i in (1, -1, 2):
                arrive(self.key[("s", i)], block_in.at[self.arr, i % SIDE - 1])
                value = value + block_in[self.arr, i % SIDE - 1].astype(f32)
            fin[self.arr, SIDE] = value.astype(bf16)
            self.back = []
            for k in range(1, N_LAYER):
                to = up(sx, k)
                self.back.append(send(fin.at[self.arr, SIDE, :, cols(to)], gx.at[self.arr, sx], line(k)))
            gx[self.arr, sx] = fin[self.arr, SIDE, :, cols(sx)]

        def done(self):
            for k in range(1, N_LAYER):
                arrive(self.back[k - 1], gx.at[self.arr, up(sx, -k)])

    both = (Scatter(0, "y"), Scatter(1, "z"))
    for s in both:
        s.start()
    for s in both:
        s.middle()
    for s in both:
        s.end()
    for s in both:
        s.end2()
    for s in both:
        s.done()

    tokens_total = tseq * 2 * CHIPS
    shrink = 1.0 / (damping * tokens_total * width)
    grad = gx[...].astype(f32).reshape(2, own, rank)
    big = grad * shrink + direc

    def fold2(v):
        return jnp.sum(v.reshape(2 * own // 8, 8, rank), axis=0)

    stat_out[...] = jnp.concatenate([fold2(res * res), fold2(direc * big), fold2(res * big), fold2(big * big)], axis=0)
    keys = []
    for k in range(1, 8):
        keys.append(send(stat_out, stat_in.at[k - 1], (up(sx, k // 2), fs(y, z, lax.rem(c + k, 2)))))
    total = stat_out[...]
    for k in range(1, 8):
        arrive(keys[k - 1], stat_in.at[k - 1])
        total = total + stat_in[k - 1]
    stat2_out[...] = total
    keys = []
    for k in range(1, CHIPS):
        keys.append(send(stat2_out, stat2_in.at[k - 1], (sx, fs(up(y, k // SIDE), up(z, k % SIDE), c))))
    for k in range(1, CHIPS):
        arrive(keys[k - 1], stat2_in.at[k - 1])
        total = total + stat2_in[k - 1]
    rr = jnp.sum(total[0:8], keepdims=True)
    pq = jnp.sum(total[8:16], keepdims=True) * damping
    rp = jnp.sum(total[16:24], keepdims=True)
    pp = jnp.sum(total[24:32], keepdims=True)
    step = rr / pq * damping
    norm_new = rr - 2.0 * (step * rp) + step * (step * pp)
    beta = norm_new / rr
    new_res = res - step * big
    newres_ref[...] = new_res
    newdir_ref[...] = new_res + beta * direc
    for copy in pending:
        copy.wait_send()


def step_kernel(inputs, targets, down_proj, up_proj, direction, residual):
    tseq, width = inputs.shape
    _, own, rank = down_proj.shape
    pr = own // N_LAYER
    feats = CHIPS * pr
    tq = tseq // N_LAYER
    wide = N_LAYER * rank
    n_half = N_GRAM // 2
    n_own = n_half // N_LAYER
    vm = pltpu.VMEM
    scratch = [
        vm((tseq, width), bf16), vm((tseq, width), bf16),
        vm((2, own, rank), f32), vm((2, own, rank), f32),
        vm((2 * tseq, feats), bf16), vm((2 * tseq, feats), bf16),
        vm((tseq, feats), bf16), vm((tseq, feats), bf16),
        vm((feats, 2 * tseq), bf16), vm((feats, 2 * tseq), bf16),
        vm((4, SIDE, SIDE, pr, wide), bf16), vm((2, own, rank), bf16),
        vm((2 * tseq, 3 * wide), f32), vm((tseq, 3 * wide), bf16), vm((tseq, 3 * wide), bf16),
        vm((tseq, 3 * wide), bf16), vm((N_LAYER - 1, tq, 3 * wide), bf16),
        vm((N_GRAM, rank, rank), f32), vm((n_half, rank, rank), bf16), vm((n_half, rank, rank), bf16),
        vm((n_half, rank, rank), bf16), vm((N_LAYER - 1, n_own, rank, rank), bf16), vm((N_GRAM, rank, rank), bf16),
        vm((2 * tseq, 2 * wide + rank), bf16), vm((2 * N_LAYER, feats, 2 * tseq), bf16),
        vm((2, SIDE, SIDE, pr, wide), bf16),
        vm((2, 6, 2, pr, wide), bf16),
        vm((2, SIDE, pr, wide), f32),
        vm((2, 3, pr, wide), bf16), vm((2, SIDE + 1, pr, wide), bf16),
        vm((2, N_LAYER, pr, rank), bf16),
        vm((32, rank), f32), vm((7, 32, rank), f32), vm((32, rank), f32), vm((CHIPS - 1, 32, rank), f32),
        vm((16, rank), f32), vm((7, 16, rank), f32),
        pltpu.SemaphoreType.DMA((N_SEM,)), pltpu.SemaphoreType.DMA((N_SEM,)), pltpu.SemaphoreType.DMA((8,)),
    ]
    spec = pl.BlockSpec(memory_space=pltpu.VMEM)
    hbm = pl.BlockSpec(memory_space=pl.ANY)
    out = jax.ShapeDtypeStruct((2, own, rank), f32)
    new_res, new_dir = pl.pallas_call(
        kernel,
        out_shape=(out, out),
        in_specs=[hbm] * 6,
        out_specs=(spec, spec),
        scratch_shapes=scratch,
        compiler_params=pltpu.CompilerParams(
            collective_id=0, has_side_effects=True, vmem_limit_bytes=52 * 1024 * 1024
        ),
        cost_estimate=pl.CostEstimate(flops=4_000_000_000, bytes_accessed=8_000_000, transcendentals=0),
    )(inputs, targets, down_proj[0], up_proj[0], direction[0], residual[0])
    return new_res[None], new_dir[None]


def solution(mesh):
    in_specs = (
        P("fsdp", None),
        P("fsdp", None),
        P("section", "fsdp", None),
        P("section", "fsdp", None),
        P("section", None, "fsdp", None),
        P("section", None, "fsdp", None),
    )
    out_specs = (P("section", None, "fsdp", None), P("section", None, "fsdp", None))
    return jax.shard_map(step_kernel, mesh=mesh, in_specs=in_specs, out_specs=out_specs, check_vma=False)
```

```python
import functools

import jax
import jax.numpy as jnp
from jax import lax
from jax.experimental import pallas as pl
from jax.experimental.pallas import tpu as pltpu
from jax.sharding import PartitionSpec as P

MESH = pl.DeviceIdType.MESH
bf16 = jnp.bfloat16
f32 = jnp.float32

norm_eps = 1e-05
damping = 1e-06
N_LAYER = 4
SIDE = 4
CHIPS = 16

CROSS = {}
for _j in range(N_LAYER):
    for _l in range(_j + 1, N_LAYER):
        CROSS[(_j, _l)] = len(CROSS)
SELF = {}
for _j in range(N_LAYER):
    for _l in range(_j, N_LAYER):
        SELF[(_j, _l)] = len(CROSS) + len(SELF)
N_GRAM = len(CROSS) + len(SELF)


def dot_nn(a, b):
    return lax.dot_general(a, b, (((1,), (0,)), ((), ())), preferred_element_type=f32)


def dot_nt(a, b):
    return lax.dot_general(a, b, (((1,), (1,)), ((), ())), preferred_element_type=f32)


def dot_tn(a, b):
    return lax.dot_general(a, b, (((0,), (0,)), ((), ())), preferred_element_type=f32)


class Counter:
    def __init__(self):
        self.n = 0

    def take(self):
        self.n += 1
        return self.n - 1


N_SEM = 148


def kernel(
    x_hbm, y_hbm, a_ref, b_ref, dir_hbm, res_hbm,
    big_hbm, coef_ref,
    xin, yin, dir_ref, res_ref, xg, yg, xs, ys, xt, yt, w, pbf,
    prod, prod_out, prod_in, prodx_out, prodx_in,
    gram, gram_out, gram_in, gramx_out, gramx_in, gline_out, gline_in, gfull, res_s, big_vmem,
    act, ht, g, pair_in, acc2, block_in, fin,
    gx, stat_out, stat_in, stat2_out, stat2_in, dv_out, dv_in,
    send_sem, recv_sem, local_sem,
):
    tseq, width = xin.shape
    rank = a_ref.shape[1]
    own = a_ref.shape[0]
    pr = own // N_LAYER
    feats = CHIPS * pr
    tq = tseq // N_LAYER
    quad = SIDE * pr
    sx = lax.axis_index("section")
    f = lax.axis_index("fsdp")
    c = lax.rem(f, 2)
    z = lax.rem(lax.div(f, 2), SIDE)
    y = lax.div(f, 2 * SIDE)

    def up(v, k):
        return lax.rem(v + k + SIDE, SIDE)

    def fs(yy, zz, cc):
        return (yy * SIDE + zz) * 2 + cc

    barrier = pltpu.get_barrier_semaphore()
    sib = (sx, fs(y, z, 1 - c))

    def line(k):
        return (up(sx, k), f)

    for k in range(1, N_LAYER):
        pl.semaphore_signal(barrier, inc=1, device_id=line(k), device_id_type=MESH)
    pl.semaphore_signal(barrier, inc=1, device_id=sib, device_id_type=MESH)
    for k in range(1, SIDE):
        pl.semaphore_signal(barrier, inc=1, device_id=(sx, fs(up(y, k), z, c)), device_id_type=MESH)
        pl.semaphore_signal(barrier, inc=1, device_id=(sx, fs(y, up(z, k), c)), device_id_type=MESH)

    load_x = pltpu.make_async_copy(x_hbm, xin, local_sem.at[0])
    load_y = pltpu.make_async_copy(y_hbm, yin, local_sem.at[1])
    load_d = pltpu.make_async_copy(dir_hbm, dir_ref, local_sem.at[6])
    load_r = pltpu.make_async_copy(res_hbm, res_ref, local_sem.at[7])
    load_d.start()
    load_x.start()
    load_y.start()
    load_r.start()
    load_d.wait()
    pbf[...] = dir_ref[...].astype(bf16)

    pl.semaphore_wait(barrier, 1 + 3 * (SIDE - 1))

    counter = Counter()
    pending = []

    def send(src, dst, dev):
        k = counter.take()
        copy = pltpu.make_async_remote_copy(
            src_ref=src, dst_ref=dst, send_sem=send_sem.at[k], recv_sem=recv_sem.at[k],
            device_id=dev, device_id_type=MESH,
        )
        copy.start()
        pending.append(copy)
        return k

    def arrive(k, dst):
        pltpu.make_async_remote_copy(
            src_ref=dst, dst_ref=dst, send_sem=send_sem.at[k], recv_sem=recv_sem.at[k],
            device_id=(sx, f), device_id_type=MESH,
        ).wait_recv()

    def rows(ref, at, size):
        return ref.at[pl.ds(pl.multiple_of(at * size, size), size)]

    def rows2(ref, at):
        return ref.at[:, pl.ds(pl.multiple_of(at * pr, pr), pr)]

    def cols(at):
        return pl.ds(pl.multiple_of(at * rank, rank), rank)

    def spread(srcs, arrs):
        keys = []
        for src, arr in zip(srcs, arrs):
            for k in range(1, N_LAYER):
                to = up(sx, k)
                keys.append((arr, k, send(rows(src, to, pr), w.at[arr, y, z, :, cols(sx)], line(k))))
        copies = []
        for n, (src, arr) in enumerate(zip(srcs, arrs)):
            copy = pltpu.make_async_copy(
                rows(src, sx, pr), w.at[arr, y, z, :, cols(sx)], local_sem.at[2 + arr]
            )
            copy.start()
            copies.append(copy)
        return keys, copies

    def spread_done(keys, copies):
        for copy in copies:
            copy.wait()
        for arr, k, key in keys:
            arrive(key, w.at[arr, y, z, :, cols(up(sx, -k))])

    ab_keys = spread((a_ref, b_ref), (0, 1))

    class Gather:
        def __init__(self, arr, first):
            self.arr, self.first, self.key = arr, first, {}

        def dev(self, i, j):
            dy, dz = (i, j) if self.first == "y" else (j, i)
            return (sx, fs(up(y, dy), up(z, dz), c))

        def block(self, i):
            if self.first == "y":
                return w.at[self.arr, up(y, i), z]
            return w.at[self.arr, y, up(z, i)]

        def pair(self, p, j):
            if self.first == "y":
                return w.at[self.arr, pl.ds(2 * p, 2), up(z, j)]
            return w.at[self.arr, up(y, j), pl.ds(2 * p, 2)]

        def push(self, name, ref, di, dj):
            self.key[name] = send(ref, ref, self.dev(di, dj))

        def start(self):
            for i in (2, 1, -1):
                self.push(i, self.block(0), i, 0)

        def second_direct(self):
            for i in (1, -1, 2):
                arrive(self.key[i], self.block(-i))
            for j in (2, 1, -1):
                self.key[("d", j)] = send(self.whole(0), self.whole(0), self.dev(0, j))

        def finish_direct(self):
            for j in (1, -1, 2):
                arrive(self.key[("d", j)], self.whole(-j))

        def whole(self, j):
            if self.first == "y":
                return w.at[self.arr, :, up(z, j)]
            return w.at[self.arr, up(y, j)]

        def second(self):
            for i in (1, -1, 2):
                arrive(self.key[i], self.block(-i))
            self.push("r1", self.pair(0, 0), 0, 1)
            self.push("l1", self.pair(1, 0), 0, -1)
            self.push("r2", self.pair(1, 0), 0, 1)
            self.push("l2", self.pair(0, 0), 0, -1)

        def relay(self):
            arrive(self.key["r1"], self.pair(0, -1))
            self.push("rr", self.pair(0, -1), 0, 1)
            arrive(self.key["l1"], self.pair(1, 1))
            self.push("ll", self.pair(1, 1), 0, -1)

        def finish(self):
            arrive(self.key["r2"], self.pair(1, -1))
            arrive(self.key["l2"], self.pair(0, 1))
            arrive(self.key["rr"], self.pair(0, 2))
            arrive(self.key["ll"], self.pair(1, 2))

    ga, gb = Gather(0, "y"), Gather(1, "z")
    gpa, gpb = Gather(2, "y"), Gather(3, "z")
    def pick(src, dst, cc, put):
        odd = lax.rem(sx, 2) == 1
        for p in range(0, CHIPS, 2):
            tiles = []
            for q in (p, p + 1):
                at = (2 * q + cc) * own + lax.div(sx, 2) * (2 * pr)
                tiles.append(src[:, pl.ds(pl.multiple_of(at, 2 * pr), 2 * pr)])
            even = jnp.concatenate([t[:, :pr] for t in tiles], axis=1)
            put(dst, p, jnp.where(odd, jnp.concatenate([t[:, pr:] for t in tiles], axis=1), even))

    def put_other(dst, p, value):
        dst[:, p * pr : (p + 2) * pr] = value

    def put_own(dst, p, value):
        dst[pl.ds(pl.multiple_of(c * tseq, tseq), tseq), p * pr : (p + 2) * pr] = value

    my_rows = pl.ds(pl.multiple_of(c * tseq, tseq), tseq)
    its_rows = pl.ds(pl.multiple_of((1 - c) * tseq, tseq), tseq)
    load_x.wait()
    pick(xin, xs, 1 - c, put_other)
    key_xs = send(xs, xg.at[my_rows], sib)
    load_y.wait()
    pick(yin, ys, 1 - c, put_other)
    key_ys = send(ys, yg.at[my_rows], sib)
    spread_done(*ab_keys)
    ga.start()
    gb.start()
    p_keys = [send(rows2(pbf, up(sx, k)), w.at[2:4, y, z, :, cols(sx)], line(k)) for k in (2, 1, 3)]
    copy_p = pltpu.make_async_copy(rows2(pbf, sx), w.at[2:4, y, z, :, cols(sx)], local_sem.at[4])
    copy_p.start()
    half_rows = rank // 2
    mine_a, mine_b = w[0, y, z], w[1, y, z]
    for j in range(N_LAYER):
        left = mine_b[:, j * rank : (j + 1) * rank]
        if j < N_LAYER - 1:
            block = dot_tn(left, mine_a[:, (j + 1) * rank :])
            for l in range(j + 1, N_LAYER):
                b = CROSS[(j, l)]
                gram[2 * b : 2 * b + 2] = block[:, (l - j - 1) * rank : (l - j) * rank].reshape(2, half_rows, rank)
        block = dot_tn(left, mine_b[:, j * rank :])
        for l in range(j, N_LAYER):
            b = SELF[(j, l)]
            gram[2 * b : 2 * b + 2] = block[:, (l - j) * rank : (l - j + 1) * rank].reshape(2, half_rows, rank)
    my_gram = pl.ds(c * CHIPS, CHIPS)
    its_gram = pl.ds((1 - c) * CHIPS, CHIPS)
    gram_out[...] = gram[its_gram].astype(bf16)
    key_gram = send(gram_out, gram_in, sib)
    pick(xin, xg, c, put_own)
    pick(yin, yg, c, put_own)
    arrive(key_gram, gram_in)
    gpair = gram[my_gram] + gram_in[...].astype(f32)
    gram[my_gram] = gpair
    gramx_out[...] = gpair.astype(bf16)

    def chip(k):
        return up(y, k // SIDE) * SIDE + up(z, k % SIDE)

    def chip_dev(k):
        return (sx, fs(up(y, k // SIDE), up(z, k % SIDE), c))

    def chip_back(k):
        return up(y, -(k // SIDE)) * SIDE + up(z, -(k % SIDE))

    ga.second()
    gb.second()
    gkeys = [send(gramx_out.at[chip(k)], gramx_in.at[k - 1], chip_dev(k)) for k in range(1, CHIPS)]
    xq = xin[pl.ds(pl.multiple_of(sx * tq, tq), tq), :].astype(f32)
    norm = jnp.sum(xq * xq, axis=1, keepdims=True)
    load_r.wait()
    res = res_ref[...]
    direc = dir_ref[...]

    def fold_home(v):
        return jnp.sum(v.reshape(-1, rank), axis=0, keepdims=True)

    dd = fold_home(direc * direc)
    home = jnp.concatenate(
        [fold_home(res * res), dd, fold_home(res * direc), dd, jnp.zeros((4, rank), f32)], axis=0
    )
    arrive(key_xs, xg.at[its_rows])
    arrive(key_ys, yg.at[its_rows])
    xt[...] = xg[...].astype(f32).T.astype(bf16)
    yt[...] = yg[...].astype(f32).T.astype(bf16)
    my_piece = c * CHIPS + y * SIDE + z
    gsum = gram[my_piece]
    for k in range(1, CHIPS):
        arrive(gkeys[k - 1], gramx_in.at[k - 1])
        gsum = gsum + gramx_in[k - 1].astype(f32)
    gline_out[...] = gsum.astype(bf16)
    gkeys = [send(gline_out, gline_in.at[k - 1], line(k)) for k in (2, 1, 3)]
    ga.relay()
    gb.relay()
    for key, k in zip(gkeys, (2, 1, 3)):
        arrive(key, gline_in.at[k - 1])
        gsum = gsum + gline_in[k - 1].astype(f32)
    gfull[my_piece] = gsum.astype(bf16)
    gkeys = [send(gfull.at[my_piece], gfull.at[my_piece], chip_dev(k)) for k in range(1, CHIPS)]
    res_keys = [send(rows2(res_ref, up(sx, k)), res_s.at[:, :, cols(sx)], line(k)) for k in (2, 1, 3)]
    res_s[:, :, cols(sx)] = res_ref[:, pl.ds(pl.multiple_of(sx * pr, pr), pr)]
    copy_p.wait()
    for key, k in zip(p_keys, (2, 1, 3)):
        arrive(key, w.at[2:4, y, z, :, cols(up(sx, -k))])
    gpa.start()
    gpb.start()
    ga.finish()
    gb.finish()
    wide = N_LAYER * rank
    wa = w[0].reshape(feats, wide)
    wb = w[1].reshape(feats, wide)
    xv = xg[...]
    yv = yg[...]
    both_x = 2 * wide
    prod[:, 0:wide] = dot_nn(xv, wa)
    prod[:, wide:both_x] = dot_nn(xv, wb)
    prod_out[:, 0:both_x] = prod[its_rows, 0:both_x].astype(bf16)
    key_px = send(prod_out.at[:, 0:both_x], prod_in.at[:, 0:both_x], sib)
    prod[:, both_x:] = dot_nn(yv, wb)
    prod_out[:, both_x:] = prod[its_rows, both_x:].astype(bf16)
    key_py = send(prod_out.at[:, both_x:], prod_in.at[:, both_x:], sib)

    def pair_sum(key, at):
        arrive(key, prod_in.at[:, at])
        pair = prod[my_rows, at] + prod_in[:, at].astype(f32)
        prod[my_rows, at] = pair
        prodx_out[:, at] = pair.astype(bf16)
        keys = []
        for k in (2, 1, 3):
            src = prodx_out.at[pl.ds(pl.multiple_of(up(sx, k) * tq, tq), tq), at]
            keys.append(send(src, prodx_in.at[k - 1, :, at], line(k)))
        return keys

    in_x, in_y = slice(0, both_x), slice(both_x, 3 * wide)
    pxkeys = pair_sum(key_px, in_x)
    pykeys = pair_sum(key_py, in_y)
    for k in range(1, CHIPS):
        arrive(gkeys[k - 1], gfull.at[c * CHIPS + chip_back(k)])
    key_gfull = send(gfull.at[my_gram], gfull.at[my_gram], sib)
    gpa.second_direct()
    gpb.second_direct()
    token_rows = pl.ds(pl.multiple_of(c * tseq + sx * tq, tq), tq)

    def line_sum(keys, at):
        total = prod[token_rows, at]
        for key, k in zip(keys, (2, 1, 3)):
            arrive(key, prodx_in.at[k - 1, :, at])
            total = total + prodx_in[k - 1, :, at].astype(f32)
        return total

    psum = line_sum(pxkeys, in_x)
    arrive(key_gfull, gfull.at[its_gram])

    def gblock(b):
        return gfull[2 * b : 2 * b + 2].reshape(rank, rank)

    def part(value, k):
        return value[:, k * rank : (k + 1) * rank]

    ha = [part(psum, l) for l in range(N_LAYER)]
    hb = [part(psum, N_LAYER + l) for l in range(N_LAYER)]
    acts, slopes, rhos, pres, hbs = [], [], [], [], []
    for l in range(N_LAYER):
        rho = jnp.sqrt(norm / width + norm_eps)
        pre = ha[l] / rho
        sig = jax.nn.sigmoid(pre)
        a = (pre * sig).astype(bf16)
        hbs.append(hb[:l])
        before = hb[l]
        for m in range(l + 1, N_LAYER):
            ha[m] = ha[m] + dot_nn(a, gblock(CROSS[(l, m)]))
        nxt = []
        for m in range(N_LAYER):
            if l <= m:
                nxt.append(hb[m] + dot_nn(a, gblock(SELF[(l, m)])))
            else:
                nxt.append(hb[m] + dot_nt(a, gblock(SELF[(m, l)])))
        hb = nxt
        norm = norm + jnp.sum(a.astype(f32) * (before + hb[l]), axis=1, keepdims=True)
        acts.append(a)
        slopes.append(sig * (1.0 + pre * (1.0 - sig)))
        rhos.append(rho)
        pres.append(pre)
    my_act = token_rows
    a_cols, q_cols = slice(0, wide), slice(wide, 2 * wide + rank)
    for l in range(N_LAYER):
        act[my_act, l * rank : (l + 1) * rank] = acts[l]
    akeys = [send(act.at[my_act, a_cols], act.at[my_act, a_cols], line(k)) for k in (2, 1, 3)]
    ysum = line_sum(pykeys, in_y)
    cb = [hb[l] - part(ysum, l) for l in range(N_LAYER)]
    qs = [None] * N_LAYER
    lane = lax.broadcasted_iota(jnp.int32, (tq, rank), 1)
    gains = jnp.zeros((tq, rank), f32)
    for l in range(N_LAYER - 1, -1, -1):
        cot = cb[l] * slopes[l]
        qs[l] = (cot / rhos[l]).astype(bf16)
        if l > 0:
            gain = jnp.sum(cot * pres[l], axis=1, keepdims=True) / (width * rhos[l] * rhos[l])
            gains = jnp.where(lane == l, gain, gains)
            for j in range(l):
                cb[j] = cb[j] + dot_nt(qs[l], gblock(CROSS[(j, l)])) - gain * hbs[l][j]
    for l in range(N_LAYER):
        act[my_act, (N_LAYER + l) * rank : (N_LAYER + l + 1) * rank] = qs[l]
    act[my_act, 2 * wide :] = gains.astype(bf16)
    qkeys = [send(act.at[my_act, q_cols], act.at[my_act, q_cols], line(k)) for k in (2, 1, 3)]
    def share(keys, at):
        for key, k in zip(keys, (2, 1, 3)):
            arrive(key, act.at[pl.ds(pl.multiple_of(c * tseq + up(sx, -k) * tq, tq), tq), at])
        return send(act.at[my_rows, at], act.at[my_rows, at], sib)

    key = share(akeys, a_cols)
    arrive(key, act.at[its_rows, a_cols])

    def wq(arr, l, q):
        return w[arr, q, :, :, l * rank : (l + 1) * rank].reshape(quad, rank)

    av = [act[:, l * rank : (l + 1) * rank] for l in range(N_LAYER)]
    for q in range(SIDE):
        fr = slice(q * quad, (q + 1) * quad)
        h = xt[fr, :].astype(f32)
        for l in range(N_LAYER):
            hb16 = h.astype(bf16)
            ht[l, fr, :] = hb16
            h = hb16.astype(f32) + dot_nt(wq(1, l, q), av[l])
        ht[2 * N_LAYER - 1, fr, :] = (h - yt[fr, :].astype(f32)).astype(bf16)
    key = share(qkeys, q_cols)
    gpa.finish_direct()
    gpb.finish_direct()
    arrive(key, act.at[its_rows, q_cols])
    qv = [act[:, (N_LAYER + l) * rank : (N_LAYER + l + 1) * rank] for l in range(N_LAYER)]
    gain_t = act[:, 2 * N_LAYER * rank :].astype(f32).T
    d0 = jnp.zeros((quad, rank), f32)
    d1 = jnp.zeros((quad, rank), f32)
    for q in range(SIDE):
        fr = slice(q * quad, (q + 1) * quad)
        cot = ht[2 * N_LAYER - 1, fr, :]
        for l in range(N_LAYER - 1, -1, -1):
            hl = ht[l, fr, :]
            for arr, left, right in ((2, hl, qv[l]), (3, cot, av[l])):
                pw = wq(arr, l, q).astype(f32)
                d0 = d0 + dot_nn(left[:, :tseq], right[:tseq]) * pw
                d1 = d1 + dot_nn(left[:, tseq:], right[tseq:]) * pw
            if l > 0:
                cot = (
                    cot.astype(f32) + dot_nt(wq(0, l, q), qv[l]) - gain_t[l : l + 1, :] * hl.astype(f32)
                ).astype(bf16)
                ht[N_LAYER + l - 1, fr, :] = cot

    def fold(v):
        return jnp.sum(v.reshape(-1, rank), axis=0, keepdims=True)

    def stack(values):
        return jnp.concatenate([fold(v) for v in values] + [jnp.zeros((8 - len(values), rank), f32)], axis=0)

    dv_out[...] = stack([d0, d1])
    keys = []
    for k in range(1, 8):
        keys.append(send(dv_out, dv_in.at[k - 1], (up(sx, k // 2), fs(y, z, lax.rem(c + k, 2)))))
    dv = dv_out[...]
    for k in range(1, 8):
        arrive(keys[k - 1], dv_in.at[k - 1])
        dv = dv + dv_in[k - 1]
    s0 = jnp.sum(dv[0:1], keepdims=True) / (tseq * width)
    s1 = jnp.sum(dv[1:2], keepdims=True) / (tseq * width)
    token = lax.broadcasted_iota(jnp.int32, (2 * tseq, 1), 0)
    scale = jnp.where(token < tseq, s0, s1)
    qd = [(qv[l].astype(f32) * scale).astype(bf16) for l in range(N_LAYER)]
    ad = [(av[l].astype(f32) * scale).astype(bf16) for l in range(N_LAYER)]

    def gradient(arr, base, right):
        for l in range(N_LAYER):
            for q in range(SIDE):
                value = dot_nn(ht[base + l, q * quad : (q + 1) * quad, :], right[l])
                g[arr, q, :, :, l * rank : (l + 1) * rank] = value.astype(bf16).reshape(SIDE, pr, rank)

    class Scatter:
        def __init__(self, arr, last):
            self.arr, self.last, self.key = arr, last, {}
            self.at = y if last == "y" else z

        def dev(self, i, j):
            dy, dz = (i, j) if self.last == "y" else (j, i)
            return (sx, fs(up(y, dy), up(z, dz), c))

        def pair(self, p, j):
            if self.last == "y":
                return self.arr, pl.ds(2 * p, 2), up(z, j)
            return self.arr, up(y, j), pl.ds(2 * p, 2)

        def push(self, n, p, j, dj):
            self.key[n] = send(g.at[self.pair(p, j)], pair_in.at[self.arr, n], self.dev(0, dj))

        def arrived(self, n):
            arrive(self.key[n], pair_in.at[self.arr, n])
            return pair_in[self.arr, n].astype(f32)

        def start(self):
            self.push(0, 0, 2, 1)
            self.push(1, 1, 2, -1)
            self.push(2, 1, 1, 1)
            self.push(3, 0, -1, -1)

        def middle(self):
            at = self.pair(0, 1)
            g[at] = (g[at].astype(f32) + self.arrived(0)).astype(bf16)
            self.push(4, 0, 1, 1)
            at = self.pair(1, -1)
            g[at] = (g[at].astype(f32) + self.arrived(1)).astype(bf16)
            self.push(5, 1, -1, -1)

        def end(self):
            acc2[self.arr, 2:4] = g[self.pair(1, 0)].astype(f32) + self.arrived(2) + self.arrived(5)
            acc2[self.arr, 0:2] = g[self.pair(0, 0)].astype(f32) + self.arrived(3) + self.arrived(4)
            fin[self.arr, 0:SIDE] = acc2[self.arr].astype(bf16)
            for i in (2, 1, -1):
                self.key[("s", i)] = send(
                    fin.at[self.arr, up(self.at, i)], block_in.at[self.arr, i % SIDE - 1], self.dev(i, 0)
                )

        def end2(self):
            value = acc2[self.arr, self.at]
            for i in (1, -1, 2):
                arrive(self.key[("s", i)], block_in.at[self.arr, i % SIDE - 1])
                value = value + block_in[self.arr, i % SIDE - 1].astype(f32)
            self.value = value
            fin[self.arr, SIDE] = value.astype(bf16)
            self.back = []
            for k in range(1, N_LAYER):
                to = up(sx, k)
                self.back.append(send(fin.at[self.arr, SIDE, :, cols(to)], gx.at[self.arr, sx], line(k)))
            gx[self.arr, sx] = fin[self.arr, SIDE, :, cols(sx)]

        def done(self):
            for k in range(1, N_LAYER):
                arrive(self.back[k - 1], gx.at[self.arr, up(sx, -k)])

    both = (Scatter(0, "y"), Scatter(1, "z"))
    gradient(0, 0, qd)
    both[0].start()
    gradient(1, N_LAYER, ad)
    both[1].start()
    for s in both:
        s.middle()
    for s in both:
        s.end()
    for s in both:
        s.end2()
    tokens_total = tseq * 2 * CHIPS
    shrink = 1.0 / (damping * tokens_total * width)

    def lanes(v):
        return sum(v[:, l * rank : (l + 1) * rank] for l in range(N_LAYER))

    pg = rg = gg = 0.0
    for key, k in zip(res_keys, (2, 1, 3)):
        arrive(key, res_s.at[:, :, cols(up(sx, -k))])
    for s in both:
        pg = pg + lanes(s.value * w[2 + s.arr, y, z].astype(f32))
        rg = rg + lanes(s.value * res_s[s.arr])
        gg = gg + lanes(s.value * s.value)
    pg, rg, gg = fold(pg) * shrink, fold(rg) * shrink, fold(gg) * (shrink * shrink)
    stat_out[...] = home + jnp.concatenate(
        [jnp.zeros((1, rank), f32), pg, rg, 2.0 * pg + gg, jnp.zeros((4, rank), f32)], axis=0
    )
    keys = []
    for k in range(1, 8):
        keys.append(send(stat_out, stat_in.at[k - 1], (up(sx, k // 2), fs(y, z, lax.rem(c + k, 2)))))
    total = stat_out[...]
    for k in range(1, 8):
        arrive(keys[k - 1], stat_in.at[k - 1])
        total = total + stat_in[k - 1]
    stat2_out[...] = total
    keys = [send(stat2_out, stat2_in.at[k - 1], chip_dev(k)) for k in range(1, CHIPS)]
    for s in both:
        s.done()
    big_vmem[...] = gx[...].astype(f32).reshape(2, own, rank) * shrink + direc
    copy_big = pltpu.make_async_copy(big_vmem, big_hbm, local_sem.at[5])
    copy_big.start()
    for k in range(1, CHIPS):
        arrive(keys[k - 1], stat2_in.at[k - 1])
        total = total + stat2_in[k - 1]
    rr = jnp.sum(total[0:1], keepdims=True)
    pq = jnp.sum(total[1:2], keepdims=True) * damping
    rp = jnp.sum(total[2:3], keepdims=True)
    pp = jnp.sum(total[3:4], keepdims=True)
    step = rr / pq * damping
    norm_new = rr - 2.0 * (step * rp) + step * (step * pp)
    row = lax.broadcasted_iota(jnp.int32, (8, rank), 0)
    coef_ref[...] = jnp.where(row == 0, step, norm_new / rr)
    copy_big.wait()
    for copy in pending:
        copy.wait_send()


def step_kernel(inputs, targets, down_proj, up_proj, direction, residual):
    tseq, width = inputs.shape
    _, own, rank = down_proj.shape
    pr = own // N_LAYER
    feats = CHIPS * pr
    tq = tseq // N_LAYER
    wide = N_LAYER * rank
    hr = rank // 2
    vm = pltpu.VMEM
    scratch = [
        vm((tseq, width), bf16), vm((tseq, width), bf16),
        vm((2, own, rank), f32), vm((2, own, rank), f32),
        vm((2 * tseq, feats), bf16), vm((2 * tseq, feats), bf16),
        vm((tseq, feats), bf16), vm((tseq, feats), bf16),
        vm((feats, 2 * tseq), bf16), vm((feats, 2 * tseq), bf16),
        vm((4, SIDE, SIDE, pr, wide), bf16), vm((2, own, rank), bf16),
        vm((2 * tseq, 3 * wide), f32), vm((tseq, 3 * wide), bf16), vm((tseq, 3 * wide), bf16),
        vm((tseq, 3 * wide), bf16), vm((N_LAYER - 1, tq, 3 * wide), bf16),
        vm((2 * CHIPS, hr, rank), f32), vm((CHIPS, hr, rank), bf16), vm((CHIPS, hr, rank), bf16),
        vm((CHIPS, hr, rank), bf16), vm((CHIPS - 1, hr, rank), bf16), vm((hr, rank), bf16),
        vm((N_LAYER - 1, hr, rank), bf16), vm((2 * CHIPS, hr, rank), bf16),
        vm((2, pr, wide), f32), vm((2, own, rank), f32),
        vm((2 * tseq, 2 * wide + rank), bf16), vm((2 * N_LAYER, feats, 2 * tseq), bf16),
        vm((2, SIDE, SIDE, pr, wide), bf16),
        vm((2, 6, 2, pr, wide), bf16),
        vm((2, SIDE, pr, wide), f32),
        vm((2, 3, pr, wide), bf16), vm((2, SIDE + 1, pr, wide), bf16),
        vm((2, N_LAYER, pr, rank), bf16),
        vm((8, rank), f32), vm((7, 8, rank), f32), vm((8, rank), f32), vm((CHIPS - 1, 8, rank), f32),
        vm((8, rank), f32), vm((7, 8, rank), f32),
        pltpu.SemaphoreType.DMA((N_SEM,)), pltpu.SemaphoreType.DMA((N_SEM,)), pltpu.SemaphoreType.DMA((8,)),
    ]
    hbm = pl.BlockSpec(memory_space=pl.ANY)
    big, coef = pl.pallas_call(
        kernel,
        out_shape=(jax.ShapeDtypeStruct((2, own, rank), f32), jax.ShapeDtypeStruct((8, rank), f32)),
        in_specs=[hbm] * 6,
        out_specs=(hbm, pl.BlockSpec(memory_space=pltpu.VMEM)),
        scratch_shapes=scratch,
        compiler_params=pltpu.CompilerParams(
            collective_id=0, has_side_effects=True, vmem_limit_bytes=58 * 1024 * 1024
        ),
        cost_estimate=pl.CostEstimate(flops=4_000_000_000, bytes_accessed=8_000_000, transcendentals=0),
    )(inputs, targets, down_proj[0], up_proj[0], direction[0], residual[0])
    new_res = residual[0] - coef[0, 0] * big
    new_dir = new_res + coef[1, 0] * direction[0]
    return new_res[None], new_dir[None]


def solution(mesh):
    in_specs = (
        P("fsdp", None),
        P("fsdp", None),
        P("section", "fsdp", None),
        P("section", "fsdp", None),
        P("section", None, "fsdp", None),
        P("section", None, "fsdp", None),
    )
    out_specs = (P("section", None, "fsdp", None), P("section", None, "fsdp", None))
    return jax.shard_map(step_kernel, mesh=mesh, in_specs=in_specs, out_specs=out_specs, check_vma=False)
```

```python
import functools

import jax
import jax.numpy as jnp
from jax import lax
from jax.experimental import pallas as pl
from jax.experimental.pallas import tpu as pltpu
from jax.sharding import PartitionSpec as P

MESH = pl.DeviceIdType.MESH
bf16 = jnp.bfloat16
f32 = jnp.float32

norm_eps = 1e-05
damping = 1e-06
N_LAYER = 4
SIDE = 4
CHIPS = 16

CROSS = {}
for _j in range(N_LAYER):
    for _l in range(_j + 1, N_LAYER):
        CROSS[(_j, _l)] = len(CROSS)
SELF = {}
for _j in range(N_LAYER):
    for _l in range(_j, N_LAYER):
        SELF[(_j, _l)] = len(CROSS) + len(SELF)
N_GRAM = len(CROSS) + len(SELF)


def dot_nn(a, b):
    return lax.dot_general(a, b, (((1,), (0,)), ((), ())), preferred_element_type=f32)


def dot_nt(a, b):
    return lax.dot_general(a, b, (((1,), (1,)), ((), ())), preferred_element_type=f32)


def dot_tn(a, b):
    return lax.dot_general(a, b, (((0,), (0,)), ((), ())), preferred_element_type=f32)


class Counter:
    def __init__(self):
        self.n = 0

    def take(self):
        self.n += 1
        return self.n - 1


N_SEM = 154


def kernel(
    x_hbm, y_hbm, a_ref, b_ref, dir_hbm, res_hbm,
    newres_ref, newdir_ref,
    xin, yin, dir_ref, res_ref, xg, yg, xs, ys, xt, yt, w, pbf,
    prod, prod_out, prod_in, prodx_out, prodx_in,
    gram, gram_out, gram_in, gramx_out, gramx_in, gline_out, gline_in, gfull, res_s,
    act, ht, g, pair_in, acc2, block_in, fin,
    gx, stat_out, stat_in, stat2_out, stat2_in, dv_out, dv_in,
    send_sem, recv_sem, local_sem,
):
    tseq, width = xin.shape
    rank = a_ref.shape[1]
    own = a_ref.shape[0]
    pr = own // N_LAYER
    feats = CHIPS * pr
    tq = tseq // N_LAYER
    quad = SIDE * pr
    sx = lax.axis_index("section")
    f = lax.axis_index("fsdp")
    c = lax.rem(f, 2)
    z = lax.rem(lax.div(f, 2), SIDE)
    y = lax.div(f, 2 * SIDE)

    def up(v, k):
        return lax.rem(v + k + SIDE, SIDE)

    def fs(yy, zz, cc):
        return (yy * SIDE + zz) * 2 + cc

    barrier = pltpu.get_barrier_semaphore()
    sib = (sx, fs(y, z, 1 - c))

    def line(k):
        return (up(sx, k), f)

    for k in range(1, N_LAYER):
        pl.semaphore_signal(barrier, inc=1, device_id=line(k), device_id_type=MESH)
    pl.semaphore_signal(barrier, inc=1, device_id=sib, device_id_type=MESH)
    for k in range(1, SIDE):
        pl.semaphore_signal(barrier, inc=1, device_id=(sx, fs(up(y, k), z, c)), device_id_type=MESH)
        pl.semaphore_signal(barrier, inc=1, device_id=(sx, fs(y, up(z, k), c)), device_id_type=MESH)

    load_x = pltpu.make_async_copy(x_hbm, xin, local_sem.at[0])
    load_y = pltpu.make_async_copy(y_hbm, yin, local_sem.at[1])
    load_d = pltpu.make_async_copy(dir_hbm, dir_ref, local_sem.at[6])
    load_r = pltpu.make_async_copy(res_hbm, res_ref, local_sem.at[7])
    load_d.start()
    load_x.start()
    load_y.start()
    load_r.start()

    pl.semaphore_wait(barrier, 1 + 3 * (SIDE - 1))

    counter = Counter()
    pending = []

    def send(src, dst, dev):
        k = counter.take()
        copy = pltpu.make_async_remote_copy(
            src_ref=src, dst_ref=dst, send_sem=send_sem.at[k], recv_sem=recv_sem.at[k],
            device_id=dev, device_id_type=MESH,
        )
        copy.start()
        pending.append(copy)
        return k

    def arrive(k, dst):
        pltpu.make_async_remote_copy(
            src_ref=dst, dst_ref=dst, send_sem=send_sem.at[k], recv_sem=recv_sem.at[k],
            device_id=(sx, f), device_id_type=MESH,
        ).wait_recv()

    def rows(ref, at, size):
        return ref.at[pl.ds(pl.multiple_of(at * size, size), size)]

    def rows2(ref, at):
        return ref.at[:, pl.ds(pl.multiple_of(at * pr, pr), pr)]

    def cols(at):
        return pl.ds(pl.multiple_of(at * rank, rank), rank)

    def spread(srcs, arrs):
        keys = []
        for src, arr in zip(srcs, arrs):
            for k in range(1, N_LAYER):
                to = up(sx, k)
                keys.append((arr, k, send(rows(src, to, pr), w.at[arr, y, z, :, cols(sx)], line(k))))
        copies = []
        for n, (src, arr) in enumerate(zip(srcs, arrs)):
            copy = pltpu.make_async_copy(
                rows(src, sx, pr), w.at[arr, y, z, :, cols(sx)], local_sem.at[2 + arr]
            )
            copy.start()
            copies.append(copy)
        return keys, copies

    def spread_done(keys, copies):
        for copy in copies:
            copy.wait()
        for arr, k, key in keys:
            arrive(key, w.at[arr, y, z, :, cols(up(sx, -k))])

    ab_keys = spread((a_ref, b_ref), (0, 1))
    load_d.wait()
    pbf[...] = dir_ref[...].astype(bf16)

    class Gather:
        def __init__(self, arr, first):
            self.arr, self.first, self.key = arr, first, {}

        def dev(self, i, j):
            dy, dz = (i, j) if self.first == "y" else (j, i)
            return (sx, fs(up(y, dy), up(z, dz), c))

        def block(self, i):
            if self.first == "y":
                return w.at[self.arr, up(y, i), z]
            return w.at[self.arr, y, up(z, i)]

        def pair(self, p, j):
            if self.first == "y":
                return w.at[self.arr, pl.ds(2 * p, 2), up(z, j)]
            return w.at[self.arr, up(y, j), pl.ds(2 * p, 2)]

        def push(self, name, ref, di, dj):
            self.key[name] = send(ref, ref, self.dev(di, dj))

        def start(self):
            for i in (2, 1, -1):
                self.push(i, self.block(0), i, 0)

        def second(self):
            for i in (1, -1, 2):
                arrive(self.key[i], self.block(-i))
            self.push("r1", self.pair(0, 0), 0, 1)
            self.push("l1", self.pair(1, 0), 0, -1)
            self.push("r2", self.pair(1, 0), 0, 1)
            self.push("l2", self.pair(0, 0), 0, -1)

        def relay(self):
            arrive(self.key["r1"], self.pair(0, -1))
            self.push("rr", self.pair(0, -1), 0, 1)
            arrive(self.key["l1"], self.pair(1, 1))
            self.push("ll", self.pair(1, 1), 0, -1)

        def finish(self):
            arrive(self.key["r2"], self.pair(1, -1))
            arrive(self.key["l2"], self.pair(0, 1))
            arrive(self.key["rr"], self.pair(0, 2))
            arrive(self.key["ll"], self.pair(1, 2))

    ga, gb = Gather(0, "y"), Gather(1, "z")
    gpa, gpb = Gather(2, "y"), Gather(3, "z")
    def pick(src, dst, cc, put):
        odd = lax.rem(sx, 2) == 1
        for p in range(0, CHIPS, 2):
            tiles = []
            for q in (p, p + 1):
                at = (2 * q + cc) * own + lax.div(sx, 2) * (2 * pr)
                tiles.append(src[:, pl.ds(pl.multiple_of(at, 2 * pr), 2 * pr)])
            even = jnp.concatenate([t[:, :pr] for t in tiles], axis=1)
            put(dst, p, jnp.where(odd, jnp.concatenate([t[:, pr:] for t in tiles], axis=1), even))

    def put_other(dst, p, value):
        dst[:, p * pr : (p + 2) * pr] = value

    def put_own(dst, p, value):
        dst[pl.ds(pl.multiple_of(c * tseq, tseq), tseq), p * pr : (p + 2) * pr] = value

    my_rows = pl.ds(pl.multiple_of(c * tseq, tseq), tseq)
    its_rows = pl.ds(pl.multiple_of((1 - c) * tseq, tseq), tseq)
    load_x.wait()
    pick(xin, xs, 1 - c, put_other)
    key_xs = send(xs, xg.at[my_rows], sib)
    load_y.wait()
    pick(yin, ys, 1 - c, put_other)
    key_ys = send(ys, yg.at[my_rows], sib)
    spread_done(*ab_keys)
    ga.start()
    gb.start()
    p_keys = [send(rows2(pbf, up(sx, k)), w.at[2:4, y, z, :, cols(sx)], line(k)) for k in (2, 1, 3)]
    copy_p = pltpu.make_async_copy(rows2(pbf, sx), w.at[2:4, y, z, :, cols(sx)], local_sem.at[4])
    copy_p.start()
    half_rows = rank // 2
    mine_a, mine_b = w[0, y, z], w[1, y, z]
    for j in range(N_LAYER):
        left = mine_b[:, j * rank : (j + 1) * rank]
        if j < N_LAYER - 1:
            block = dot_tn(left, mine_a[:, (j + 1) * rank :])
            for l in range(j + 1, N_LAYER):
                b = CROSS[(j, l)]
                gram[2 * b : 2 * b + 2] = block[:, (l - j - 1) * rank : (l - j) * rank].reshape(2, half_rows, rank)
        block = dot_tn(left, mine_b[:, j * rank :])
        for l in range(j, N_LAYER):
            b = SELF[(j, l)]
            gram[2 * b : 2 * b + 2] = block[:, (l - j) * rank : (l - j + 1) * rank].reshape(2, half_rows, rank)
    my_gram = pl.ds(c * CHIPS, CHIPS)
    its_gram = pl.ds((1 - c) * CHIPS, CHIPS)
    gram_out[...] = gram[its_gram].astype(bf16)
    key_gram = send(gram_out, gram_in, sib)
    pick(xin, xg, c, put_own)
    pick(yin, yg, c, put_own)
    arrive(key_gram, gram_in)
    gpair = gram[my_gram] + gram_in[...].astype(f32)
    gram[my_gram] = gpair
    gramx_out[...] = gpair.astype(bf16)

    def chip(k):
        return up(y, k // SIDE) * SIDE + up(z, k % SIDE)

    def chip_dev(k):
        return (sx, fs(up(y, k // SIDE), up(z, k % SIDE), c))

    def chip_back(k):
        return up(y, -(k // SIDE)) * SIDE + up(z, -(k % SIDE))

    ga.second()
    gb.second()
    gkeys = [send(gramx_out.at[chip(k)], gramx_in.at[k - 1], chip_dev(k)) for k in range(1, CHIPS)]
    xq = xin[pl.ds(pl.multiple_of(sx * tq, tq), tq), :].astype(f32)
    norm = jnp.sum(xq * xq, axis=1, keepdims=True)
    load_r.wait()
    res = res_ref[...]
    direc = dir_ref[...]

    def fold_home(v):
        return jnp.sum(v.reshape(-1, rank), axis=0, keepdims=True)

    dd = fold_home(direc * direc)
    home = jnp.concatenate(
        [fold_home(res * res), dd, fold_home(res * direc), dd, jnp.zeros((4, rank), f32)], axis=0
    )
    arrive(key_xs, xg.at[its_rows])
    arrive(key_ys, yg.at[its_rows])
    xt[...] = xg[...].astype(f32).T.astype(bf16)
    yt[...] = yg[...].astype(f32).T.astype(bf16)
    ga.relay()
    gb.relay()
    copy_p.wait()
    for key, k in zip(p_keys, (2, 1, 3)):
        arrive(key, w.at[2:4, y, z, :, cols(up(sx, -k))])
    gpa.start()
    gpb.start()
    res_keys = [send(rows2(res_ref, up(sx, k)), res_s.at[:, :, cols(sx)], line(k)) for k in (2, 1, 3)]
    res_s[:, :, cols(sx)] = res_ref[:, pl.ds(pl.multiple_of(sx * pr, pr), pr)]
    my_piece = c * CHIPS + y * SIDE + z
    gsum = gram[my_piece]
    for k in range(1, CHIPS):
        arrive(gkeys[k - 1], gramx_in.at[k - 1])
        gsum = gsum + gramx_in[k - 1].astype(f32)
    gline_out[...] = gsum.astype(bf16)
    gkeys = [send(gline_out, gline_in.at[k - 1], line(k)) for k in (2, 1, 3)]
    ga.finish()
    gb.finish()

    wide = N_LAYER * rank
    wa = w[0].reshape(feats, wide)
    wb = w[1].reshape(feats, wide)
    xv = xg[...]
    yv = yg[...]
    both_x = 2 * wide
    prod[:, 0:wide] = dot_nn(xv, wa)
    prod[:, wide:both_x] = dot_nn(xv, wb)
    prod_out[:, 0:both_x] = prod[its_rows, 0:both_x].astype(bf16)
    key_px = send(prod_out.at[:, 0:both_x], prod_in.at[:, 0:both_x], sib)
    for key, k in zip(gkeys, (2, 1, 3)):
        arrive(key, gline_in.at[k - 1])
        gsum = gsum + gline_in[k - 1].astype(f32)
    gfull[my_piece] = gsum.astype(bf16)
    gkeys = [send(gfull.at[my_piece], gfull.at[my_piece], chip_dev(k)) for k in range(1, CHIPS)]
    gpa.second()
    gpb.second()
    prod[:, both_x:] = dot_nn(yv, wb)
    prod_out[:, both_x:] = prod[its_rows, both_x:].astype(bf16)
    key_py = send(prod_out.at[:, both_x:], prod_in.at[:, both_x:], sib)

    def pair_sum(key, at):
        arrive(key, prod_in.at[:, at])
        pair = prod[my_rows, at] + prod_in[:, at].astype(f32)
        prod[my_rows, at] = pair
        prodx_out[:, at] = pair.astype(bf16)
        keys = []
        for k in (2, 1, 3):
            src = prodx_out.at[pl.ds(pl.multiple_of(up(sx, k) * tq, tq), tq), at]
            keys.append(send(src, prodx_in.at[k - 1, :, at], line(k)))
        return keys

    in_x, in_y = slice(0, both_x), slice(both_x, 3 * wide)
    pxkeys = pair_sum(key_px, in_x)
    pykeys = pair_sum(key_py, in_y)
    for k in range(1, CHIPS):
        arrive(gkeys[k - 1], gfull.at[c * CHIPS + chip_back(k)])
    key_gfull = send(gfull.at[my_gram], gfull.at[my_gram], sib)
    gpa.relay()
    gpb.relay()
    token_rows = pl.ds(pl.multiple_of(c * tseq + sx * tq, tq), tq)

    def line_sum(keys, at):
        total = prod[token_rows, at]
        for key, k in zip(keys, (2, 1, 3)):
            arrive(key, prodx_in.at[k - 1, :, at])
            total = total + prodx_in[k - 1, :, at].astype(f32)
        return total

    psum = line_sum(pxkeys, in_x)
    arrive(key_gfull, gfull.at[its_gram])

    def gblock(b):
        return gfull[2 * b : 2 * b + 2].reshape(rank, rank)

    def part(value, k):
        return value[:, k * rank : (k + 1) * rank]

    ha = [part(psum, l) for l in range(N_LAYER)]
    hb = [part(psum, N_LAYER + l) for l in range(N_LAYER)]
    acts, slopes, rhos, pres, hbs = [], [], [], [], []
    for l in range(N_LAYER):
        rho = jnp.sqrt(norm / width + norm_eps)
        pre = ha[l] / rho
        sig = jax.nn.sigmoid(pre)
        a = (pre * sig).astype(bf16)
        hbs.append(hb[:l])
        before = hb[l]
        for m in range(l + 1, N_LAYER):
            ha[m] = ha[m] + dot_nn(a, gblock(CROSS[(l, m)]))
        nxt = []
        for m in range(N_LAYER):
            if l <= m:
                nxt.append(hb[m] + dot_nn(a, gblock(SELF[(l, m)])))
            else:
                nxt.append(hb[m] + dot_nt(a, gblock(SELF[(m, l)])))
        hb = nxt
        norm = norm + jnp.sum(a.astype(f32) * (before + hb[l]), axis=1, keepdims=True)
        acts.append(a)
        slopes.append(sig * (1.0 + pre * (1.0 - sig)))
        rhos.append(rho)
        pres.append(pre)
    my_act = token_rows
    a_cols, q_cols = slice(0, wide), slice(wide, 2 * wide + rank)
    for l in range(N_LAYER):
        act[my_act, l * rank : (l + 1) * rank] = acts[l]
    akeys = [send(act.at[my_act, a_cols], act.at[my_act, a_cols], line(k)) for k in (2, 1, 3)]
    ysum = line_sum(pykeys, in_y)
    cb = [hb[l] - part(ysum, l) for l in range(N_LAYER)]
    qs = [None] * N_LAYER
    lane = lax.broadcasted_iota(jnp.int32, (tq, rank), 1)
    gains = jnp.zeros((tq, rank), f32)
    for l in range(N_LAYER - 1, -1, -1):
        cot = cb[l] * slopes[l]
        qs[l] = (cot / rhos[l]).astype(bf16)
        if l > 0:
            gain = jnp.sum(cot * pres[l], axis=1, keepdims=True) / (width * rhos[l] * rhos[l])
            gains = jnp.where(lane == l, gain, gains)
            for j in range(l):
                cb[j] = cb[j] + dot_nt(qs[l], gblock(CROSS[(j, l)])) - gain * hbs[l][j]
    for l in range(N_LAYER):
        act[my_act, (N_LAYER + l) * rank : (N_LAYER + l + 1) * rank] = qs[l]
    act[my_act, 2 * wide :] = gains.astype(bf16)
    qkeys = [send(act.at[my_act, q_cols], act.at[my_act, q_cols], line(k)) for k in (2, 1, 3)]
    def share(keys, at):
        for key, k in zip(keys, (2, 1, 3)):
            arrive(key, act.at[pl.ds(pl.multiple_of(c * tseq + up(sx, -k) * tq, tq), tq), at])
        return send(act.at[my_rows, at], act.at[my_rows, at], sib)

    key = share(akeys, a_cols)
    arrive(key, act.at[its_rows, a_cols])

    def wq(arr, l, q):
        return w[arr, q, :, :, l * rank : (l + 1) * rank].reshape(quad, rank)

    av = [act[:, l * rank : (l + 1) * rank] for l in range(N_LAYER)]
    for q in range(SIDE):
        fr = slice(q * quad, (q + 1) * quad)
        h = xt[fr, :].astype(f32)
        for l in range(N_LAYER):
            hb16 = h.astype(bf16)
            ht[l, fr, :] = hb16
            h = hb16.astype(f32) + dot_nt(wq(1, l, q), av[l])
        ht[2 * N_LAYER - 1, fr, :] = (h - yt[fr, :].astype(f32)).astype(bf16)
    key = share(qkeys, q_cols)
    gpa.finish()
    gpb.finish()
    arrive(key, act.at[its_rows, q_cols])
    qv = [act[:, (N_LAYER + l) * rank : (N_LAYER + l + 1) * rank] for l in range(N_LAYER)]
    gain_t = act[:, 2 * N_LAYER * rank :].astype(f32).T
    d0 = jnp.zeros((quad, rank), f32)
    d1 = jnp.zeros((quad, rank), f32)
    for q in range(SIDE):
        fr = slice(q * quad, (q + 1) * quad)
        cot = ht[2 * N_LAYER - 1, fr, :]
        for l in range(N_LAYER - 1, -1, -1):
            hl = ht[l, fr, :]
            for arr, left, right in ((2, hl, qv[l]), (3, cot, av[l])):
                pw = wq(arr, l, q).astype(f32)
                d0 = d0 + dot_nn(left[:, :tseq], right[:tseq]) * pw
                d1 = d1 + dot_nn(left[:, tseq:], right[tseq:]) * pw
            if l > 0:
                cot = (
                    cot.astype(f32) + dot_nt(wq(0, l, q), qv[l]) - gain_t[l : l + 1, :] * hl.astype(f32)
                ).astype(bf16)
                ht[N_LAYER + l - 1, fr, :] = cot

    def fold(v):
        return jnp.sum(v.reshape(-1, rank), axis=0, keepdims=True)

    def stack(values):
        return jnp.concatenate([fold(v) for v in values] + [jnp.zeros((8 - len(values), rank), f32)], axis=0)

    dv_out[...] = stack([d0, d1])
    keys = []
    for k in range(1, 8):
        keys.append(send(dv_out, dv_in.at[k - 1], (up(sx, k // 2), fs(y, z, lax.rem(c + k, 2)))))
    dv = dv_out[...]
    for k in range(1, 8):
        arrive(keys[k - 1], dv_in.at[k - 1])
        dv = dv + dv_in[k - 1]
    s0 = jnp.sum(dv[0:1], keepdims=True) / (tseq * width)
    s1 = jnp.sum(dv[1:2], keepdims=True) / (tseq * width)
    token = lax.broadcasted_iota(jnp.int32, (2 * tseq, 1), 0)
    scale = jnp.where(token < tseq, s0, s1)
    qd = [(qv[l].astype(f32) * scale).astype(bf16) for l in range(N_LAYER)]
    ad = [(av[l].astype(f32) * scale).astype(bf16) for l in range(N_LAYER)]

    def gradient(arr, base, right):
        for l in range(N_LAYER):
            for q in range(SIDE):
                value = dot_nn(ht[base + l, q * quad : (q + 1) * quad, :], right[l])
                g[arr, q, :, :, l * rank : (l + 1) * rank] = value.astype(bf16).reshape(SIDE, pr, rank)

    class Scatter:
        def __init__(self, arr, last):
            self.arr, self.last, self.key = arr, last, {}
            self.at = y if last == "y" else z

        def dev(self, i, j):
            dy, dz = (i, j) if self.last == "y" else (j, i)
            return (sx, fs(up(y, dy), up(z, dz), c))

        def pair(self, p, j):
            if self.last == "y":
                return self.arr, pl.ds(2 * p, 2), up(z, j)
            return self.arr, up(y, j), pl.ds(2 * p, 2)

        def push(self, n, p, j, dj):
            self.key[n] = send(g.at[self.pair(p, j)], pair_in.at[self.arr, n], self.dev(0, dj))

        def arrived(self, n):
            arrive(self.key[n], pair_in.at[self.arr, n])
            return pair_in[self.arr, n].astype(f32)

        def start(self):
            self.push(0, 0, 2, 1)
            self.push(1, 1, 2, -1)
            self.push(2, 1, 1, 1)
            self.push(3, 0, -1, -1)

        def middle(self):
            at = self.pair(0, 1)
            g[at] = (g[at].astype(f32) + self.arrived(0)).astype(bf16)
            self.push(4, 0, 1, 1)
            at = self.pair(1, -1)
            g[at] = (g[at].astype(f32) + self.arrived(1)).astype(bf16)
            self.push(5, 1, -1, -1)

        def end(self):
            acc2[self.arr, 2:4] = g[self.pair(1, 0)].astype(f32) + self.arrived(2) + self.arrived(5)
            acc2[self.arr, 0:2] = g[self.pair(0, 0)].astype(f32) + self.arrived(3) + self.arrived(4)
            fin[self.arr, 0:SIDE] = acc2[self.arr].astype(bf16)
            for i in (2, 1, -1):
                self.key[("s", i)] = send(
                    fin.at[self.arr, up(self.at, i)], block_in.at[self.arr, i % SIDE - 1], self.dev(i, 0)
                )

        def end2(self):
            value = acc2[self.arr, self.at]
            for i in (1, -1, 2):
                arrive(self.key[("s", i)], block_in.at[self.arr, i % SIDE - 1])
                value = value + block_in[self.arr, i % SIDE - 1].astype(f32)
            self.value = value
            fin[self.arr, SIDE] = value.astype(bf16)
            self.back = []
            for k in range(1, N_LAYER):
                to = up(sx, k)
                self.back.append(send(fin.at[self.arr, SIDE, :, cols(to)], gx.at[self.arr, sx], line(k)))
            gx[self.arr, sx] = fin[self.arr, SIDE, :, cols(sx)]

        def done(self):
            for k in range(1, N_LAYER):
                arrive(self.back[k - 1], gx.at[self.arr, up(sx, -k)])

    both = (Scatter(0, "y"), Scatter(1, "z"))
    gradient(0, 0, qd)
    both[0].start()
    gradient(1, N_LAYER, ad)
    both[1].start()
    for s in both:
        s.middle()
    for s in both:
        s.end()
    for s in both:
        s.end2()
    tokens_total = tseq * 2 * CHIPS
    shrink = 1.0 / (damping * tokens_total * width)

    def lanes(v):
        return sum(v[:, l * rank : (l + 1) * rank] for l in range(N_LAYER))

    pg = rg = gg = 0.0
    for key, k in zip(res_keys, (2, 1, 3)):
        arrive(key, res_s.at[:, :, cols(up(sx, -k))])
    for s in both:
        pg = pg + lanes(s.value * w[2 + s.arr, y, z].astype(f32))
        rg = rg + lanes(s.value * res_s[s.arr])
        gg = gg + lanes(s.value * s.value)
    pg, rg, gg = fold(pg) * shrink, fold(rg) * shrink, fold(gg) * (shrink * shrink)
    stat_out[...] = home + jnp.concatenate(
        [jnp.zeros((1, rank), f32), pg, rg, 2.0 * pg + gg, jnp.zeros((4, rank), f32)], axis=0
    )
    keys = []
    for k in range(1, 8):
        keys.append(send(stat_out, stat_in.at[k - 1], (up(sx, k // 2), fs(y, z, lax.rem(c + k, 2)))))
    total = stat_out[...]
    for k in range(1, 8):
        arrive(keys[k - 1], stat_in.at[k - 1])
        total = total + stat_in[k - 1]
    stat2_out[...] = total
    keys = [send(stat2_out, stat2_in.at[k - 1], chip_dev(k)) for k in range(1, CHIPS)]
    for s in both:
        s.done()
    big = gx[...].astype(f32).reshape(2, own, rank) * shrink + direc
    for k in range(1, CHIPS):
        arrive(keys[k - 1], stat2_in.at[k - 1])
        total = total + stat2_in[k - 1]
    rr = jnp.sum(total[0:1], keepdims=True)
    pq = jnp.sum(total[1:2], keepdims=True) * damping
    rp = jnp.sum(total[2:3], keepdims=True)
    pp = jnp.sum(total[3:4], keepdims=True)
    step = rr / pq * damping
    norm_new = rr - 2.0 * (step * rp) + step * (step * pp)
    new_res = res - step * big
    newres_ref[...] = new_res
    newdir_ref[...] = new_res + (norm_new / rr) * direc
    assert counter.n == N_SEM, counter.n
    for copy in pending:
        copy.wait_send()


def step_kernel(inputs, targets, down_proj, up_proj, direction, residual):
    tseq, width = inputs.shape
    _, own, rank = down_proj.shape
    pr = own // N_LAYER
    feats = CHIPS * pr
    tq = tseq // N_LAYER
    wide = N_LAYER * rank
    hr = rank // 2
    vm = pltpu.VMEM
    scratch = [
        vm((tseq, width), bf16), vm((tseq, width), bf16),
        vm((2, own, rank), f32), vm((2, own, rank), f32),
        vm((2 * tseq, feats), bf16), vm((2 * tseq, feats), bf16),
        vm((tseq, feats), bf16), vm((tseq, feats), bf16),
        vm((feats, 2 * tseq), bf16), vm((feats, 2 * tseq), bf16),
        vm((4, SIDE, SIDE, pr, wide), bf16), vm((2, own, rank), bf16),
        vm((2 * tseq, 3 * wide), f32), vm((tseq, 3 * wide), bf16), vm((tseq, 3 * wide), bf16),
        vm((tseq, 3 * wide), bf16), vm((N_LAYER - 1, tq, 3 * wide), bf16),
        vm((2 * CHIPS, hr, rank), f32), vm((CHIPS, hr, rank), bf16), vm((CHIPS, hr, rank), bf16),
        vm((CHIPS, hr, rank), bf16), vm((CHIPS - 1, hr, rank), bf16), vm((hr, rank), bf16),
        vm((N_LAYER - 1, hr, rank), bf16), vm((2 * CHIPS, hr, rank), bf16),
        vm((2, pr, wide), f32),
        vm((2 * tseq, 2 * wide + rank), bf16), vm((2 * N_LAYER, feats, 2 * tseq), bf16),
        vm((2, SIDE, SIDE, pr, wide), bf16),
        vm((2, 6, 2, pr, wide), bf16),
        vm((2, SIDE, pr, wide), f32),
        vm((2, 3, pr, wide), bf16), vm((2, SIDE + 1, pr, wide), bf16),
        vm((2, N_LAYER, pr, rank), bf16),
        vm((8, rank), f32), vm((7, 8, rank), f32), vm((8, rank), f32), vm((CHIPS - 1, 8, rank), f32),
        vm((8, rank), f32), vm((7, 8, rank), f32),
        pltpu.SemaphoreType.DMA((N_SEM,)), pltpu.SemaphoreType.DMA((N_SEM,)), pltpu.SemaphoreType.DMA((8,)),
    ]
    hbm = pl.BlockSpec(memory_space=pl.ANY)
    spec = pl.BlockSpec(memory_space=pltpu.VMEM)
    out = jax.ShapeDtypeStruct((2, own, rank), f32)
    new_res, new_dir = pl.pallas_call(
        kernel,
        out_shape=(out, out),
        in_specs=[hbm] * 6,
        out_specs=(spec, spec),
        scratch_shapes=scratch,
        compiler_params=pltpu.CompilerParams(
            collective_id=0, has_side_effects=True, vmem_limit_bytes=58 * 1024 * 1024
        ),
        cost_estimate=pl.CostEstimate(flops=4_000_000_000, bytes_accessed=8_000_000, transcendentals=0),
    )(inputs, targets, down_proj[0], up_proj[0], direction[0], residual[0])
    return new_res[None], new_dir[None]


def solution(mesh):
    in_specs = (
        P("fsdp", None),
        P("fsdp", None),
        P("section", "fsdp", None),
        P("section", "fsdp", None),
        P("section", None, "fsdp", None),
        P("section", None, "fsdp", None),
    )
    out_specs = (P("section", None, "fsdp", None), P("section", None, "fsdp", None))
    return jax.shard_map(step_kernel, mesh=mesh, in_specs=in_specs, out_specs=out_specs, check_vma=False)
```

```python
import functools

import jax
import jax.numpy as jnp
from jax import lax
from jax.experimental import pallas as pl
from jax.experimental.pallas import tpu as pltpu
from jax.sharding import PartitionSpec as P

MESH = pl.DeviceIdType.MESH
bf16 = jnp.bfloat16
f32 = jnp.float32

norm_eps = 1e-05
damping = 1e-06
N_LAYER = 4
SIDE = 4
CHIPS = 16

CROSS = {}
for _j in range(N_LAYER):
    for _l in range(_j + 1, N_LAYER):
        CROSS[(_j, _l)] = len(CROSS)
SELF = {}
for _j in range(N_LAYER):
    for _l in range(_j, N_LAYER):
        SELF[(_j, _l)] = len(CROSS) + len(SELF)
N_GRAM = len(CROSS) + len(SELF)


def dot_nn(a, b):
    return lax.dot_general(a, b, (((1,), (0,)), ((), ())), preferred_element_type=f32)


def dot_nt(a, b):
    return lax.dot_general(a, b, (((1,), (1,)), ((), ())), preferred_element_type=f32)


def dot_tn(a, b):
    return lax.dot_general(a, b, (((0,), (0,)), ((), ())), preferred_element_type=f32)


class Counter:
    def __init__(self):
        self.n = 0

    def take(self):
        self.n += 1
        return self.n - 1


N_SEM = 98


def kernel(
    x_hbm, y_hbm, a_ref, b_ref, dir_hbm, res_hbm,
    newres_ref, newdir_ref,
    xin, yin, dir_ref, res_ref, xg, yg, xs, ys, xt, yt, w, pbf,
    prod, prod_out, prod_in, prodx_out, prodx_in,
    gram, gram_out, gram_in, gramx_out, gramx_in, gline_out, gline_in, gfull, res_s,
    act, ht, g, pair_in, acc2, block_in, fin,
    gx, stat_out, stat_in, stat2_out, stat2_in, dv_out, dv_in,
    send_sem, recv_sem, local_sem,
):
    tseq, width = xin.shape
    rank = a_ref.shape[1]
    own = a_ref.shape[0]
    pr = own // N_LAYER
    feats = CHIPS * pr
    tq = tseq // N_LAYER
    quad = SIDE * pr
    sx = lax.axis_index("section")
    f = lax.axis_index("fsdp")
    c = lax.rem(f, 2)
    z = lax.rem(lax.div(f, 2), SIDE)
    y = lax.div(f, 2 * SIDE)

    def up(v, k):
        return lax.rem(v + k + SIDE, SIDE)

    def fs(yy, zz, cc):
        return (yy * SIDE + zz) * 2 + cc

    barrier = pltpu.get_barrier_semaphore()
    sib = (sx, fs(y, z, 1 - c))

    def line(k):
        return (up(sx, k), f)

    for k in range(1, N_LAYER):
        pl.semaphore_signal(barrier, inc=1, device_id=line(k), device_id_type=MESH)
    pl.semaphore_signal(barrier, inc=1, device_id=sib, device_id_type=MESH)
    for k in range(1, SIDE):
        pl.semaphore_signal(barrier, inc=1, device_id=(sx, fs(up(y, k), z, c)), device_id_type=MESH)
        pl.semaphore_signal(barrier, inc=1, device_id=(sx, fs(y, up(z, k), c)), device_id_type=MESH)

    load_x = pltpu.make_async_copy(x_hbm, xin, local_sem.at[0])
    load_y = pltpu.make_async_copy(y_hbm, yin, local_sem.at[1])
    load_d = pltpu.make_async_copy(dir_hbm, dir_ref, local_sem.at[6])
    load_r = pltpu.make_async_copy(res_hbm, res_ref, local_sem.at[7])
    load_d.start()
    load_x.start()
    load_y.start()
    load_r.start()

    pl.semaphore_wait(barrier, 1 + 3 * (SIDE - 1))

    counter = Counter()
    pending = []

    def send(src, dst, dev):
        k = counter.take()
        copy = pltpu.make_async_remote_copy(
            src_ref=src, dst_ref=dst, send_sem=send_sem.at[k], recv_sem=recv_sem.at[k],
            device_id=dev, device_id_type=MESH,
        )
        copy.start()
        pending.append(copy)
        return k

    def send_all(triples):
        k = counter.take()
        for src, dst, dev in triples:
            pltpu.make_async_remote_copy(
                src_ref=src, dst_ref=dst, send_sem=send_sem.at[k], recv_sem=recv_sem.at[k],
                device_id=dev, device_id_type=MESH,
            ).start()
        return k

    def arrive_all(k, whole):
        copy = pltpu.make_async_remote_copy(
            src_ref=whole, dst_ref=whole, send_sem=send_sem.at[k], recv_sem=recv_sem.at[k],
            device_id=(sx, f), device_id_type=MESH,
        )
        copy.wait_recv()
        pending.append(copy)

    def flush():
        while pending:
            pending.pop(0).wait_send()

    def arrive(k, dst):
        pltpu.make_async_remote_copy(
            src_ref=dst, dst_ref=dst, send_sem=send_sem.at[k], recv_sem=recv_sem.at[k],
            device_id=(sx, f), device_id_type=MESH,
        ).wait_recv()

    def rows(ref, at, size):
        return ref.at[pl.ds(pl.multiple_of(at * size, size), size)]

    def rows2(ref, at):
        return ref.at[:, pl.ds(pl.multiple_of(at * pr, pr), pr)]

    def cols(at):
        return pl.ds(pl.multiple_of(at * rank, rank), rank)

    def spread(srcs, arrs):
        keys = []
        for src, arr in zip(srcs, arrs):
            for k in range(1, N_LAYER):
                to = up(sx, k)
                keys.append((arr, k, send(rows(src, to, pr), w.at[arr, y, z, :, cols(sx)], line(k))))
        copies = []
        for n, (src, arr) in enumerate(zip(srcs, arrs)):
            copy = pltpu.make_async_copy(
                rows(src, sx, pr), w.at[arr, y, z, :, cols(sx)], local_sem.at[2 + arr]
            )
            copy.start()
            copies.append(copy)
        return keys, copies

    def spread_done(keys, copies):
        for copy in copies:
            copy.wait()
        for arr, k, key in keys:
            arrive(key, w.at[arr, y, z, :, cols(up(sx, -k))])

    ab_keys = spread((a_ref, b_ref), (0, 1))
    load_d.wait()
    pbf[...] = dir_ref[...].astype(bf16)

    class Gather:
        def __init__(self, arr, first):
            self.arr, self.first, self.key = arr, first, {}

        def dev(self, i, j):
            dy, dz = (i, j) if self.first == "y" else (j, i)
            return (sx, fs(up(y, dy), up(z, dz), c))

        def block(self, i):
            if self.first == "y":
                return w.at[self.arr, up(y, i), z]
            return w.at[self.arr, y, up(z, i)]

        def pair(self, p, j):
            if self.first == "y":
                return w.at[self.arr, pl.ds(2 * p, 2), up(z, j)]
            return w.at[self.arr, up(y, j), pl.ds(2 * p, 2)]

        def push(self, name, ref, di, dj):
            self.key[name] = send(ref, ref, self.dev(di, dj))

        def start(self):
            for i in (2, 1, -1):
                self.push(i, self.block(0), i, 0)

        def second(self):
            for i in (1, -1, 2):
                arrive(self.key[i], self.block(-i))
            self.push("r1", self.pair(0, 0), 0, 1)
            self.push("l1", self.pair(1, 0), 0, -1)

        def second_rest(self):
            self.push("r2", self.pair(1, 0), 0, 1)
            self.push("l2", self.pair(0, 0), 0, -1)

        def relay(self):
            arrive(self.key["r1"], self.pair(0, -1))
            self.push("rr", self.pair(0, -1), 0, 1)
            arrive(self.key["l1"], self.pair(1, 1))
            self.push("ll", self.pair(1, 1), 0, -1)

        def finish(self):
            arrive(self.key["r2"], self.pair(1, -1))
            arrive(self.key["l2"], self.pair(0, 1))
            arrive(self.key["rr"], self.pair(0, 2))
            arrive(self.key["ll"], self.pair(1, 2))

    ga, gb = Gather(0, "y"), Gather(1, "z")
    gpa, gpb = Gather(2, "y"), Gather(3, "z")
    def pick(src, dst, cc, put):
        odd = lax.rem(sx, 2) == 1
        for p in range(0, CHIPS, 2):
            tiles = []
            for q in (p, p + 1):
                at = (2 * q + cc) * own + lax.div(sx, 2) * (2 * pr)
                tiles.append(src[:, pl.ds(pl.multiple_of(at, 2 * pr), 2 * pr)])
            even = jnp.concatenate([t[:, :pr] for t in tiles], axis=1)
            put(dst, p, jnp.where(odd, jnp.concatenate([t[:, pr:] for t in tiles], axis=1), even))

    def put_other(dst, p, value):
        dst[:, p * pr : (p + 2) * pr] = value

    def put_own(dst, p, value):
        dst[pl.ds(pl.multiple_of(c * tseq, tseq), tseq), p * pr : (p + 2) * pr] = value

    my_rows = pl.ds(pl.multiple_of(c * tseq, tseq), tseq)
    its_rows = pl.ds(pl.multiple_of((1 - c) * tseq, tseq), tseq)
    load_x.wait()
    pick(xin, xs, 1 - c, put_other)
    key_xs = send(xs, xg.at[my_rows], sib)
    load_y.wait()
    pick(yin, ys, 1 - c, put_other)
    key_ys = send(ys, yg.at[my_rows], sib)
    spread_done(*ab_keys)
    ga.start()
    gb.start()
    p_keys = [send(rows2(pbf, up(sx, k)), w.at[2:4, y, z, :, cols(sx)], line(k)) for k in (2, 1, 3)]
    copy_p = pltpu.make_async_copy(rows2(pbf, sx), w.at[2:4, y, z, :, cols(sx)], local_sem.at[4])
    copy_p.start()
    half_rows = rank // 2
    mine_a, mine_b = w[0, y, z], w[1, y, z]
    for j in range(N_LAYER):
        left = mine_b[:, j * rank : (j + 1) * rank]
        if j < N_LAYER - 1:
            block = dot_tn(left, mine_a[:, (j + 1) * rank :])
            for l in range(j + 1, N_LAYER):
                b = CROSS[(j, l)]
                gram[2 * b : 2 * b + 2] = block[:, (l - j - 1) * rank : (l - j) * rank].reshape(2, half_rows, rank)
        block = dot_tn(left, mine_b[:, j * rank :])
        for l in range(j, N_LAYER):
            b = SELF[(j, l)]
            gram[2 * b : 2 * b + 2] = block[:, (l - j) * rank : (l - j + 1) * rank].reshape(2, half_rows, rank)
    my_gram = pl.ds(c * CHIPS, CHIPS)
    its_gram = pl.ds((1 - c) * CHIPS, CHIPS)
    gram_out[...] = gram[its_gram].astype(bf16)
    key_gram = send(gram_out, gram_in, sib)
    pick(xin, xg, c, put_own)
    pick(yin, yg, c, put_own)
    arrive(key_gram, gram_in)
    gpair = gram[my_gram] + gram_in[...].astype(f32)
    gram[my_gram] = gpair
    gramx_out[...] = gpair.astype(bf16)

    def chip(k):
        return up(y, k // SIDE) * SIDE + up(z, k % SIDE)

    def chip_dev(k):
        return (sx, fs(up(y, k // SIDE), up(z, k % SIDE), c))

    ga.second()
    gb.second()
    gkey = send_all([(gramx_out.at[chip(k)], gramx_in.at[k - 1], chip_dev(k)) for k in range(1, CHIPS)])
    ga.second_rest()
    gb.second_rest()
    xq = xin[pl.ds(pl.multiple_of(sx * tq, tq), tq), :].astype(f32)
    norm = jnp.sum(xq * xq, axis=1, keepdims=True)
    load_r.wait()
    res = res_ref[...]
    direc = dir_ref[...]

    def fold_home(v):
        return jnp.sum(v.reshape(-1, rank), axis=0, keepdims=True)

    dd = fold_home(direc * direc)
    home = jnp.concatenate(
        [fold_home(res * res), dd, fold_home(res * direc), dd, jnp.zeros((4, rank), f32)], axis=0
    )
    arrive(key_xs, xg.at[its_rows])
    arrive(key_ys, yg.at[its_rows])
    xt[...] = xg[...].astype(f32).T.astype(bf16)
    yt[...] = yg[...].astype(f32).T.astype(bf16)
    my_piece = c * CHIPS + y * SIDE + z
    arrive_all(gkey, gramx_in)
    gsum = gram[my_piece] + jnp.sum(gramx_in[...].astype(f32), axis=0)
    gline_out[...] = gsum.astype(bf16)
    gkey = send_all([(gline_out, gline_in.at[k - 1], line(k)) for k in (2, 1, 3)])
    ga.relay()
    gb.relay()
    copy_p.wait()
    for key, k in zip(p_keys, (2, 1, 3)):
        arrive(key, w.at[2:4, y, z, :, cols(up(sx, -k))])
    gpa.start()
    gpb.start()
    arrive_all(gkey, gline_in)
    gfull[my_piece] = (gsum + jnp.sum(gline_in[...].astype(f32), axis=0)).astype(bf16)
    gkey = send_all([(gfull.at[my_piece], gfull.at[my_piece], chip_dev(k)) for k in range(1, CHIPS)])
    res_keys = [send(rows2(res_ref, up(sx, k)), res_s.at[:, :, cols(sx)], line(k)) for k in (2, 1, 3)]
    res_s[:, :, cols(sx)] = res_ref[:, pl.ds(pl.multiple_of(sx * pr, pr), pr)]
    ga.finish()
    gb.finish()

    wide = N_LAYER * rank
    wa = w[0].reshape(feats, wide)
    wb = w[1].reshape(feats, wide)
    xv = xg[...]
    yv = yg[...]
    both_x = 2 * wide
    prod[:, 0:wide] = dot_nn(xv, wa)
    prod[:, wide:both_x] = dot_nn(xv, wb)
    prod_out[:, 0:both_x] = prod[its_rows, 0:both_x].astype(bf16)
    key_px = send(prod_out.at[:, 0:both_x], prod_in.at[:, 0:both_x], sib)
    gpa.second()
    gpb.second()
    gpa.second_rest()
    gpb.second_rest()
    prod[:, both_x:] = dot_nn(yv, wb)
    prod_out[:, both_x:] = prod[its_rows, both_x:].astype(bf16)
    key_py = send(prod_out.at[:, both_x:], prod_in.at[:, both_x:], sib)

    def pair_sum(key, at):
        arrive(key, prod_in.at[:, at])
        pair = prod[my_rows, at] + prod_in[:, at].astype(f32)
        prod[my_rows, at] = pair
        prodx_out[:, at] = pair.astype(bf16)
        keys = []
        for k in (2, 1, 3):
            src = prodx_out.at[pl.ds(pl.multiple_of(up(sx, k) * tq, tq), tq), at]
            keys.append(send(src, prodx_in.at[k - 1, :, at], line(k)))
        return keys

    in_x, in_y = slice(0, both_x), slice(both_x, 3 * wide)
    pxkeys = pair_sum(key_px, in_x)
    pykeys = pair_sum(key_py, in_y)
    arrive_all(gkey, gfull.at[0 : CHIPS - 1])
    key_gfull = send(gfull.at[my_gram], gfull.at[my_gram], sib)
    gpa.relay()
    gpb.relay()
    token_rows = pl.ds(pl.multiple_of(c * tseq + sx * tq, tq), tq)

    def line_sum(keys, at):
        total = prod[token_rows, at]
        for key, k in zip(keys, (2, 1, 3)):
            arrive(key, prodx_in.at[k - 1, :, at])
            total = total + prodx_in[k - 1, :, at].astype(f32)
        return total

    psum = line_sum(pxkeys, in_x)
    arrive(key_gfull, gfull.at[its_gram])

    def gblock(b):
        return gfull[2 * b : 2 * b + 2].reshape(rank, rank)

    def part(value, k):
        return value[:, k * rank : (k + 1) * rank]

    ha = [part(psum, l) for l in range(N_LAYER)]
    hb = [part(psum, N_LAYER + l) for l in range(N_LAYER)]
    acts, slopes, rhos, pres, hbs = [], [], [], [], []
    for l in range(N_LAYER):
        rho = jnp.sqrt(norm / width + norm_eps)
        pre = ha[l] / rho
        sig = jax.nn.sigmoid(pre)
        a = (pre * sig).astype(bf16)
        hbs.append(hb[:l])
        before = hb[l]
        for m in range(l + 1, N_LAYER):
            ha[m] = ha[m] + dot_nn(a, gblock(CROSS[(l, m)]))
        nxt = []
        for m in range(N_LAYER):
            if l <= m:
                nxt.append(hb[m] + dot_nn(a, gblock(SELF[(l, m)])))
            else:
                nxt.append(hb[m] + dot_nt(a, gblock(SELF[(m, l)])))
        hb = nxt
        norm = norm + jnp.sum(a.astype(f32) * (before + hb[l]), axis=1, keepdims=True)
        acts.append(a)
        slopes.append(sig * (1.0 + pre * (1.0 - sig)))
        rhos.append(rho)
        pres.append(pre)
    my_act = token_rows
    a_cols, q_cols = slice(0, wide), slice(wide, 2 * wide + rank)
    for l in range(N_LAYER):
        act[my_act, l * rank : (l + 1) * rank] = acts[l]
    akeys = [send(act.at[my_act, a_cols], act.at[my_act, a_cols], line(k)) for k in (2, 1, 3)]
    ysum = line_sum(pykeys, in_y)
    cb = [hb[l] - part(ysum, l) for l in range(N_LAYER)]
    qs = [None] * N_LAYER
    lane = lax.broadcasted_iota(jnp.int32, (tq, rank), 1)
    gains = jnp.zeros((tq, rank), f32)
    for l in range(N_LAYER - 1, -1, -1):
        cot = cb[l] * slopes[l]
        qs[l] = (cot / rhos[l]).astype(bf16)
        if l > 0:
            gain = jnp.sum(cot * pres[l], axis=1, keepdims=True) / (width * rhos[l] * rhos[l])
            gains = jnp.where(lane == l, gain, gains)
            for j in range(l):
                cb[j] = cb[j] + dot_nt(qs[l], gblock(CROSS[(j, l)])) - gain * hbs[l][j]
    for l in range(N_LAYER):
        act[my_act, (N_LAYER + l) * rank : (N_LAYER + l + 1) * rank] = qs[l]
    act[my_act, 2 * wide :] = gains.astype(bf16)
    qkeys = [send(act.at[my_act, q_cols], act.at[my_act, q_cols], line(k)) for k in (2, 1, 3)]
    def share(keys, at):
        for key, k in zip(keys, (2, 1, 3)):
            arrive(key, act.at[pl.ds(pl.multiple_of(c * tseq + up(sx, -k) * tq, tq), tq), at])
        return send(act.at[my_rows, at], act.at[my_rows, at], sib)

    key = share(akeys, a_cols)
    arrive(key, act.at[its_rows, a_cols])

    def wq(arr, l, q):
        return w[arr, q, :, :, l * rank : (l + 1) * rank].reshape(quad, rank)

    av = [act[:, l * rank : (l + 1) * rank] for l in range(N_LAYER)]
    for q in range(SIDE):
        fr = slice(q * quad, (q + 1) * quad)
        h = xt[fr, :].astype(f32)
        for l in range(N_LAYER):
            hb16 = h.astype(bf16)
            ht[l, fr, :] = hb16
            h = hb16.astype(f32) + dot_nt(wq(1, l, q), av[l])
        ht[2 * N_LAYER - 1, fr, :] = (h - yt[fr, :].astype(f32)).astype(bf16)
    key = share(qkeys, q_cols)
    gpa.finish()
    gpb.finish()
    arrive(key, act.at[its_rows, q_cols])
    qv = [act[:, (N_LAYER + l) * rank : (N_LAYER + l + 1) * rank] for l in range(N_LAYER)]
    gain_t = act[:, 2 * N_LAYER * rank :].astype(f32).T
    d0 = jnp.zeros((quad, rank), f32)
    d1 = jnp.zeros((quad, rank), f32)
    for q in range(SIDE):
        fr = slice(q * quad, (q + 1) * quad)
        cot = ht[2 * N_LAYER - 1, fr, :]
        for l in range(N_LAYER - 1, -1, -1):
            hl = ht[l, fr, :]
            for arr, left, right in ((2, hl, qv[l]), (3, cot, av[l])):
                pw = wq(arr, l, q).astype(f32)
                d0 = d0 + dot_nn(left[:, :tseq], right[:tseq]) * pw
                d1 = d1 + dot_nn(left[:, tseq:], right[tseq:]) * pw
            if l > 0:
                cot = (
                    cot.astype(f32) + dot_nt(wq(0, l, q), qv[l]) - gain_t[l : l + 1, :] * hl.astype(f32)
                ).astype(bf16)
                ht[N_LAYER + l - 1, fr, :] = cot

    def fold(v):
        return jnp.sum(v.reshape(-1, rank), axis=0, keepdims=True)

    def stack(values):
        return jnp.concatenate([fold(v) for v in values] + [jnp.zeros((8 - len(values), rank), f32)], axis=0)

    dv_out[...] = stack([d0, d1])
    eight = [(up(sx, k // 2), fs(y, z, lax.rem(c + k, 2))) for k in range(1, 8)]
    key = send_all([(dv_out, dv_in.at[k], dev) for k, dev in enumerate(eight)])
    arrive_all(key, dv_in)
    dv = dv_out[...] + jnp.sum(dv_in[...], axis=0)
    s0 = jnp.sum(dv[0:1], keepdims=True) / (tseq * width)
    s1 = jnp.sum(dv[1:2], keepdims=True) / (tseq * width)
    token = lax.broadcasted_iota(jnp.int32, (2 * tseq, 1), 0)
    scale = jnp.where(token < tseq, s0, s1)
    qd = [(qv[l].astype(f32) * scale).astype(bf16) for l in range(N_LAYER)]
    ad = [(av[l].astype(f32) * scale).astype(bf16) for l in range(N_LAYER)]

    def gradient(arr, base, right):
        for l in range(N_LAYER):
            for q in range(SIDE):
                value = dot_nn(ht[base + l, q * quad : (q + 1) * quad, :], right[l])
                g[arr, q, :, :, l * rank : (l + 1) * rank] = value.astype(bf16).reshape(SIDE, pr, rank)

    class Scatter:
        def __init__(self, arr, last):
            self.arr, self.last, self.key = arr, last, {}
            self.at = y if last == "y" else z

        def dev(self, i, j):
            dy, dz = (i, j) if self.last == "y" else (j, i)
            return (sx, fs(up(y, dy), up(z, dz), c))

        def pair(self, p, j):
            if self.last == "y":
                return self.arr, pl.ds(2 * p, 2), up(z, j)
            return self.arr, up(y, j), pl.ds(2 * p, 2)

        def push(self, n, p, j, dj):
            self.key[n] = send(g.at[self.pair(p, j)], pair_in.at[self.arr, n], self.dev(0, dj))

        def arrived(self, n):
            arrive(self.key[n], pair_in.at[self.arr, n])
            return pair_in[self.arr, n].astype(f32)

        def start(self):
            self.push(0, 0, 2, 1)
            self.push(1, 1, 2, -1)
            self.push(2, 1, 1, 1)
            self.push(3, 0, -1, -1)

        def middle(self):
            at = self.pair(0, 1)
            g[at] = (g[at].astype(f32) + self.arrived(0)).astype(bf16)
            self.push(4, 0, 1, 1)
            at = self.pair(1, -1)
            g[at] = (g[at].astype(f32) + self.arrived(1)).astype(bf16)
            self.push(5, 1, -1, -1)

        def end(self):
            acc2[self.arr, 2:4] = g[self.pair(1, 0)].astype(f32) + self.arrived(2) + self.arrived(5)
            acc2[self.arr, 0:2] = g[self.pair(0, 0)].astype(f32) + self.arrived(3) + self.arrived(4)
            fin[self.arr, 0:SIDE] = acc2[self.arr].astype(bf16)
            for i in (2, 1, -1):
                self.key[("s", i)] = send(
                    fin.at[self.arr, up(self.at, i)], block_in.at[self.arr, i % SIDE - 1], self.dev(i, 0)
                )

        def end2(self):
            value = acc2[self.arr, self.at]
            for i in (1, -1, 2):
                arrive(self.key[("s", i)], block_in.at[self.arr, i % SIDE - 1])
                value = value + block_in[self.arr, i % SIDE - 1].astype(f32)
            self.value = value
            fin[self.arr, SIDE] = value.astype(bf16)
            self.back = []
            for k in range(1, N_LAYER):
                to = up(sx, k)
                self.back.append(send(fin.at[self.arr, SIDE, :, cols(to)], gx.at[self.arr, sx], line(k)))
            gx[self.arr, sx] = fin[self.arr, SIDE, :, cols(sx)]

        def done(self):
            for k in range(1, N_LAYER):
                arrive(self.back[k - 1], gx.at[self.arr, up(sx, -k)])

    both = (Scatter(0, "y"), Scatter(1, "z"))
    gradient(0, 0, qd)
    both[0].start()
    gradient(1, N_LAYER, ad)
    both[1].start()
    flush()
    for s in both:
        s.middle()
    for s in both:
        s.end()
    for s in both:
        s.end2()
    tokens_total = tseq * 2 * CHIPS
    shrink = 1.0 / (damping * tokens_total * width)

    def lanes(v):
        return sum(v[:, l * rank : (l + 1) * rank] for l in range(N_LAYER))

    pg = rg = gg = 0.0
    for key, k in zip(res_keys, (2, 1, 3)):
        arrive(key, res_s.at[:, :, cols(up(sx, -k))])
    for s in both:
        pg = pg + lanes(s.value * w[2 + s.arr, y, z].astype(f32))
        rg = rg + lanes(s.value * res_s[s.arr])
        gg = gg + lanes(s.value * s.value)
    pg, rg, gg = fold(pg) * shrink, fold(rg) * shrink, fold(gg) * (shrink * shrink)
    stat_out[...] = home + jnp.concatenate(
        [jnp.zeros((1, rank), f32), pg, rg, 2.0 * pg + gg, jnp.zeros((4, rank), f32)], axis=0
    )
    key = send_all([(stat_out, stat_in.at[k], dev) for k, dev in enumerate(eight)])
    flush()
    arrive_all(key, stat_in)
    total = stat_out[...] + jnp.sum(stat_in[...], axis=0)
    stat2_out[...] = total
    key = send_all([(stat2_out, stat2_in.at[k - 1], chip_dev(k)) for k in range(1, CHIPS)])
    for s in both:
        s.done()
    big = gx[...].astype(f32).reshape(2, own, rank) * shrink + direc
    flush()
    arrive_all(key, stat2_in)
    total = total + jnp.sum(stat2_in[...], axis=0)
    rr = jnp.sum(total[0:1], keepdims=True)
    pq = jnp.sum(total[1:2], keepdims=True) * damping
    rp = jnp.sum(total[2:3], keepdims=True)
    pp = jnp.sum(total[3:4], keepdims=True)
    step = rr / pq * damping
    norm_new = rr - 2.0 * (step * rp) + step * (step * pp)
    new_res = res - step * big
    newres_ref[...] = new_res
    newdir_ref[...] = new_res + (norm_new / rr) * direc
    assert counter.n == N_SEM
    flush()


def step_kernel(inputs, targets, down_proj, up_proj, direction, residual):
    tseq, width = inputs.shape
    _, own, rank = down_proj.shape
    pr = own // N_LAYER
    feats = CHIPS * pr
    tq = tseq // N_LAYER
    wide = N_LAYER * rank
    hr = rank // 2
    vm = pltpu.VMEM
    scratch = [
        vm((tseq, width), bf16), vm((tseq, width), bf16),
        vm((2, own, rank), f32), vm((2, own, rank), f32),
        vm((2 * tseq, feats), bf16), vm((2 * tseq, feats), bf16),
        vm((tseq, feats), bf16), vm((tseq, feats), bf16),
        vm((feats, 2 * tseq), bf16), vm((feats, 2 * tseq), bf16),
        vm((4, SIDE, SIDE, pr, wide), bf16), vm((2, own, rank), bf16),
        vm((2 * tseq, 3 * wide), f32), vm((tseq, 3 * wide), bf16), vm((tseq, 3 * wide), bf16),
        vm((tseq, 3 * wide), bf16), vm((N_LAYER - 1, tq, 3 * wide), bf16),
        vm((2 * CHIPS, hr, rank), f32), vm((CHIPS, hr, rank), bf16), vm((CHIPS, hr, rank), bf16),
        vm((CHIPS, hr, rank), bf16), vm((CHIPS - 1, hr, rank), bf16), vm((hr, rank), bf16),
        vm((N_LAYER - 1, hr, rank), bf16), vm((2 * CHIPS, hr, rank), bf16),
        vm((2, pr, wide), f32),
        vm((2 * tseq, 2 * wide + rank), bf16), vm((2 * N_LAYER, feats, 2 * tseq), bf16),
        vm((2, SIDE, SIDE, pr, wide), bf16),
        vm((2, 6, 2, pr, wide), bf16),
        vm((2, SIDE, pr, wide), f32),
        vm((2, 3, pr, wide), bf16), vm((2, SIDE + 1, pr, wide), bf16),
        vm((2, N_LAYER, pr, rank), bf16),
        vm((8, rank), f32), vm((7, 8, rank), f32), vm((8, rank), f32), vm((CHIPS - 1, 8, rank), f32),
        vm((8, rank), f32), vm((7, 8, rank), f32),
        pltpu.SemaphoreType.DMA((N_SEM,)), pltpu.SemaphoreType.DMA((N_SEM,)), pltpu.SemaphoreType.DMA((8,)),
    ]
    hbm = pl.BlockSpec(memory_space=pl.ANY)
    spec = pl.BlockSpec(memory_space=pltpu.VMEM)
    out = jax.ShapeDtypeStruct((2, own, rank), f32)
    new_res, new_dir = pl.pallas_call(
        kernel,
        out_shape=(out, out),
        in_specs=[hbm] * 6,
        out_specs=(spec, spec),
        scratch_shapes=scratch,
        compiler_params=pltpu.CompilerParams(
            collective_id=0, has_side_effects=True, vmem_limit_bytes=58 * 1024 * 1024
        ),
        cost_estimate=pl.CostEstimate(flops=4_000_000_000, bytes_accessed=8_000_000, transcendentals=0),
    )(inputs, targets, down_proj[0], up_proj[0], direction[0], residual[0])
    return new_res[None], new_dir[None]


def solution(mesh):
    in_specs = (
        P("fsdp", None),
        P("fsdp", None),
        P("section", "fsdp", None),
        P("section", "fsdp", None),
        P("section", None, "fsdp", None),
        P("section", None, "fsdp", None),
    )
    out_specs = (P("section", None, "fsdp", None), P("section", None, "fsdp", None))
    return jax.shard_map(step_kernel, mesh=mesh, in_specs=in_specs, out_specs=out_specs, check_vma=False)
```

```python
import functools

import jax
import jax.numpy as jnp
from jax import lax
from jax.experimental import pallas as pl
from jax.experimental.pallas import tpu as pltpu
from jax.sharding import PartitionSpec as P

MESH = pl.DeviceIdType.MESH
bf16 = jnp.bfloat16
f32 = jnp.float32

norm_eps = 1e-05
damping = 1e-06
N_LAYER = 4
SIDE = 4
CHIPS = 16

CROSS = {}
for _j in range(N_LAYER):
    for _l in range(_j + 1, N_LAYER):
        CROSS[(_j, _l)] = len(CROSS)
SELF = {}
for _j in range(N_LAYER):
    for _l in range(_j, N_LAYER):
        SELF[(_j, _l)] = len(CROSS) + len(SELF)
N_GRAM = len(CROSS) + len(SELF)


def dot_nn(a, b):
    return lax.dot_general(a, b, (((1,), (0,)), ((), ())), preferred_element_type=f32)


def dot_nt(a, b):
    return lax.dot_general(a, b, (((1,), (1,)), ((), ())), preferred_element_type=f32)


def dot_tn(a, b):
    return lax.dot_general(a, b, (((0,), (0,)), ((), ())), preferred_element_type=f32)


class Counter:
    def __init__(self):
        self.n = 0

    def take(self):
        self.n += 1
        return self.n - 1


N_SEM = 98


def kernel(
    x_hbm, y_hbm, a_ref, b_ref, dir_hbm, res_hbm,
    newres_ref, newdir_ref,
    xin, yin, dir_ref, res_ref, xg, yg, xs, ys, xt, yt, w, pbf,
    prod, prod_out, prod_in, prodx_out, prodx_in,
    gram, gram_out, gram_in, gramx_out, gramx_in, gline_out, gline_in, gfull, res_s,
    act, ht, g, pair_in, acc2, block_in, fin,
    gx, stat_out, stat_in, stat2_out, stat2_in, dv_out, dv_in,
    send_sem, recv_sem, local_sem,
):
    tseq, width = xin.shape
    rank = a_ref.shape[1]
    own = a_ref.shape[0]
    pr = own // N_LAYER
    feats = CHIPS * pr
    tq = tseq // N_LAYER
    quad = SIDE * pr
    sx = lax.axis_index("section")
    f = lax.axis_index("fsdp")
    c = lax.rem(f, 2)
    z = lax.rem(lax.div(f, 2), SIDE)
    y = lax.div(f, 2 * SIDE)

    def up(v, k):
        return lax.rem(v + k + SIDE, SIDE)

    def fs(yy, zz, cc):
        return (yy * SIDE + zz) * 2 + cc

    barrier = pltpu.get_barrier_semaphore()
    sib = (sx, fs(y, z, 1 - c))

    def line(k):
        return (up(sx, k), f)

    for k in range(1, N_LAYER):
        pl.semaphore_signal(barrier, inc=1, device_id=line(k), device_id_type=MESH)
    pl.semaphore_signal(barrier, inc=1, device_id=sib, device_id_type=MESH)
    for k in range(1, SIDE):
        pl.semaphore_signal(barrier, inc=1, device_id=(sx, fs(up(y, k), z, c)), device_id_type=MESH)
        pl.semaphore_signal(barrier, inc=1, device_id=(sx, fs(y, up(z, k), c)), device_id_type=MESH)

    load_x = pltpu.make_async_copy(x_hbm, xin, local_sem.at[0])
    load_y = pltpu.make_async_copy(y_hbm, yin, local_sem.at[1])
    load_d = pltpu.make_async_copy(dir_hbm, dir_ref, local_sem.at[6])
    load_r = pltpu.make_async_copy(res_hbm, res_ref, local_sem.at[7])
    load_d.start()
    load_x.start()
    load_y.start()
    load_r.start()

    pl.semaphore_wait(barrier, 1 + 3 * (SIDE - 1))

    counter = Counter()
    pending = []

    def send(src, dst, dev):
        k = counter.take()
        copy = pltpu.make_async_remote_copy(
            src_ref=src, dst_ref=dst, send_sem=send_sem.at[k], recv_sem=recv_sem.at[k],
            device_id=dev, device_id_type=MESH,
        )
        copy.start()
        pending.append(copy)
        return k

    def send_all(triples):
        k = counter.take()
        for src, dst, dev in triples:
            pltpu.make_async_remote_copy(
                src_ref=src, dst_ref=dst, send_sem=send_sem.at[k], recv_sem=recv_sem.at[k],
                device_id=dev, device_id_type=MESH,
            ).start()
        return k

    def arrive_all(k, whole):
        copy = pltpu.make_async_remote_copy(
            src_ref=whole, dst_ref=whole, send_sem=send_sem.at[k], recv_sem=recv_sem.at[k],
            device_id=(sx, f), device_id_type=MESH,
        )
        copy.wait_recv()
        pending.append(copy)

    def flush():
        while pending:
            pending.pop(0).wait_send()

    def arrive(k, dst):
        pltpu.make_async_remote_copy(
            src_ref=dst, dst_ref=dst, send_sem=send_sem.at[k], recv_sem=recv_sem.at[k],
            device_id=(sx, f), device_id_type=MESH,
        ).wait_recv()

    def rows(ref, at, size):
        return ref.at[pl.ds(pl.multiple_of(at * size, size), size)]

    def rows2(ref, at):
        return ref.at[:, pl.ds(pl.multiple_of(at * pr, pr), pr)]

    def cols(at):
        return pl.ds(pl.multiple_of(at * rank, rank), rank)

    def spread(srcs, arrs):
        keys = []
        for src, arr in zip(srcs, arrs):
            for k in range(1, N_LAYER):
                to = up(sx, k)
                keys.append((arr, k, send(rows(src, to, pr), w.at[arr, y, z, :, cols(sx)], line(k))))
        copies = []
        for n, (src, arr) in enumerate(zip(srcs, arrs)):
            copy = pltpu.make_async_copy(
                rows(src, sx, pr), w.at[arr, y, z, :, cols(sx)], local_sem.at[2 + arr]
            )
            copy.start()
            copies.append(copy)
        return keys, copies

    def spread_done(keys, copies):
        for copy in copies:
            copy.wait()
        for arr, k, key in keys:
            arrive(key, w.at[arr, y, z, :, cols(up(sx, -k))])

    ab_keys = spread((a_ref, b_ref), (0, 1))
    load_d.wait()
    pbf[...] = dir_ref[...].astype(bf16)

    class Gather:
        def __init__(self, arr, first):
            self.arr, self.first, self.key = arr, first, {}

        def dev(self, i, j):
            dy, dz = (i, j) if self.first == "y" else (j, i)
            return (sx, fs(up(y, dy), up(z, dz), c))

        def block(self, i):
            if self.first == "y":
                return w.at[self.arr, up(y, i), z]
            return w.at[self.arr, y, up(z, i)]

        def pair(self, p, j):
            if self.first == "y":
                return w.at[self.arr, pl.ds(2 * p, 2), up(z, j)]
            return w.at[self.arr, up(y, j), pl.ds(2 * p, 2)]

        def push(self, name, ref, di, dj):
            self.key[name] = send(ref, ref, self.dev(di, dj))

        def start(self):
            for i in (2, 1, -1):
                self.push(i, self.block(0), i, 0)

        def second(self):
            for i in (1, -1, 2):
                arrive(self.key[i], self.block(-i))
            self.push("r1", self.pair(0, 0), 0, 1)
            self.push("l1", self.pair(1, 0), 0, -1)

        def second_rest(self):
            self.push("r2", self.pair(1, 0), 0, 1)
            self.push("l2", self.pair(0, 0), 0, -1)

        def relay(self):
            arrive(self.key["r1"], self.pair(0, -1))
            self.push("rr", self.pair(0, -1), 0, 1)
            arrive(self.key["l1"], self.pair(1, 1))
            self.push("ll", self.pair(1, 1), 0, -1)

        def finish(self):
            arrive(self.key["r2"], self.pair(1, -1))
            arrive(self.key["l2"], self.pair(0, 1))
            arrive(self.key["rr"], self.pair(0, 2))
            arrive(self.key["ll"], self.pair(1, 2))

    ga, gb = Gather(0, "y"), Gather(1, "z")
    gpa, gpb = Gather(2, "y"), Gather(3, "z")
    def pick(src, dst, cc, put):
        odd = lax.rem(sx, 2) == 1
        for p in range(0, CHIPS, 2):
            tiles = []
            for q in (p, p + 1):
                at = (2 * q + cc) * own + lax.div(sx, 2) * (2 * pr)
                tiles.append(src[:, pl.ds(pl.multiple_of(at, 2 * pr), 2 * pr)])
            even = jnp.concatenate([t[:, :pr] for t in tiles], axis=1)
            put(dst, p, jnp.where(odd, jnp.concatenate([t[:, pr:] for t in tiles], axis=1), even))

    def put_other(dst, p, value):
        dst[:, p * pr : (p + 2) * pr] = value

    def put_own(dst, p, value):
        dst[pl.ds(pl.multiple_of(c * tseq, tseq), tseq), p * pr : (p + 2) * pr] = value

    my_rows = pl.ds(pl.multiple_of(c * tseq, tseq), tseq)
    its_rows = pl.ds(pl.multiple_of((1 - c) * tseq, tseq), tseq)
    load_x.wait()
    pick(xin, xs, 1 - c, put_other)
    key_xs = send(xs, xg.at[my_rows], sib)
    load_y.wait()
    pick(yin, ys, 1 - c, put_other)
    key_ys = send(ys, yg.at[my_rows], sib)
    spread_done(*ab_keys)
    ga.start()
    gb.start()
    p_keys = [send(rows2(pbf, up(sx, k)), w.at[2:4, y, z, :, cols(sx)], line(k)) for k in (2, 1, 3)]
    copy_p = pltpu.make_async_copy(rows2(pbf, sx), w.at[2:4, y, z, :, cols(sx)], local_sem.at[4])
    copy_p.start()
    half_rows = rank // 2
    mine_a, mine_b = w[0, y, z], w[1, y, z]
    for j in range(N_LAYER):
        left = mine_b[:, j * rank : (j + 1) * rank]
        if j < N_LAYER - 1:
            block = dot_tn(left, mine_a[:, (j + 1) * rank :])
            for l in range(j + 1, N_LAYER):
                b = CROSS[(j, l)]
                gram[2 * b : 2 * b + 2] = block[:, (l - j - 1) * rank : (l - j) * rank].reshape(2, half_rows, rank)
        block = dot_tn(left, mine_b[:, j * rank :])
        for l in range(j, N_LAYER):
            b = SELF[(j, l)]
            gram[2 * b : 2 * b + 2] = block[:, (l - j) * rank : (l - j + 1) * rank].reshape(2, half_rows, rank)
    my_gram = pl.ds(c * CHIPS, CHIPS)
    its_gram = pl.ds((1 - c) * CHIPS, CHIPS)
    gram_out[...] = gram[its_gram].astype(bf16)
    key_gram = send(gram_out, gram_in, sib)
    pick(xin, xg, c, put_own)
    pick(yin, yg, c, put_own)
    arrive(key_gram, gram_in)
    gpair = gram[my_gram] + gram_in[...].astype(f32)
    gram[my_gram] = gpair
    gramx_out[...] = gpair.astype(bf16)

    def chip(k):
        return up(y, k // SIDE) * SIDE + up(z, k % SIDE)

    def chip_dev(k):
        return (sx, fs(up(y, k // SIDE), up(z, k % SIDE), c))

    ga.second()
    gb.second()
    gkey = send_all([(gramx_out.at[chip(k)], gramx_in.at[k - 1], chip_dev(k)) for k in range(1, CHIPS)])
    ga.second_rest()
    gb.second_rest()
    xq = xin[pl.ds(pl.multiple_of(sx * tq, tq), tq), :].astype(f32)
    norm = jnp.sum(xq * xq, axis=1, keepdims=True)
    load_r.wait()
    res = res_ref[...]
    direc = dir_ref[...]

    def fold_home(v):
        return jnp.sum(v.reshape(-1, rank), axis=0, keepdims=True)

    dd = fold_home(direc * direc)
    home = jnp.concatenate(
        [fold_home(res * res), dd, fold_home(res * direc), dd, jnp.zeros((4, rank), f32)], axis=0
    )
    arrive(key_xs, xg.at[its_rows])
    arrive(key_ys, yg.at[its_rows])
    xt[...] = xg[...].astype(f32).T.astype(bf16)
    yt[...] = yg[...].astype(f32).T.astype(bf16)
    my_piece = c * CHIPS + y * SIDE + z
    arrive_all(gkey, gramx_in)
    gsum = gram[my_piece] + jnp.sum(gramx_in[...].astype(f32), axis=0)
    gline_out[...] = gsum.astype(bf16)
    gkey = send_all([(gline_out, gline_in.at[k - 1], line(k)) for k in (2, 1, 3)])
    ga.relay()
    gb.relay()
    copy_p.wait()
    for key, k in zip(p_keys, (2, 1, 3)):
        arrive(key, w.at[2:4, y, z, :, cols(up(sx, -k))])
    gpa.start()
    gpb.start()
    arrive_all(gkey, gline_in)
    gfull[my_piece] = (gsum + jnp.sum(gline_in[...].astype(f32), axis=0)).astype(bf16)
    gkey = send_all([(gfull.at[my_piece], gfull.at[my_piece], chip_dev(k)) for k in range(1, CHIPS)])
    res_keys = [send(rows2(res_ref, up(sx, k)), res_s.at[:, :, cols(sx)], line(k)) for k in (2, 1, 3)]
    res_s[:, :, cols(sx)] = res_ref[:, pl.ds(pl.multiple_of(sx * pr, pr), pr)]
    ga.finish()
    gb.finish()

    wide = N_LAYER * rank
    wa = w[0].reshape(feats, wide)
    wb = w[1].reshape(feats, wide)
    xv = xg[...]
    yv = yg[...]
    both_x = 2 * wide
    prod[:, 0:wide] = dot_nn(xv, wa)
    prod[:, wide:both_x] = dot_nn(xv, wb)
    prod_out[:, 0:both_x] = prod[its_rows, 0:both_x].astype(bf16)
    key_px = send(prod_out.at[:, 0:both_x], prod_in.at[:, 0:both_x], sib)
    gpa.second()
    gpb.second()
    gpa.second_rest()
    gpb.second_rest()
    prod[:, both_x:] = dot_nn(yv, wb)
    prod_out[:, both_x:] = prod[its_rows, both_x:].astype(bf16)
    key_py = send(prod_out.at[:, both_x:], prod_in.at[:, both_x:], sib)

    def pair_sum(key, at):
        arrive(key, prod_in.at[:, at])
        pair = prod[my_rows, at] + prod_in[:, at].astype(f32)
        prod[my_rows, at] = pair
        prodx_out[:, at] = pair.astype(bf16)
        keys = []
        for k in (2, 1, 3):
            src = prodx_out.at[pl.ds(pl.multiple_of(up(sx, k) * tq, tq), tq), at]
            keys.append(send(src, prodx_in.at[k - 1, :, at], line(k)))
        return keys

    in_x, in_y = slice(0, both_x), slice(both_x, 3 * wide)
    pxkeys = pair_sum(key_px, in_x)
    pykeys = pair_sum(key_py, in_y)
    arrive_all(gkey, gfull.at[0 : CHIPS - 1])
    key_gfull = send(gfull.at[my_gram], gfull.at[my_gram], sib)
    gpa.relay()
    gpb.relay()
    token_rows = pl.ds(pl.multiple_of(c * tseq + sx * tq, tq), tq)

    def line_sum(keys, at):
        total = prod[token_rows, at]
        for key, k in zip(keys, (2, 1, 3)):
            arrive(key, prodx_in.at[k - 1, :, at])
            total = total + prodx_in[k - 1, :, at].astype(f32)
        return total

    psum = line_sum(pxkeys, in_x)
    arrive(key_gfull, gfull.at[its_gram])

    def gblock(b):
        return gfull[2 * b : 2 * b + 2].reshape(rank, rank)

    def part(value, k):
        return value[:, k * rank : (k + 1) * rank]

    ha = [part(psum, l) for l in range(N_LAYER)]
    hb = [part(psum, N_LAYER + l) for l in range(N_LAYER)]
    acts, slopes, rhos, pres, hbs = [], [], [], [], []
    for l in range(N_LAYER):
        rho = jnp.sqrt(norm / width + norm_eps)
        pre = ha[l] / rho
        sig = jax.nn.sigmoid(pre)
        a = (pre * sig).astype(bf16)
        hbs.append(hb[:l])
        before = hb[l]
        for m in range(l + 1, N_LAYER):
            ha[m] = ha[m] + dot_nn(a, gblock(CROSS[(l, m)]))
        nxt = []
        for m in range(N_LAYER):
            if l <= m:
                nxt.append(hb[m] + dot_nn(a, gblock(SELF[(l, m)])))
            else:
                nxt.append(hb[m] + dot_nt(a, gblock(SELF[(m, l)])))
        hb = nxt
        norm = norm + jnp.sum(a.astype(f32) * (before + hb[l]), axis=1, keepdims=True)
        acts.append(a)
        slopes.append(sig * (1.0 + pre * (1.0 - sig)))
        rhos.append(rho)
        pres.append(pre)
    my_act = token_rows
    a_cols, q_cols = slice(0, wide), slice(wide, 2 * wide + rank)
    for l in range(N_LAYER):
        act[my_act, l * rank : (l + 1) * rank] = acts[l]
    akeys = [send(act.at[my_act, a_cols], act.at[my_act, a_cols], line(k)) for k in (2, 1, 3)]
    ysum = line_sum(pykeys, in_y)
    cb = [hb[l] - part(ysum, l) for l in range(N_LAYER)]
    qs = [None] * N_LAYER
    lane = lax.broadcasted_iota(jnp.int32, (tq, rank), 1)
    gains = jnp.zeros((tq, rank), f32)
    for l in range(N_LAYER - 1, -1, -1):
        cot = cb[l] * slopes[l]
        qs[l] = (cot / rhos[l]).astype(bf16)
        if l > 0:
            gain = jnp.sum(cot * pres[l], axis=1, keepdims=True) / (width * rhos[l] * rhos[l])
            gains = jnp.where(lane == l, gain, gains)
            for j in range(l):
                cb[j] = cb[j] + dot_nt(qs[l], gblock(CROSS[(j, l)])) - gain * hbs[l][j]
    for l in range(N_LAYER):
        act[my_act, (N_LAYER + l) * rank : (N_LAYER + l + 1) * rank] = qs[l]
    act[my_act, 2 * wide :] = gains.astype(bf16)
    qkeys = [send(act.at[my_act, q_cols], act.at[my_act, q_cols], line(k)) for k in (2, 1, 3)]
    def share(keys, at):
        for key, k in zip(keys, (2, 1, 3)):
            arrive(key, act.at[pl.ds(pl.multiple_of(c * tseq + up(sx, -k) * tq, tq), tq), at])
        return send(act.at[my_rows, at], act.at[my_rows, at], sib)

    key = share(akeys, a_cols)
    arrive(key, act.at[its_rows, a_cols])

    def wq(arr, l, q):
        return w[arr, q, :, :, l * rank : (l + 1) * rank].reshape(quad, rank)

    av = [act[:, l * rank : (l + 1) * rank] for l in range(N_LAYER)]
    for q in range(SIDE):
        fr = slice(q * quad, (q + 1) * quad)
        h = xt[fr, :].astype(f32)
        for l in range(N_LAYER):
            hb16 = h.astype(bf16)
            ht[l, fr, :] = hb16
            h = hb16.astype(f32) + dot_nt(wq(1, l, q), av[l])
        ht[2 * N_LAYER - 1, fr, :] = (h - yt[fr, :].astype(f32)).astype(bf16)
    key = share(qkeys, q_cols)
    gpa.finish()
    gpb.finish()
    arrive(key, act.at[its_rows, q_cols])
    qv = [act[:, (N_LAYER + l) * rank : (N_LAYER + l + 1) * rank] for l in range(N_LAYER)]
    gain_t = act[:, 2 * N_LAYER * rank :].astype(f32).T
    d0 = jnp.zeros((quad, rank), f32)
    d1 = jnp.zeros((quad, rank), f32)
    for q in range(SIDE):
        fr = slice(q * quad, (q + 1) * quad)
        cot = ht[2 * N_LAYER - 1, fr, :]
        for l in range(N_LAYER - 1, -1, -1):
            hl = ht[l, fr, :]
            for arr, left, right in ((2, hl, qv[l]), (3, cot, av[l])):
                pw = wq(arr, l, q).astype(f32)
                d0 = d0 + dot_nn(left[:, :tseq], right[:tseq]) * pw
                d1 = d1 + dot_nn(left[:, tseq:], right[tseq:]) * pw
            if l > 0:
                cot = (
                    cot.astype(f32) + dot_nt(wq(0, l, q), qv[l]) - gain_t[l : l + 1, :] * hl.astype(f32)
                ).astype(bf16)
                ht[N_LAYER + l - 1, fr, :] = cot

    def fold(v):
        return jnp.sum(v.reshape(-1, rank), axis=0, keepdims=True)

    def stack(values):
        return jnp.concatenate([fold(v) for v in values] + [jnp.zeros((8 - len(values), rank), f32)], axis=0)

    dv_out[...] = stack([d0, d1])
    eight = [(up(sx, k // 2), fs(y, z, lax.rem(c + k, 2))) for k in range(1, 8)]
    key = send_all([(dv_out, dv_in.at[k], dev) for k, dev in enumerate(eight)])
    arrive_all(key, dv_in)
    dv = dv_out[...] + jnp.sum(dv_in[...], axis=0)
    s0 = jnp.sum(dv[0:1], keepdims=True) / (tseq * width)
    s1 = jnp.sum(dv[1:2], keepdims=True) / (tseq * width)
    token = lax.broadcasted_iota(jnp.int32, (2 * tseq, 1), 0)
    scale = jnp.where(token < tseq, s0, s1)
    qd = [(qv[l].astype(f32) * scale).astype(bf16) for l in range(N_LAYER)]
    ad = [(av[l].astype(f32) * scale).astype(bf16) for l in range(N_LAYER)]

    def gradient(arr, base, right):
        for l in range(N_LAYER):
            for q in range(SIDE):
                value = dot_nn(ht[base + l, q * quad : (q + 1) * quad, :], right[l])
                g[arr, q, :, :, l * rank : (l + 1) * rank] = value.astype(bf16).reshape(SIDE, pr, rank)

    class Scatter:
        def __init__(self, arr, last):
            self.arr, self.last, self.key = arr, last, {}
            self.at = y if last == "y" else z

        def dev(self, i, j):
            dy, dz = (i, j) if self.last == "y" else (j, i)
            return (sx, fs(up(y, dy), up(z, dz), c))

        def pair(self, p, j):
            if self.last == "y":
                return self.arr, pl.ds(2 * p, 2), up(z, j)
            return self.arr, up(y, j), pl.ds(2 * p, 2)

        def push(self, n, p, j, dj):
            self.key[n] = send(g.at[self.pair(p, j)], pair_in.at[self.arr, n], self.dev(0, dj))

        def arrived(self, n):
            arrive(self.key[n], pair_in.at[self.arr, n])
            return pair_in[self.arr, n].astype(f32)

        def start(self):
            self.push(0, 0, 2, 1)
            self.push(1, 1, 2, -1)
            self.push(2, 1, 1, 1)
            self.push(3, 0, -1, -1)

        def middle(self):
            at = self.pair(0, 1)
            g[at] = (g[at].astype(f32) + self.arrived(0)).astype(bf16)
            self.push(4, 0, 1, 1)
            at = self.pair(1, -1)
            g[at] = (g[at].astype(f32) + self.arrived(1)).astype(bf16)
            self.push(5, 1, -1, -1)

        def end(self):
            acc2[self.arr, 2:4] = g[self.pair(1, 0)].astype(f32) + self.arrived(2) + self.arrived(5)
            acc2[self.arr, 0:2] = g[self.pair(0, 0)].astype(f32) + self.arrived(3) + self.arrived(4)
            fin[self.arr, 0:SIDE] = acc2[self.arr].astype(bf16)
            for i in (2, 1, -1):
                self.key[("s", i)] = send(
                    fin.at[self.arr, up(self.at, i)], block_in.at[self.arr, i % SIDE - 1], self.dev(i, 0)
                )

        def end2(self):
            value = acc2[self.arr, self.at]
            for i in (1, -1, 2):
                arrive(self.key[("s", i)], block_in.at[self.arr, i % SIDE - 1])
                value = value + block_in[self.arr, i % SIDE - 1].astype(f32)
            self.value = value
            fin[self.arr, SIDE] = value.astype(bf16)
            self.back = []
            for k in range(1, N_LAYER):
                to = up(sx, k)
                self.back.append(send(fin.at[self.arr, SIDE, :, cols(to)], gx.at[self.arr, sx], line(k)))
            gx[self.arr, sx] = fin[self.arr, SIDE, :, cols(sx)]

        def done(self):
            for k in range(1, N_LAYER):
                arrive(self.back[k - 1], gx.at[self.arr, up(sx, -k)])

    both = (Scatter(0, "y"), Scatter(1, "z"))
    gradient(0, 0, qd)
    both[0].start()
    gradient(1, N_LAYER, ad)
    both[1].start()
    flush()
    for s in both:
        s.middle()
    for s in both:
        s.end()
    for s in both:
        s.end2()
    tokens_total = tseq * 2 * CHIPS
    shrink = 1.0 / (damping * tokens_total * width)

    def lanes(v):
        return sum(v[:, l * rank : (l + 1) * rank] for l in range(N_LAYER))

    pg = rg = gg = 0.0
    for key, k in zip(res_keys, (2, 1, 3)):
        arrive(key, res_s.at[:, :, cols(up(sx, -k))])
    for s in both:
        pg = pg + lanes(s.value * w[2 + s.arr, y, z].astype(f32))
        rg = rg + lanes(s.value * res_s[s.arr])
        gg = gg + lanes(s.value * s.value)
    pg, rg, gg = fold(pg) * shrink, fold(rg) * shrink, fold(gg) * (shrink * shrink)
    stat_out[...] = home + jnp.concatenate(
        [jnp.zeros((1, rank), f32), pg, rg, 2.0 * pg + gg, jnp.zeros((4, rank), f32)], axis=0
    )
    key = send_all([(stat_out, stat_in.at[k], dev) for k, dev in enumerate(eight)])
    flush()
    arrive_all(key, stat_in)
    total = stat_out[...] + jnp.sum(stat_in[...], axis=0)
    stat2_out[...] = total
    key = send_all([(stat2_out, stat2_in.at[k - 1], chip_dev(k)) for k in range(1, CHIPS)])
    for s in both:
        s.done()
    big = gx[...].astype(f32).reshape(2, own, rank) * shrink + direc
    flush()
    arrive_all(key, stat2_in)
    total = total + jnp.sum(stat2_in[...], axis=0)
    rr = jnp.sum(total[0:1], keepdims=True)
    pq = jnp.sum(total[1:2], keepdims=True) * damping
    rp = jnp.sum(total[2:3], keepdims=True)
    pp = jnp.sum(total[3:4], keepdims=True)
    step = rr / pq * damping
    norm_new = rr - 2.0 * (step * rp) + step * (step * pp)
    new_res = res - step * big
    newres_ref[...] = new_res
    newdir_ref[...] = new_res + (norm_new / rr) * direc
    assert counter.n == N_SEM
    flush()


def step_kernel(inputs, targets, down_proj, up_proj, direction, residual):
    tseq, width = inputs.shape
    _, own, rank = down_proj.shape
    pr = own // N_LAYER
    feats = CHIPS * pr
    tq = tseq // N_LAYER
    wide = N_LAYER * rank
    hr = rank // 2
    vm = pltpu.VMEM
    scratch = [
        vm((tseq, width), bf16), vm((tseq, width), bf16),
        vm((2, own, rank), f32), vm((2, own, rank), f32),
        vm((2 * tseq, feats), bf16), vm((2 * tseq, feats), bf16),
        vm((tseq, feats), bf16), vm((tseq, feats), bf16),
        vm((feats, 2 * tseq), bf16), vm((feats, 2 * tseq), bf16),
        vm((4, SIDE, SIDE, pr, wide), bf16), vm((2, own, rank), bf16),
        vm((2 * tseq, 3 * wide), f32), vm((tseq, 3 * wide), bf16), vm((tseq, 3 * wide), bf16),
        vm((tseq, 3 * wide), bf16), vm((N_LAYER - 1, tq, 3 * wide), bf16),
        vm((2 * CHIPS, hr, rank), f32), vm((CHIPS, hr, rank), bf16), vm((CHIPS, hr, rank), bf16),
        vm((CHIPS, hr, rank), bf16), vm((CHIPS - 1, hr, rank), bf16), vm((hr, rank), bf16),
        vm((N_LAYER - 1, hr, rank), bf16), vm((2 * CHIPS, hr, rank), bf16),
        vm((2, pr, wide), f32),
        vm((2 * tseq, 2 * wide + rank), bf16), vm((2 * N_LAYER, feats, 2 * tseq), bf16),
        vm((2, SIDE, SIDE, pr, wide), bf16),
        vm((2, 6, 2, pr, wide), bf16),
        vm((2, SIDE, pr, wide), f32),
        vm((2, 3, pr, wide), bf16), vm((2, SIDE + 1, pr, wide), bf16),
        vm((2, N_LAYER, pr, rank), bf16),
        vm((8, rank), f32), vm((7, 8, rank), f32), vm((8, rank), f32), vm((CHIPS - 1, 8, rank), f32),
        vm((8, rank), f32), vm((7, 8, rank), f32),
        pltpu.SemaphoreType.DMA((N_SEM,)), pltpu.SemaphoreType.DMA((N_SEM,)), pltpu.SemaphoreType.DMA((8,)),
    ]
    hbm = pl.BlockSpec(memory_space=pl.ANY)
    spec = pl.BlockSpec(memory_space=pltpu.VMEM)
    operands = (inputs, targets, down_proj[0], up_proj[0], direction[0], residual[0])
    out = pltpu.VMEM((2, own, rank), f32)
    new_res, new_dir = pl.pallas_call(
        kernel,
        out_shape=(out, out),
        in_specs=[hbm] * 6,
        out_specs=(spec, spec),
        scratch_shapes=scratch,
        compiler_params=pltpu.CompilerParams(
            collective_id=0, has_side_effects=True, vmem_limit_bytes=50 * 1024 * 1024
        ),
        cost_estimate=pl.CostEstimate(flops=4_000_000_000, bytes_accessed=8_000_000, transcendentals=0),
    )(*(pltpu.with_memory_space_constraint(v, pltpu.HBM) for v in operands))
    return new_res[None], new_dir[None]


def solution(mesh):
    in_specs = (
        P("fsdp", None),
        P("fsdp", None),
        P("section", "fsdp", None),
        P("section", "fsdp", None),
        P("section", None, "fsdp", None),
        P("section", None, "fsdp", None),
    )
    out_specs = (P("section", None, "fsdp", None), P("section", None, "fsdp", None))
    return jax.shard_map(step_kernel, mesh=mesh, in_specs=in_specs, out_specs=out_specs, check_vma=False)
```

```python
import functools

import jax
import jax.numpy as jnp
from jax import lax
from jax.experimental import pallas as pl
from jax.experimental.pallas import tpu as pltpu
from jax.sharding import PartitionSpec as P

MESH = pl.DeviceIdType.MESH
bf16 = jnp.bfloat16
f32 = jnp.float32

norm_eps = 1e-05
damping = 1e-06
N_LAYER = 4
SIDE = 4
CHIPS = 16

CROSS = {}
for _j in range(N_LAYER):
    for _l in range(_j + 1, N_LAYER):
        CROSS[(_j, _l)] = len(CROSS)
SELF = {}
for _j in range(N_LAYER):
    for _l in range(_j, N_LAYER):
        SELF[(_j, _l)] = len(CROSS) + len(SELF)
N_GRAM = len(CROSS) + len(SELF)


def dot_nn(a, b):
    return lax.dot_general(a, b, (((1,), (0,)), ((), ())), preferred_element_type=f32)


def dot_nt(a, b):
    return lax.dot_general(a, b, (((1,), (1,)), ((), ())), preferred_element_type=f32)


def dot_tn(a, b):
    return lax.dot_general(a, b, (((0,), (0,)), ((), ())), preferred_element_type=f32)


class Counter:
    def __init__(self):
        self.n = 0

    def take(self):
        self.n += 1
        return self.n - 1


N_SEM = 98


def kernel(
    x_hbm, y_hbm, a_ref, b_ref, dir_hbm, res_hbm,
    newres_ref, newdir_ref,
    xin, yin, dir_ref, res_ref, xg, yg, xs, ys, xt, yt, w, pbf,
    prod, prod_out, prod_in, prodx_out, prodx_in,
    gram, gram_out, gram_in, gramx_out, gramx_in, gline_out, gline_in, gfull, res_s,
    act, ht, g, pair_in, acc2, block_in, fin,
    gx, stat_out, stat_in, stat2_out, stat2_in, dv_out, dv_in,
    send_sem, recv_sem, local_sem,
):
    tseq, width = xin.shape
    rank = a_ref.shape[1]
    own = a_ref.shape[0]
    pr = own // N_LAYER
    feats = CHIPS * pr
    tq = tseq // N_LAYER
    quad = SIDE * pr
    sx = lax.axis_index("section")
    f = lax.axis_index("fsdp")
    c = lax.rem(f, 2)
    z = lax.rem(lax.div(f, 2), SIDE)
    y = lax.div(f, 2 * SIDE)

    def up(v, k):
        return lax.rem(v + k + SIDE, SIDE)

    def fs(yy, zz, cc):
        return (yy * SIDE + zz) * 2 + cc

    barrier = pltpu.get_barrier_semaphore()
    sib = (sx, fs(y, z, 1 - c))

    def line(k):
        return (up(sx, k), f)

    for k in range(1, N_LAYER):
        pl.semaphore_signal(barrier, inc=1, device_id=line(k), device_id_type=MESH)
    pl.semaphore_signal(barrier, inc=1, device_id=sib, device_id_type=MESH)
    for k in range(1, SIDE):
        pl.semaphore_signal(barrier, inc=1, device_id=(sx, fs(up(y, k), z, c)), device_id_type=MESH)
        pl.semaphore_signal(barrier, inc=1, device_id=(sx, fs(y, up(z, k), c)), device_id_type=MESH)

    load_x = pltpu.make_async_copy(x_hbm, xin, local_sem.at[0])
    load_y = pltpu.make_async_copy(y_hbm, yin, local_sem.at[1])
    load_d = pltpu.make_async_copy(dir_hbm, dir_ref, local_sem.at[6])
    load_r = pltpu.make_async_copy(res_hbm, res_ref, local_sem.at[7])
    load_d.start()
    load_x.start()
    load_y.start()
    load_r.start()

    pl.semaphore_wait(barrier, 1 + 3 * (SIDE - 1))

    counter = Counter()
    pending = []

    def send(src, dst, dev):
        k = counter.take()
        copy = pltpu.make_async_remote_copy(
            src_ref=src, dst_ref=dst, send_sem=send_sem.at[k], recv_sem=recv_sem.at[k],
            device_id=dev, device_id_type=MESH,
        )
        copy.start()
        pending.append(copy)
        return k

    def send_all(triples):
        k = counter.take()
        for src, dst, dev in triples:
            pltpu.make_async_remote_copy(
                src_ref=src, dst_ref=dst, send_sem=send_sem.at[k], recv_sem=recv_sem.at[k],
                device_id=dev, device_id_type=MESH,
            ).start()
        return k

    def arrive_all(k, whole):
        copy = pltpu.make_async_remote_copy(
            src_ref=whole, dst_ref=whole, send_sem=send_sem.at[k], recv_sem=recv_sem.at[k],
            device_id=(sx, f), device_id_type=MESH,
        )
        copy.wait_recv()
        pending.append(copy)

    def flush():
        while pending:
            pending.pop(0).wait_send()

    def arrive(k, dst):
        pltpu.make_async_remote_copy(
            src_ref=dst, dst_ref=dst, send_sem=send_sem.at[k], recv_sem=recv_sem.at[k],
            device_id=(sx, f), device_id_type=MESH,
        ).wait_recv()

    def rows(ref, at, size):
        return ref.at[pl.ds(pl.multiple_of(at * size, size), size)]

    def rows2(ref, at):
        return ref.at[:, pl.ds(pl.multiple_of(at * pr, pr), pr)]

    def cols(at):
        return pl.ds(pl.multiple_of(at * rank, rank), rank)

    def spread(srcs, arrs):
        keys = []
        for src, arr in zip(srcs, arrs):
            for k in range(1, N_LAYER):
                to = up(sx, k)
                keys.append((arr, k, send(rows(src, to, pr), w.at[arr, y, z, :, cols(sx)], line(k))))
        copies = []
        for n, (src, arr) in enumerate(zip(srcs, arrs)):
            copy = pltpu.make_async_copy(
                rows(src, sx, pr), w.at[arr, y, z, :, cols(sx)], local_sem.at[2 + arr]
            )
            copy.start()
            copies.append(copy)
        return keys, copies

    def spread_done(keys, copies):
        for copy in copies:
            copy.wait()
        for arr, k, key in keys:
            arrive(key, w.at[arr, y, z, :, cols(up(sx, -k))])

    ab_keys = spread((a_ref, b_ref), (0, 1))
    load_d.wait()
    pbf[...] = dir_ref[...].astype(bf16)

    class Gather:
        def __init__(self, arr, first):
            self.arr, self.first, self.key = arr, first, {}

        def dev(self, i, j):
            dy, dz = (i, j) if self.first == "y" else (j, i)
            return (sx, fs(up(y, dy), up(z, dz), c))

        def block(self, i):
            if self.first == "y":
                return w.at[self.arr, up(y, i), z]
            return w.at[self.arr, y, up(z, i)]

        def pair(self, p, j):
            if self.first == "y":
                return w.at[self.arr, pl.ds(2 * p, 2), up(z, j)]
            return w.at[self.arr, up(y, j), pl.ds(2 * p, 2)]

        def push(self, name, ref, di, dj):
            self.key[name] = send(ref, ref, self.dev(di, dj))

        def start(self):
            for i in (2, 1, -1):
                self.push(i, self.block(0), i, 0)

        def second(self):
            for i in (1, -1, 2):
                arrive(self.key[i], self.block(-i))
            self.push("r1", self.pair(0, 0), 0, 1)
            self.push("l1", self.pair(1, 0), 0, -1)

        def second_rest(self):
            self.push("r2", self.pair(1, 0), 0, 1)
            self.push("l2", self.pair(0, 0), 0, -1)

        def relay(self):
            arrive(self.key["r1"], self.pair(0, -1))
            self.push("rr", self.pair(0, -1), 0, 1)
            arrive(self.key["l1"], self.pair(1, 1))
            self.push("ll", self.pair(1, 1), 0, -1)

        def finish(self):
            arrive(self.key["r2"], self.pair(1, -1))
            arrive(self.key["l2"], self.pair(0, 1))
            arrive(self.key["rr"], self.pair(0, 2))
            arrive(self.key["ll"], self.pair(1, 2))

    ga, gb = Gather(0, "y"), Gather(1, "z")
    gpa, gpb = Gather(2, "y"), Gather(3, "z")
    def pick(src, dst, cc, put):
        odd = lax.rem(sx, 2) == 1
        for p in range(0, CHIPS, 2):
            tiles = []
            for q in (p, p + 1):
                at = (2 * q + cc) * own + lax.div(sx, 2) * (2 * pr)
                tiles.append(src[:, pl.ds(pl.multiple_of(at, 2 * pr), 2 * pr)])
            even = jnp.concatenate([t[:, :pr] for t in tiles], axis=1)
            put(dst, p, jnp.where(odd, jnp.concatenate([t[:, pr:] for t in tiles], axis=1), even))

    def put_other(dst, p, value):
        dst[:, p * pr : (p + 2) * pr] = value

    def put_own(dst, p, value):
        dst[pl.ds(pl.multiple_of(c * tseq, tseq), tseq), p * pr : (p + 2) * pr] = value

    my_rows = pl.ds(pl.multiple_of(c * tseq, tseq), tseq)
    its_rows = pl.ds(pl.multiple_of((1 - c) * tseq, tseq), tseq)
    load_x.wait()
    pick(xin, xs, 1 - c, put_other)
    key_xs = send(xs, xg.at[my_rows], sib)
    load_y.wait()
    pick(yin, ys, 1 - c, put_other)
    key_ys = send(ys, yg.at[my_rows], sib)
    spread_done(*ab_keys)
    ga.start()
    gb.start()
    p_keys = [send(rows2(pbf, up(sx, k)), w.at[2:4, y, z, :, cols(sx)], line(k)) for k in (2, 1, 3)]
    copy_p = pltpu.make_async_copy(rows2(pbf, sx), w.at[2:4, y, z, :, cols(sx)], local_sem.at[4])
    copy_p.start()
    half_rows = rank // 2
    mine_a, mine_b = w[0, y, z], w[1, y, z]
    for j in range(N_LAYER):
        left = mine_b[:, j * rank : (j + 1) * rank]
        if j < N_LAYER - 1:
            block = dot_tn(left, mine_a[:, (j + 1) * rank :])
            for l in range(j + 1, N_LAYER):
                b = CROSS[(j, l)]
                gram[2 * b : 2 * b + 2] = block[:, (l - j - 1) * rank : (l - j) * rank].reshape(2, half_rows, rank)
        block = dot_tn(left, mine_b[:, j * rank :])
        for l in range(j, N_LAYER):
            b = SELF[(j, l)]
            gram[2 * b : 2 * b + 2] = block[:, (l - j) * rank : (l - j + 1) * rank].reshape(2, half_rows, rank)
    my_gram = pl.ds(c * CHIPS, CHIPS)
    its_gram = pl.ds((1 - c) * CHIPS, CHIPS)
    gram_out[...] = gram[its_gram].astype(bf16)
    key_gram = send(gram_out, gram_in, sib)
    pick(xin, xg, c, put_own)
    pick(yin, yg, c, put_own)
    arrive(key_gram, gram_in)
    gpair = gram[my_gram] + gram_in[...].astype(f32)
    gram[my_gram] = gpair
    gramx_out[...] = gpair.astype(bf16)

    def chip(k):
        return up(y, k // SIDE) * SIDE + up(z, k % SIDE)

    def chip_dev(k):
        return (sx, fs(up(y, k // SIDE), up(z, k % SIDE), c))

    ga.second()
    gb.second()
    gkey = send_all([(gramx_out.at[chip(k)], gramx_in.at[k - 1], chip_dev(k)) for k in range(1, CHIPS)])
    ga.second_rest()
    gb.second_rest()
    xq = xin[pl.ds(pl.multiple_of(sx * tq, tq), tq), :].astype(f32)
    norm = jnp.sum(xq * xq, axis=1, keepdims=True)
    load_r.wait()
    res = res_ref[...]
    direc = dir_ref[...]

    def fold_home(v):
        return jnp.sum(v.reshape(-1, rank), axis=0, keepdims=True)

    dd = fold_home(direc * direc)
    home = jnp.concatenate(
        [fold_home(res * res), dd, fold_home(res * direc), dd, jnp.zeros((4, rank), f32)], axis=0
    )
    arrive(key_xs, xg.at[its_rows])
    arrive(key_ys, yg.at[its_rows])
    xt[...] = xg[...].astype(f32).T.astype(bf16)
    yt[...] = yg[...].astype(f32).T.astype(bf16)
    my_piece = c * CHIPS + y * SIDE + z
    arrive_all(gkey, gramx_in)
    gsum = gram[my_piece] + jnp.sum(gramx_in[...].astype(f32), axis=0)
    gline_out[...] = gsum.astype(bf16)
    gkey = send_all([(gline_out, gline_in.at[k - 1], line(k)) for k in (2, 1, 3)])
    ga.relay()
    gb.relay()
    copy_p.wait()
    for key, k in zip(p_keys, (2, 1, 3)):
        arrive(key, w.at[2:4, y, z, :, cols(up(sx, -k))])
    gpa.start()
    gpb.start()
    arrive_all(gkey, gline_in)
    gfull[my_piece] = (gsum + jnp.sum(gline_in[...].astype(f32), axis=0)).astype(bf16)
    gkey = send_all([(gfull.at[my_piece], gfull.at[my_piece], chip_dev(k)) for k in range(1, CHIPS)])
    res_keys = [send(rows2(res_ref, up(sx, k)), res_s.at[:, :, cols(sx)], line(k)) for k in (2, 1, 3)]
    res_s[:, :, cols(sx)] = res_ref[:, pl.ds(pl.multiple_of(sx * pr, pr), pr)]
    ga.finish()
    gb.finish()

    wide = N_LAYER * rank
    wa = w[0].reshape(feats, wide)
    wb = w[1].reshape(feats, wide)
    xv = xg[...]
    yv = yg[...]
    both_x = 2 * wide
    prod[:, 0:wide] = dot_nn(xv, wa)
    prod[:, wide:both_x] = dot_nn(xv, wb)
    prod_out[:, 0:both_x] = prod[its_rows, 0:both_x].astype(bf16)
    key_px = send(prod_out.at[:, 0:both_x], prod_in.at[:, 0:both_x], sib)
    gpa.second()
    gpb.second()
    gpa.second_rest()
    gpb.second_rest()
    prod[:, both_x:] = dot_nn(yv, wb)
    prod_out[:, both_x:] = prod[its_rows, both_x:].astype(bf16)
    key_py = send(prod_out.at[:, both_x:], prod_in.at[:, both_x:], sib)

    def pair_sum(key, at):
        arrive(key, prod_in.at[:, at])
        pair = prod[my_rows, at] + prod_in[:, at].astype(f32)
        prod[my_rows, at] = pair
        prodx_out[:, at] = pair.astype(bf16)
        keys = []
        for k in (2, 1, 3):
            src = prodx_out.at[pl.ds(pl.multiple_of(up(sx, k) * tq, tq), tq), at]
            keys.append(send(src, prodx_in.at[k - 1, :, at], line(k)))
        return keys

    in_x, in_y = slice(0, both_x), slice(both_x, 3 * wide)
    pxkeys = pair_sum(key_px, in_x)
    pykeys = pair_sum(key_py, in_y)
    arrive_all(gkey, gfull.at[0 : CHIPS - 1])
    key_gfull = send(gfull.at[my_gram], gfull.at[my_gram], sib)
    gpa.relay()
    gpb.relay()
    token_rows = pl.ds(pl.multiple_of(c * tseq + sx * tq, tq), tq)

    def line_sum(keys, at):
        total = prod[token_rows, at]
        for key, k in zip(keys, (2, 1, 3)):
            arrive(key, prodx_in.at[k - 1, :, at])
            total = total + prodx_in[k - 1, :, at].astype(f32)
        return total

    psum = line_sum(pxkeys, in_x)
    arrive(key_gfull, gfull.at[its_gram])

    def gblock(b):
        return gfull[2 * b : 2 * b + 2].reshape(rank, rank)

    def part(value, k):
        return value[:, k * rank : (k + 1) * rank]

    ha = [part(psum, l) for l in range(N_LAYER)]
    hb = [part(psum, N_LAYER + l) for l in range(N_LAYER)]
    acts, slopes, rhos, pres, hbs = [], [], [], [], []
    for l in range(N_LAYER):
        rho = jnp.sqrt(norm / width + norm_eps)
        pre = ha[l] / rho
        sig = jax.nn.sigmoid(pre)
        a = (pre * sig).astype(bf16)
        hbs.append(hb[:l])
        before = hb[l]
        for m in range(l + 1, N_LAYER):
            ha[m] = ha[m] + dot_nn(a, gblock(CROSS[(l, m)]))
        nxt = []
        for m in range(N_LAYER):
            if l <= m:
                nxt.append(hb[m] + dot_nn(a, gblock(SELF[(l, m)])))
            else:
                nxt.append(hb[m] + dot_nt(a, gblock(SELF[(m, l)])))
        hb = nxt
        norm = norm + jnp.sum(a.astype(f32) * (before + hb[l]), axis=1, keepdims=True)
        acts.append(a)
        slopes.append(sig * (1.0 + pre * (1.0 - sig)))
        rhos.append(rho)
        pres.append(pre)
    my_act = token_rows
    a_cols, q_cols = slice(0, wide), slice(wide, 2 * wide + rank)
    for l in range(N_LAYER):
        act[my_act, l * rank : (l + 1) * rank] = acts[l]
    akeys = [send(act.at[my_act, a_cols], act.at[my_act, a_cols], line(k)) for k in (2, 1, 3)]
    ysum = line_sum(pykeys, in_y)
    cb = [hb[l] - part(ysum, l) for l in range(N_LAYER)]
    qs = [None] * N_LAYER
    lane = lax.broadcasted_iota(jnp.int32, (tq, rank), 1)
    gains = jnp.zeros((tq, rank), f32)
    for l in range(N_LAYER - 1, -1, -1):
        cot = cb[l] * slopes[l]
        qs[l] = (cot / rhos[l]).astype(bf16)
        if l > 0:
            gain = jnp.sum(cot * pres[l], axis=1, keepdims=True) / (width * rhos[l] * rhos[l])
            gains = jnp.where(lane == l, gain, gains)
            for j in range(l):
                cb[j] = cb[j] + dot_nt(qs[l], gblock(CROSS[(j, l)])) - gain * hbs[l][j]
    for l in range(N_LAYER):
        act[my_act, (N_LAYER + l) * rank : (N_LAYER + l + 1) * rank] = qs[l]
    act[my_act, 2 * wide :] = gains.astype(bf16)
    qkeys = [send(act.at[my_act, q_cols], act.at[my_act, q_cols], line(k)) for k in (2, 1, 3)]
    def share(keys, at):
        for key, k in zip(keys, (2, 1, 3)):
            arrive(key, act.at[pl.ds(pl.multiple_of(c * tseq + up(sx, -k) * tq, tq), tq), at])
        return send(act.at[my_rows, at], act.at[my_rows, at], sib)

    key = share(akeys, a_cols)
    arrive(key, act.at[its_rows, a_cols])

    def wq(arr, l, q):
        return w[arr, q, :, :, l * rank : (l + 1) * rank].reshape(quad, rank)

    av = [act[:, l * rank : (l + 1) * rank] for l in range(N_LAYER)]
    for q in range(SIDE):
        fr = slice(q * quad, (q + 1) * quad)
        h = xt[fr, :].astype(f32)
        for l in range(N_LAYER):
            hb16 = h.astype(bf16)
            ht[l, fr, :] = hb16
            h = hb16.astype(f32) + dot_nt(wq(1, l, q), av[l])
        ht[2 * N_LAYER - 1, fr, :] = (h - yt[fr, :].astype(f32)).astype(bf16)
    key = share(qkeys, q_cols)
    gpa.finish()
    gpb.finish()
    arrive(key, act.at[its_rows, q_cols])
    qv = [act[:, (N_LAYER + l) * rank : (N_LAYER + l + 1) * rank] for l in range(N_LAYER)]
    gain_t = act[:, 2 * N_LAYER * rank :].astype(f32).T
    first = lax.broadcasted_iota(jnp.int32, (2 * tseq, rank), 0) < tseq

    def apart(v):
        none = jnp.zeros_like(v)
        return jnp.concatenate([jnp.where(first, v, none), jnp.where(first, none, v)], axis=1)

    apart_q, apart_a = [apart(v) for v in qv], [apart(v) for v in av]
    both_d = jnp.zeros((quad, 2 * rank), f32)
    for q in range(SIDE):
        fr = slice(q * quad, (q + 1) * quad)
        cot = ht[2 * N_LAYER - 1, fr, :]
        for l in range(N_LAYER - 1, -1, -1):
            hl = ht[l, fr, :]
            for arr, left, right in ((2, hl, apart_q[l]), (3, cot, apart_a[l])):
                pw = wq(arr, l, q).astype(f32)
                both_d = both_d + dot_nn(left, right) * jnp.concatenate([pw, pw], axis=1)
            if l > 0:
                cot = (
                    cot.astype(f32) + dot_nt(wq(0, l, q), qv[l]) - gain_t[l : l + 1, :] * hl.astype(f32)
                ).astype(bf16)
                ht[N_LAYER + l - 1, fr, :] = cot

    def fold(v):
        return jnp.sum(v.reshape(-1, rank), axis=0, keepdims=True)

    def stack(values):
        return jnp.concatenate([fold(v) for v in values] + [jnp.zeros((8 - len(values), rank), f32)], axis=0)

    dv_out[...] = stack([both_d[:, :rank], both_d[:, rank:]])
    eight = [(up(sx, k // 2), fs(y, z, lax.rem(c + k, 2))) for k in range(1, 8)]
    key = send_all([(dv_out, dv_in.at[k], dev) for k, dev in enumerate(eight)])
    arrive_all(key, dv_in)
    dv = dv_out[...] + jnp.sum(dv_in[...], axis=0)
    s0 = jnp.sum(dv[0:1], keepdims=True) / (tseq * width)
    s1 = jnp.sum(dv[1:2], keepdims=True) / (tseq * width)
    token = lax.broadcasted_iota(jnp.int32, (2 * tseq, 1), 0)
    scale = jnp.where(token < tseq, s0, s1)
    qd = [(qv[l].astype(f32) * scale).astype(bf16) for l in range(N_LAYER)]
    ad = [(av[l].astype(f32) * scale).astype(bf16) for l in range(N_LAYER)]

    def gradient(arr, q):
        base, right = ((0, qd), (N_LAYER, ad))[arr]
        at = pl.ds(pl.multiple_of(q * quad, quad), quad)
        for l in range(N_LAYER):
            value = dot_nn(ht[base + l, at, :], right[l])
            g[arr, q, :, :, l * rank : (l + 1) * rank] = value.astype(bf16).reshape(SIDE, pr, rank)

    class Scatter:
        def __init__(self, arr, last):
            self.arr, self.last, self.key = arr, last, {}
            self.at = y if last == "y" else z

        def dev(self, i, j):
            dy, dz = (i, j) if self.last == "y" else (j, i)
            return (sx, fs(up(y, dy), up(z, dz), c))

        def pair(self, p, j):
            if self.last == "y":
                return self.arr, pl.ds(2 * p, 2), up(z, j)
            return self.arr, up(y, j), pl.ds(2 * p, 2)

        def push(self, n, p, j, dj):
            self.key[n] = send(g.at[self.pair(p, j)], pair_in.at[self.arr, n], self.dev(0, dj))

        def arrived(self, n):
            arrive(self.key[n], pair_in.at[self.arr, n])
            return pair_in[self.arr, n].astype(f32)

        def start(self, n):
            self.push(n, *((0, 2, 1), (1, 2, -1), (1, 1, 1), (0, -1, -1))[n])

        def middle(self):
            at = self.pair(0, 1)
            g[at] = (g[at].astype(f32) + self.arrived(0)).astype(bf16)
            self.push(4, 0, 1, 1)
            at = self.pair(1, -1)
            g[at] = (g[at].astype(f32) + self.arrived(1)).astype(bf16)
            self.push(5, 1, -1, -1)

        def end(self):
            acc2[self.arr, 2:4] = g[self.pair(1, 0)].astype(f32) + self.arrived(2) + self.arrived(5)
            acc2[self.arr, 0:2] = g[self.pair(0, 0)].astype(f32) + self.arrived(3) + self.arrived(4)
            fin[self.arr, 0:SIDE] = acc2[self.arr].astype(bf16)
            for i in (2, 1, -1):
                self.key[("s", i)] = send(
                    fin.at[self.arr, up(self.at, i)], block_in.at[self.arr, i % SIDE - 1], self.dev(i, 0)
                )

        def end2(self):
            value = acc2[self.arr, self.at]
            for i in (1, -1, 2):
                arrive(self.key[("s", i)], block_in.at[self.arr, i % SIDE - 1])
                value = value + block_in[self.arr, i % SIDE - 1].astype(f32)
            self.value = value
            fin[self.arr, SIDE] = value.astype(bf16)
            self.back = []
            for k in range(1, N_LAYER):
                to = up(sx, k)
                self.back.append(send(fin.at[self.arr, SIDE, :, cols(to)], gx.at[self.arr, sx], line(k)))
            gx[self.arr, sx] = fin[self.arr, SIDE, :, cols(sx)]

        def done(self):
            for k in range(1, N_LAYER):
                arrive(self.back[k - 1], gx.at[self.arr, up(sx, -k)])

    both = (Scatter(0, "y"), Scatter(1, "z"))
    gradient(1, up(y, 2))
    both[1].start(0)
    both[1].start(1)
    for q in range(2):
        gradient(0, q)
    both[0].start(0)
    for q in range(2, SIDE):
        gradient(0, q)
    for n in range(1, SIDE):
        both[0].start(n)
    gradient(1, up(y, 1))
    both[1].start(2)
    gradient(1, up(y, -1))
    both[1].start(3)
    gradient(1, y)
    flush()
    for s in both:
        s.middle()
    for s in both:
        s.end()
    for s in both:
        s.end2()
    tokens_total = tseq * 2 * CHIPS
    shrink = 1.0 / (damping * tokens_total * width)

    def lanes(v):
        return sum(v[:, l * rank : (l + 1) * rank] for l in range(N_LAYER))

    pg = rg = gg = 0.0
    for key, k in zip(res_keys, (2, 1, 3)):
        arrive(key, res_s.at[:, :, cols(up(sx, -k))])
    for s in both:
        pg = pg + lanes(s.value * w[2 + s.arr, y, z].astype(f32))
        rg = rg + lanes(s.value * res_s[s.arr])
        gg = gg + lanes(s.value * s.value)
    pg, rg, gg = fold(pg) * shrink, fold(rg) * shrink, fold(gg) * (shrink * shrink)
    stat_out[...] = home + jnp.concatenate(
        [jnp.zeros((1, rank), f32), pg, rg, 2.0 * pg + gg, jnp.zeros((4, rank), f32)], axis=0
    )
    key = send_all([(stat_out, stat_in.at[k], dev) for k, dev in enumerate(eight)])
    flush()
    arrive_all(key, stat_in)
    total = stat_out[...] + jnp.sum(stat_in[...], axis=0)
    stat2_out[...] = total
    key = send_all([(stat2_out, stat2_in.at[k - 1], chip_dev(k)) for k in range(1, CHIPS)])
    for s in both:
        s.done()
    big = gx[...].astype(f32).reshape(2, own, rank) * shrink + direc
    flush()
    arrive_all(key, stat2_in)
    total = total + jnp.sum(stat2_in[...], axis=0)
    rr = jnp.sum(total[0:1], keepdims=True)
    pq = jnp.sum(total[1:2], keepdims=True) * damping
    rp = jnp.sum(total[2:3], keepdims=True)
    pp = jnp.sum(total[3:4], keepdims=True)
    step = rr / pq * damping
    norm_new = rr - 2.0 * (step * rp) + step * (step * pp)
    new_res = res - step * big
    newres_ref[...] = new_res
    newdir_ref[...] = new_res + (norm_new / rr) * direc
    assert counter.n == N_SEM
    flush()


def step_kernel(inputs, targets, down_proj, up_proj, direction, residual):
    tseq, width = inputs.shape
    _, own, rank = down_proj.shape
    pr = own // N_LAYER
    feats = CHIPS * pr
    tq = tseq // N_LAYER
    wide = N_LAYER * rank
    hr = rank // 2
    vm = pltpu.VMEM
    scratch = [
        vm((tseq, width), bf16), vm((tseq, width), bf16),
        vm((2, own, rank), f32), vm((2, own, rank), f32),
        vm((2 * tseq, feats), bf16), vm((2 * tseq, feats), bf16),
        vm((tseq, feats), bf16), vm((tseq, feats), bf16),
        vm((feats, 2 * tseq), bf16), vm((feats, 2 * tseq), bf16),
        vm((4, SIDE, SIDE, pr, wide), bf16), vm((2, own, rank), bf16),
        vm((2 * tseq, 3 * wide), f32), vm((tseq, 3 * wide), bf16), vm((tseq, 3 * wide), bf16),
        vm((tseq, 3 * wide), bf16), vm((N_LAYER - 1, tq, 3 * wide), bf16),
        vm((2 * CHIPS, hr, rank), f32), vm((CHIPS, hr, rank), bf16), vm((CHIPS, hr, rank), bf16),
        vm((CHIPS, hr, rank), bf16), vm((CHIPS - 1, hr, rank), bf16), vm((hr, rank), bf16),
        vm((N_LAYER - 1, hr, rank), bf16), vm((2 * CHIPS, hr, rank), bf16),
        vm((2, pr, wide), f32),
        vm((2 * tseq, 2 * wide + rank), bf16), vm((2 * N_LAYER, feats, 2 * tseq), bf16),
        vm((2, SIDE, SIDE, pr, wide), bf16),
        vm((2, 6, 2, pr, wide), bf16),
        vm((2, SIDE, pr, wide), f32),
        vm((2, 3, pr, wide), bf16), vm((2, SIDE + 1, pr, wide), bf16),
        vm((2, N_LAYER, pr, rank), bf16),
        vm((8, rank), f32), vm((7, 8, rank), f32), vm((8, rank), f32), vm((CHIPS - 1, 8, rank), f32),
        vm((8, rank), f32), vm((7, 8, rank), f32),
        pltpu.SemaphoreType.DMA((N_SEM,)), pltpu.SemaphoreType.DMA((N_SEM,)), pltpu.SemaphoreType.DMA((8,)),
    ]
    hbm = pl.BlockSpec(memory_space=pl.ANY)
    spec = pl.BlockSpec(memory_space=pltpu.VMEM)
    operands = (inputs, targets, down_proj[0], up_proj[0], direction[0], residual[0])
    out = pltpu.VMEM((2, own, rank), f32)
    new_res, new_dir = pl.pallas_call(
        kernel,
        out_shape=(out, out),
        in_specs=[hbm] * 6,
        out_specs=(spec, spec),
        scratch_shapes=scratch,
        compiler_params=pltpu.CompilerParams(
            collective_id=0, has_side_effects=True, vmem_limit_bytes=50 * 1024 * 1024
        ),
        cost_estimate=pl.CostEstimate(flops=4_000_000_000, bytes_accessed=8_000_000, transcendentals=0),
    )(*(pltpu.with_memory_space_constraint(v, pltpu.HBM) for v in operands))
    return new_res[None], new_dir[None]


def solution(mesh):
    in_specs = (
        P("fsdp", None),
        P("fsdp", None),
        P("section", "fsdp", None),
        P("section", "fsdp", None),
        P("section", None, "fsdp", None),
        P("section", None, "fsdp", None),
    )
    out_specs = (P("section", None, "fsdp", None), P("section", None, "fsdp", None))
    return jax.shard_map(step_kernel, mesh=mesh, in_specs=in_specs, out_specs=out_specs, check_vma=False)
```

```python
import functools

import jax
import jax.numpy as jnp
from jax import lax
from jax.experimental import pallas as pl
from jax.experimental.pallas import tpu as pltpu
from jax.sharding import PartitionSpec as P

MESH = pl.DeviceIdType.MESH
bf16 = jnp.bfloat16
f32 = jnp.float32

norm_eps = 1e-05
damping = 1e-06
N_LAYER = 4
SIDE = 4
CHIPS = 16

CROSS = {}
for _j in range(N_LAYER):
    for _l in range(_j + 1, N_LAYER):
        CROSS[(_j, _l)] = len(CROSS)
SELF = {}
for _j in range(N_LAYER):
    for _l in range(_j, N_LAYER):
        SELF[(_j, _l)] = len(CROSS) + len(SELF)
N_GRAM = len(CROSS) + len(SELF)


def dot_nn(a, b):
    return lax.dot_general(a, b, (((1,), (0,)), ((), ())), preferred_element_type=f32)


def dot_nt(a, b):
    return lax.dot_general(a, b, (((1,), (1,)), ((), ())), preferred_element_type=f32)


def dot_tn(a, b):
    return lax.dot_general(a, b, (((0,), (0,)), ((), ())), preferred_element_type=f32)


class Counter:
    def __init__(self):
        self.n = 0

    def take(self):
        self.n += 1
        return self.n - 1


N_SEM = 98


def kernel(
    x_hbm, y_hbm, a_ref, b_ref, dir_hbm, res_hbm,
    newres_ref, newdir_ref,
    xin, yin, dir_ref, res_ref, xg, yg, xs, ys, xt, yt, w, pbf,
    prod, prod_out, prod_in, prodx_out, prodx_in,
    gram, gram_out, gram_in, gramx_out, gramx_in, gline_out, gline_in, gfull, res_s,
    act, ht, g, pair_in, acc2, block_in, fin,
    gx, stat_out, stat_in, stat2_out, stat2_in, dv_out, dv_in,
    send_sem, recv_sem, local_sem,
):
    tseq, width = xin.shape
    rank = a_ref.shape[1]
    own = a_ref.shape[0]
    pr = own // N_LAYER
    feats = CHIPS * pr
    tq = tseq // N_LAYER
    quad = SIDE * pr
    sx = lax.axis_index("section")
    f = lax.axis_index("fsdp")
    c = lax.rem(f, 2)
    z = lax.rem(lax.div(f, 2), SIDE)
    y = lax.div(f, 2 * SIDE)

    def up(v, k):
        return lax.rem(v + k + SIDE, SIDE)

    def fs(yy, zz, cc):
        return (yy * SIDE + zz) * 2 + cc

    barrier = pltpu.get_barrier_semaphore()
    sib = (sx, fs(y, z, 1 - c))

    def line(k):
        return (up(sx, k), f)

    for k in range(1, N_LAYER):
        pl.semaphore_signal(barrier, inc=1, device_id=line(k), device_id_type=MESH)
    pl.semaphore_signal(barrier, inc=1, device_id=sib, device_id_type=MESH)
    for k in range(1, SIDE):
        pl.semaphore_signal(barrier, inc=1, device_id=(sx, fs(up(y, k), z, c)), device_id_type=MESH)
        pl.semaphore_signal(barrier, inc=1, device_id=(sx, fs(y, up(z, k), c)), device_id_type=MESH)

    load_x = pltpu.make_async_copy(x_hbm, xin, local_sem.at[0])
    load_y = pltpu.make_async_copy(y_hbm, yin, local_sem.at[1])
    load_d = pltpu.make_async_copy(dir_hbm, dir_ref, local_sem.at[6])
    load_r = pltpu.make_async_copy(res_hbm, res_ref, local_sem.at[7])
    load_d.start()
    load_x.start()
    load_y.start()
    load_r.start()

    pl.semaphore_wait(barrier, 1 + 3 * (SIDE - 1))

    counter = Counter()
    pending = []

    def send(src, dst, dev):
        k = counter.take()
        copy = pltpu.make_async_remote_copy(
            src_ref=src, dst_ref=dst, send_sem=send_sem.at[k], recv_sem=recv_sem.at[k],
            device_id=dev, device_id_type=MESH,
        )
        copy.start()
        pending.append(copy)
        return k

    def send_all(triples):
        k = counter.take()
        for src, dst, dev in triples:
            pltpu.make_async_remote_copy(
                src_ref=src, dst_ref=dst, send_sem=send_sem.at[k], recv_sem=recv_sem.at[k],
                device_id=dev, device_id_type=MESH,
            ).start()
        return k

    def arrive_all(k, whole):
        copy = pltpu.make_async_remote_copy(
            src_ref=whole, dst_ref=whole, send_sem=send_sem.at[k], recv_sem=recv_sem.at[k],
            device_id=(sx, f), device_id_type=MESH,
        )
        copy.wait_recv()
        pending.append(copy)

    def flush():
        while pending:
            pending.pop(0).wait_send()

    def arrive(k, dst):
        pltpu.make_async_remote_copy(
            src_ref=dst, dst_ref=dst, send_sem=send_sem.at[k], recv_sem=recv_sem.at[k],
            device_id=(sx, f), device_id_type=MESH,
        ).wait_recv()

    def rows(ref, at, size):
        return ref.at[pl.ds(pl.multiple_of(at * size, size), size)]

    def rows2(ref, at):
        return ref.at[:, pl.ds(pl.multiple_of(at * pr, pr), pr)]

    def cols(at):
        return pl.ds(pl.multiple_of(at * rank, rank), rank)

    def spread(srcs, arrs):
        keys = []
        for src, arr in zip(srcs, arrs):
            for k in range(1, N_LAYER):
                to = up(sx, k)
                keys.append((arr, k, send(rows(src, to, pr), w.at[arr, y, z, :, cols(sx)], line(k))))
        copies = []
        for n, (src, arr) in enumerate(zip(srcs, arrs)):
            copy = pltpu.make_async_copy(
                rows(src, sx, pr), w.at[arr, y, z, :, cols(sx)], local_sem.at[2 + arr]
            )
            copy.start()
            copies.append(copy)
        return keys, copies

    def spread_done(keys, copies):
        for copy in copies:
            copy.wait()
        for arr, k, key in keys:
            arrive(key, w.at[arr, y, z, :, cols(up(sx, -k))])

    ab_keys = spread((a_ref, b_ref), (0, 1))
    load_d.wait()
    pbf[...] = dir_ref[...].astype(bf16)

    class Gather:
        def __init__(self, arr, first):
            self.arr, self.first, self.key = arr, first, {}

        def dev(self, i, j):
            dy, dz = (i, j) if self.first == "y" else (j, i)
            return (sx, fs(up(y, dy), up(z, dz), c))

        def block(self, i):
            if self.first == "y":
                return w.at[self.arr, up(y, i), z]
            return w.at[self.arr, y, up(z, i)]

        def pair(self, p, j):
            if self.first == "y":
                return w.at[self.arr, pl.ds(2 * p, 2), up(z, j)]
            return w.at[self.arr, up(y, j), pl.ds(2 * p, 2)]

        def push(self, name, ref, di, dj):
            self.key[name] = send(ref, ref, self.dev(di, dj))

        def start(self):
            for i in (2, 1, -1):
                self.push(i, self.block(0), i, 0)

        def second(self):
            for i in (1, -1, 2):
                arrive(self.key[i], self.block(-i))
            self.push("r1", self.pair(0, 0), 0, 1)
            self.push("l1", self.pair(1, 0), 0, -1)

        def second_rest(self):
            self.push("r2", self.pair(1, 0), 0, 1)
            self.push("l2", self.pair(0, 0), 0, -1)

        def relay(self):
            arrive(self.key["r1"], self.pair(0, -1))
            self.push("rr", self.pair(0, -1), 0, 1)
            arrive(self.key["l1"], self.pair(1, 1))
            self.push("ll", self.pair(1, 1), 0, -1)

        def finish(self):
            arrive(self.key["r2"], self.pair(1, -1))
            arrive(self.key["l2"], self.pair(0, 1))
            arrive(self.key["rr"], self.pair(0, 2))
            arrive(self.key["ll"], self.pair(1, 2))

    ga, gb = Gather(0, "y"), Gather(1, "z")
    gpa, gpb = Gather(2, "y"), Gather(3, "z")
    def pick(src, dst, cc, put):
        odd = lax.rem(sx, 2) == 1
        for p in range(0, CHIPS, 2):
            tiles = []
            for q in (p, p + 1):
                at = (2 * q + cc) * own + lax.div(sx, 2) * (2 * pr)
                tiles.append(src[:, pl.ds(pl.multiple_of(at, 2 * pr), 2 * pr)])
            even = jnp.concatenate([t[:, :pr] for t in tiles], axis=1)
            put(dst, p, jnp.where(odd, jnp.concatenate([t[:, pr:] for t in tiles], axis=1), even))

    def put_other(dst, p, value):
        dst[:, p * pr : (p + 2) * pr] = value

    def put_own(dst, p, value):
        dst[pl.ds(pl.multiple_of(c * tseq, tseq), tseq), p * pr : (p + 2) * pr] = value

    my_rows = pl.ds(pl.multiple_of(c * tseq, tseq), tseq)
    its_rows = pl.ds(pl.multiple_of((1 - c) * tseq, tseq), tseq)
    load_x.wait()
    pick(xin, xs, 1 - c, put_other)
    key_xs = send(xs, xg.at[my_rows], sib)
    load_y.wait()
    pick(yin, ys, 1 - c, put_other)
    key_ys = send(ys, yg.at[my_rows], sib)
    spread_done(*ab_keys)
    ga.start()
    gb.start()
    p_keys = [send(rows2(pbf, up(sx, k)), w.at[2:4, y, z, :, cols(sx)], line(k)) for k in (2, 1, 3)]
    copy_p = pltpu.make_async_copy(rows2(pbf, sx), w.at[2:4, y, z, :, cols(sx)], local_sem.at[4])
    copy_p.start()
    half_rows = rank // 2
    mine_a, mine_b = w[0, y, z], w[1, y, z]
    for j in range(N_LAYER):
        left = mine_b[:, j * rank : (j + 1) * rank]
        if j < N_LAYER - 1:
            block = dot_tn(left, mine_a[:, (j + 1) * rank :])
            for l in range(j + 1, N_LAYER):
                b = CROSS[(j, l)]
                gram[2 * b : 2 * b + 2] = block[:, (l - j - 1) * rank : (l - j) * rank].reshape(2, half_rows, rank)
        block = dot_tn(left, mine_b[:, j * rank :])
        for l in range(j, N_LAYER):
            b = SELF[(j, l)]
            gram[2 * b : 2 * b + 2] = block[:, (l - j) * rank : (l - j + 1) * rank].reshape(2, half_rows, rank)
    my_gram = pl.ds(c * CHIPS, CHIPS)
    its_gram = pl.ds((1 - c) * CHIPS, CHIPS)
    gram_out[...] = gram[its_gram].astype(bf16)
    key_gram = send(gram_out, gram_in, sib)
    pick(xin, xg, c, put_own)
    pick(yin, yg, c, put_own)
    arrive(key_gram, gram_in)
    gpair = gram[my_gram] + gram_in[...].astype(f32)
    gram[my_gram] = gpair
    gramx_out[...] = gpair.astype(bf16)

    def chip(k):
        return up(y, k // SIDE) * SIDE + up(z, k % SIDE)

    def chip_dev(k):
        return (sx, fs(up(y, k // SIDE), up(z, k % SIDE), c))

    ga.second()
    gb.second()
    gkey = send_all([(gramx_out.at[chip(k)], gramx_in.at[k - 1], chip_dev(k)) for k in range(1, CHIPS)])
    ga.second_rest()
    gb.second_rest()
    xq = xin[pl.ds(pl.multiple_of(sx * tq, tq), tq), :].astype(f32)
    norm = jnp.sum(xq * xq, axis=1, keepdims=True)
    load_r.wait()
    res = res_ref[...]
    direc = dir_ref[...]

    def fold_home(v):
        return jnp.sum(v.reshape(-1, rank), axis=0, keepdims=True)

    dd = fold_home(direc * direc)
    home = jnp.concatenate(
        [fold_home(res * res), dd, fold_home(res * direc), dd, jnp.zeros((4, rank), f32)], axis=0
    )
    arrive(key_xs, xg.at[its_rows])
    arrive(key_ys, yg.at[its_rows])
    xt[...] = xg[...].astype(f32).T.astype(bf16)
    yt[...] = yg[...].astype(f32).T.astype(bf16)
    my_piece = c * CHIPS + y * SIDE + z
    arrive_all(gkey, gramx_in)
    gsum = gram[my_piece] + jnp.sum(gramx_in[...].astype(f32), axis=0)
    gline_out[...] = gsum.astype(bf16)
    gkey = send_all([(gline_out, gline_in.at[k - 1], line(k)) for k in (2, 1, 3)])
    ga.relay()
    gb.relay()
    copy_p.wait()
    for key, k in zip(p_keys, (2, 1, 3)):
        arrive(key, w.at[2:4, y, z, :, cols(up(sx, -k))])
    gpa.start()
    gpb.start()
    arrive_all(gkey, gline_in)
    gfull[my_piece] = (gsum + jnp.sum(gline_in[...].astype(f32), axis=0)).astype(bf16)
    gkey = send_all([(gfull.at[my_piece], gfull.at[my_piece], chip_dev(k)) for k in range(1, CHIPS)])
    res_keys = [send(rows2(res_ref, up(sx, k)), res_s.at[:, :, cols(sx)], line(k)) for k in (2, 1, 3)]
    res_s[:, :, cols(sx)] = res_ref[:, pl.ds(pl.multiple_of(sx * pr, pr), pr)]
    ga.finish()
    gb.finish()

    wide = N_LAYER * rank
    wa = w[0].reshape(feats, wide)
    wb = w[1].reshape(feats, wide)
    xv = xg[...]
    yv = yg[...]
    both_x = 2 * wide
    prod[:, 0:wide] = dot_nn(xv, wa)
    prod[:, wide:both_x] = dot_nn(xv, wb)
    prod_out[:, 0:both_x] = prod[its_rows, 0:both_x].astype(bf16)
    key_px = send(prod_out.at[:, 0:both_x], prod_in.at[:, 0:both_x], sib)
    gpa.second()
    gpb.second()
    gpa.second_rest()
    gpb.second_rest()
    prod[:, both_x:] = dot_nn(yv, wb)
    prod_out[:, both_x:] = prod[its_rows, both_x:].astype(bf16)
    key_py = send(prod_out.at[:, both_x:], prod_in.at[:, both_x:], sib)

    def pair_sum(key, at):
        arrive(key, prod_in.at[:, at])
        pair = prod[my_rows, at] + prod_in[:, at].astype(f32)
        prod[my_rows, at] = pair
        prodx_out[:, at] = pair.astype(bf16)
        keys = []
        for k in (2, 1, 3):
            src = prodx_out.at[pl.ds(pl.multiple_of(up(sx, k) * tq, tq), tq), at]
            keys.append(send(src, prodx_in.at[k - 1, :, at], line(k)))
        return keys

    in_x, in_y = slice(0, both_x), slice(both_x, 3 * wide)
    pxkeys = pair_sum(key_px, in_x)
    pykeys = pair_sum(key_py, in_y)
    arrive_all(gkey, gfull.at[0 : CHIPS - 1])
    key_gfull = send(gfull.at[my_gram], gfull.at[my_gram], sib)
    gpa.relay()
    gpb.relay()
    token_rows = pl.ds(pl.multiple_of(c * tseq + sx * tq, tq), tq)

    def line_sum(keys, at):
        total = prod[token_rows, at]
        for key, k in zip(keys, (2, 1, 3)):
            arrive(key, prodx_in.at[k - 1, :, at])
            total = total + prodx_in[k - 1, :, at].astype(f32)
        return total

    psum = line_sum(pxkeys, in_x)
    arrive(key_gfull, gfull.at[its_gram])

    def gblock(b):
        return gfull[2 * b : 2 * b + 2].reshape(rank, rank)

    def part(value, k):
        return value[:, k * rank : (k + 1) * rank]

    ha = [part(psum, l) for l in range(N_LAYER)]
    hb = [part(psum, N_LAYER + l) for l in range(N_LAYER)]
    acts, slopes, rhos, pres, hbs = [], [], [], [], []
    for l in range(N_LAYER):
        rho = jnp.sqrt(norm / width + norm_eps)
        pre = ha[l] / rho
        sig = jax.nn.sigmoid(pre)
        a = (pre * sig).astype(bf16)
        hbs.append(hb[:l])
        before = hb[l]
        for m in range(l + 1, N_LAYER):
            ha[m] = ha[m] + dot_nn(a, gblock(CROSS[(l, m)]))
        nxt = []
        for m in range(N_LAYER):
            if l <= m:
                nxt.append(hb[m] + dot_nn(a, gblock(SELF[(l, m)])))
            else:
                nxt.append(hb[m] + dot_nt(a, gblock(SELF[(m, l)])))
        hb = nxt
        norm = norm + jnp.sum(a.astype(f32) * (before + hb[l]), axis=1, keepdims=True)
        acts.append(a)
        slopes.append(sig * (1.0 + pre * (1.0 - sig)))
        rhos.append(rho)
        pres.append(pre)
    my_act = token_rows
    a_cols, q_cols = slice(0, wide), slice(wide, 2 * wide + rank)
    for l in range(N_LAYER):
        act[my_act, l * rank : (l + 1) * rank] = acts[l]
    akeys = [send(act.at[my_act, a_cols], act.at[my_act, a_cols], line(k)) for k in (2, 1, 3)]
    ysum = line_sum(pykeys, in_y)
    cb = [hb[l] - part(ysum, l) for l in range(N_LAYER)]
    qs = [None] * N_LAYER
    lane = lax.broadcasted_iota(jnp.int32, (tq, rank), 1)
    gains = jnp.zeros((tq, rank), f32)
    for l in range(N_LAYER - 1, -1, -1):
        cot = cb[l] * slopes[l]
        qs[l] = (cot / rhos[l]).astype(bf16)
        if l > 0:
            gain = jnp.sum(cot * pres[l], axis=1, keepdims=True) / (width * rhos[l] * rhos[l])
            gains = jnp.where(lane == l, gain, gains)
            for j in range(l):
                cb[j] = cb[j] + dot_nt(qs[l], gblock(CROSS[(j, l)])) - gain * hbs[l][j]
    for l in range(N_LAYER):
        act[my_act, (N_LAYER + l) * rank : (N_LAYER + l + 1) * rank] = qs[l]
    act[my_act, 2 * wide :] = gains.astype(bf16)
    qkeys = [send(act.at[my_act, q_cols], act.at[my_act, q_cols], line(k)) for k in (2, 1, 3)]
    def share(keys, at):
        for key, k in zip(keys, (2, 1, 3)):
            arrive(key, act.at[pl.ds(pl.multiple_of(c * tseq + up(sx, -k) * tq, tq), tq), at])
        return send(act.at[my_rows, at], act.at[my_rows, at], sib)

    key = share(akeys, a_cols)
    arrive(key, act.at[its_rows, a_cols])

    def wq(arr, l, q):
        return w[arr, q, :, :, l * rank : (l + 1) * rank].reshape(quad, rank)

    av = [act[:, l * rank : (l + 1) * rank] for l in range(N_LAYER)]
    for q in range(SIDE):
        fr = slice(q * quad, (q + 1) * quad)
        h = xt[fr, :].astype(f32)
        for l in range(N_LAYER):
            hb16 = h.astype(bf16)
            ht[l, fr, :] = hb16
            h = hb16.astype(f32) + dot_nt(wq(1, l, q), av[l])
        ht[2 * N_LAYER - 1, fr, :] = (h - yt[fr, :].astype(f32)).astype(bf16)
    key = share(qkeys, q_cols)
    gpa.finish()
    gpb.finish()
    arrive(key, act.at[its_rows, q_cols])
    qv = [act[:, (N_LAYER + l) * rank : (N_LAYER + l + 1) * rank] for l in range(N_LAYER)]
    gain_t = act[:, 2 * N_LAYER * rank :].astype(f32).T
    first = lax.broadcasted_iota(jnp.int32, (2 * tseq, rank), 0) < tseq

    def apart(v):
        none = jnp.zeros_like(v)
        return jnp.concatenate([jnp.where(first, v, none), jnp.where(first, none, v)], axis=1)

    apart_q, apart_a = [apart(v) for v in qv], [apart(v) for v in av]
    both_d = jnp.zeros((quad, 2 * rank), f32)
    for q in range(SIDE):
        fr = slice(q * quad, (q + 1) * quad)
        cot = ht[2 * N_LAYER - 1, fr, :]
        for l in range(N_LAYER - 1, -1, -1):
            hl = ht[l, fr, :]
            for arr, left, right in ((2, hl, apart_q[l]), (3, cot, apart_a[l])):
                pw = wq(arr, l, q).astype(f32)
                both_d = both_d + dot_nn(left, right) * jnp.concatenate([pw, pw], axis=1)
            if l > 0:
                cot = (
                    cot.astype(f32) + dot_nt(wq(0, l, q), qv[l]) - gain_t[l : l + 1, :] * hl.astype(f32)
                ).astype(bf16)
                ht[N_LAYER + l - 1, fr, :] = cot

    def fold(v):
        return jnp.sum(v.reshape(-1, rank), axis=0, keepdims=True)

    def stack(values):
        return jnp.concatenate([fold(v) for v in values] + [jnp.zeros((8 - len(values), rank), f32)], axis=0)

    dv_out[...] = stack([both_d[:, :rank], both_d[:, rank:]])
    eight = [(up(sx, k // 2), fs(y, z, lax.rem(c + k, 2))) for k in range(1, 8)]
    key = send_all([(dv_out, dv_in.at[k], dev) for k, dev in enumerate(eight)])
    arrive_all(key, dv_in)
    dv = dv_out[...] + jnp.sum(dv_in[...], axis=0)
    s0 = jnp.sum(dv[0:1], keepdims=True) / (tseq * width)
    s1 = jnp.sum(dv[1:2], keepdims=True) / (tseq * width)
    token = lax.broadcasted_iota(jnp.int32, (2 * tseq, 1), 0)
    scale = jnp.where(token < tseq, s0, s1)
    qd = [(qv[l].astype(f32) * scale).astype(bf16) for l in range(N_LAYER)]
    ad = [(av[l].astype(f32) * scale).astype(bf16) for l in range(N_LAYER)]

    def gradient(arr, q):
        base, right = ((0, qd), (N_LAYER, ad))[arr]
        at = pl.ds(pl.multiple_of(q * quad, quad), quad)
        for l in range(N_LAYER):
            value = dot_nn(ht[base + l, at, :], right[l])
            g[arr, q, :, :, l * rank : (l + 1) * rank] = value.astype(bf16).reshape(SIDE, pr, rank)

    class Scatter:
        def __init__(self, arr, last):
            self.arr, self.last, self.key = arr, last, {}
            self.at = y if last == "y" else z

        def dev(self, i, j):
            dy, dz = (i, j) if self.last == "y" else (j, i)
            return (sx, fs(up(y, dy), up(z, dz), c))

        def pair(self, p, j):
            if self.last == "y":
                return self.arr, pl.ds(2 * p, 2), up(z, j)
            return self.arr, up(y, j), pl.ds(2 * p, 2)

        def push(self, n, p, j, dj):
            self.key[n] = send(g.at[self.pair(p, j)], pair_in.at[self.arr, n], self.dev(0, dj))

        def arrived(self, n):
            arrive(self.key[n], pair_in.at[self.arr, n])
            return pair_in[self.arr, n].astype(f32)

        def start(self, n):
            self.push(n, *((0, 2, 1), (1, 2, -1), (1, 1, 1), (0, -1, -1))[n])

        def middle(self):
            at = self.pair(0, 1)
            g[at] = (g[at].astype(f32) + self.arrived(0)).astype(bf16)
            self.push(4, 0, 1, 1)
            at = self.pair(1, -1)
            g[at] = (g[at].astype(f32) + self.arrived(1)).astype(bf16)
            self.push(5, 1, -1, -1)

        def end(self):
            acc2[self.arr, 2:4] = g[self.pair(1, 0)].astype(f32) + self.arrived(2) + self.arrived(5)
            acc2[self.arr, 0:2] = g[self.pair(0, 0)].astype(f32) + self.arrived(3) + self.arrived(4)
            fin[self.arr, 0:SIDE] = acc2[self.arr].astype(bf16)
            for i in (2, 1, -1):
                self.key[("s", i)] = send(
                    fin.at[self.arr, up(self.at, i)], block_in.at[self.arr, i % SIDE - 1], self.dev(i, 0)
                )

        def end2(self):
            value = acc2[self.arr, self.at]
            for i in (1, -1, 2):
                arrive(self.key[("s", i)], block_in.at[self.arr, i % SIDE - 1])
                value = value + block_in[self.arr, i % SIDE - 1].astype(f32)
            self.value = value

        def home(self):
            fin[self.arr, SIDE] = self.value.astype(bf16)
            self.back = []
            for k in range(1, N_LAYER):
                to = up(sx, k)
                self.back.append(send(fin.at[self.arr, SIDE, :, cols(to)], gx.at[self.arr, sx], line(k)))
            gx[self.arr, sx] = fin[self.arr, SIDE, :, cols(sx)]

        def done(self):
            for k in range(1, N_LAYER):
                arrive(self.back[k - 1], gx.at[self.arr, up(sx, -k)])

    both = (Scatter(0, "y"), Scatter(1, "z"))
    gradient(1, up(y, 2))
    both[1].start(0)
    both[1].start(1)
    for q in range(2):
        gradient(0, q)
    both[0].start(0)
    for q in range(2, SIDE):
        gradient(0, q)
    for n in range(1, SIDE):
        both[0].start(n)
    gradient(1, up(y, 1))
    both[1].start(2)
    gradient(1, up(y, -1))
    both[1].start(3)
    gradient(1, y)
    flush()
    for s in both:
        s.middle()
    for s in both:
        s.end()
    for s in both:
        s.end2()
    tokens_total = tseq * 2 * CHIPS
    shrink = 1.0 / (damping * tokens_total * width)

    def lanes(v):
        return sum(v[:, l * rank : (l + 1) * rank] for l in range(N_LAYER))

    pg = rg = gg = 0.0
    for key, k in zip(res_keys, (2, 1, 3)):
        arrive(key, res_s.at[:, :, cols(up(sx, -k))])
    for s in both:
        pg = pg + lanes(s.value * w[2 + s.arr, y, z].astype(f32))
        rg = rg + lanes(s.value * res_s[s.arr])
        gg = gg + lanes(s.value * s.value)
    pg, rg, gg = fold(pg) * shrink, fold(rg) * shrink, fold(gg) * (shrink * shrink)
    stat_out[...] = home + jnp.concatenate(
        [jnp.zeros((1, rank), f32), pg, rg, 2.0 * pg + gg, jnp.zeros((4, rank), f32)], axis=0
    )
    key = send_all([(stat_out, stat_in.at[k], dev) for k, dev in enumerate(eight)])
    for s in both:
        s.home()
    arrive_all(key, stat_in)
    total = stat_out[...] + jnp.sum(stat_in[...], axis=0)
    stat2_out[...] = total
    key = send_all([(stat2_out, stat2_in.at[k - 1], chip_dev(k)) for k in range(1, CHIPS)])
    for s in both:
        s.done()
    big = gx[...].astype(f32).reshape(2, own, rank) * shrink + direc
    flush()
    arrive_all(key, stat2_in)
    total = total + jnp.sum(stat2_in[...], axis=0)
    rr = jnp.sum(total[0:1], keepdims=True)
    pq = jnp.sum(total[1:2], keepdims=True) * damping
    rp = jnp.sum(total[2:3], keepdims=True)
    pp = jnp.sum(total[3:4], keepdims=True)
    step = rr / pq * damping
    norm_new = rr - 2.0 * (step * rp) + step * (step * pp)
    new_res = res - step * big
    newres_ref[...] = new_res
    newdir_ref[...] = new_res + (norm_new / rr) * direc
    assert counter.n == N_SEM
    flush()


def step_kernel(inputs, targets, down_proj, up_proj, direction, residual):
    tseq, width = inputs.shape
    _, own, rank = down_proj.shape
    pr = own // N_LAYER
    feats = CHIPS * pr
    tq = tseq // N_LAYER
    wide = N_LAYER * rank
    hr = rank // 2
    vm = pltpu.VMEM
    scratch = [
        vm((tseq, width), bf16), vm((tseq, width), bf16),
        vm((2, own, rank), f32), vm((2, own, rank), f32),
        vm((2 * tseq, feats), bf16), vm((2 * tseq, feats), bf16),
        vm((tseq, feats), bf16), vm((tseq, feats), bf16),
        vm((feats, 2 * tseq), bf16), vm((feats, 2 * tseq), bf16),
        vm((4, SIDE, SIDE, pr, wide), bf16), vm((2, own, rank), bf16),
        vm((2 * tseq, 3 * wide), f32), vm((tseq, 3 * wide), bf16), vm((tseq, 3 * wide), bf16),
        vm((tseq, 3 * wide), bf16), vm((N_LAYER - 1, tq, 3 * wide), bf16),
        vm((2 * CHIPS, hr, rank), f32), vm((CHIPS, hr, rank), bf16), vm((CHIPS, hr, rank), bf16),
        vm((CHIPS, hr, rank), bf16), vm((CHIPS - 1, hr, rank), bf16), vm((hr, rank), bf16),
        vm((N_LAYER - 1, hr, rank), bf16), vm((2 * CHIPS, hr, rank), bf16),
        vm((2, pr, wide), f32),
        vm((2 * tseq, 2 * wide + rank), bf16), vm((2 * N_LAYER, feats, 2 * tseq), bf16),
        vm((2, SIDE, SIDE, pr, wide), bf16),
        vm((2, 6, 2, pr, wide), bf16),
        vm((2, SIDE, pr, wide), f32),
        vm((2, 3, pr, wide), bf16), vm((2, SIDE + 1, pr, wide), bf16),
        vm((2, N_LAYER, pr, rank), bf16),
        vm((8, rank), f32), vm((7, 8, rank), f32), vm((8, rank), f32), vm((CHIPS - 1, 8, rank), f32),
        vm((8, rank), f32), vm((7, 8, rank), f32),
        pltpu.SemaphoreType.DMA((N_SEM,)), pltpu.SemaphoreType.DMA((N_SEM,)), pltpu.SemaphoreType.DMA((8,)),
    ]
    hbm = pl.BlockSpec(memory_space=pl.ANY)
    spec = pl.BlockSpec(memory_space=pltpu.VMEM)
    operands = (inputs, targets, down_proj[0], up_proj[0], direction[0], residual[0])
    out = pltpu.VMEM((2, own, rank), f32)
    new_res, new_dir = pl.pallas_call(
        kernel,
        out_shape=(out, out),
        in_specs=[hbm] * 6,
        out_specs=(spec, spec),
        scratch_shapes=scratch,
        compiler_params=pltpu.CompilerParams(
            collective_id=0, has_side_effects=True, vmem_limit_bytes=50 * 1024 * 1024
        ),
        cost_estimate=pl.CostEstimate(flops=4_000_000_000, bytes_accessed=8_000_000, transcendentals=0),
    )(*(pltpu.with_memory_space_constraint(v, pltpu.HBM) for v in operands))
    return new_res[None], new_dir[None]


def solution(mesh):
    in_specs = (
        P("fsdp", None),
        P("fsdp", None),
        P("section", "fsdp", None),
        P("section", "fsdp", None),
        P("section", None, "fsdp", None),
        P("section", None, "fsdp", None),
    )
    out_specs = (P("section", None, "fsdp", None), P("section", None, "fsdp", None))
    return jax.shard_map(step_kernel, mesh=mesh, in_specs=in_specs, out_specs=out_specs, check_vma=False)
```
